32 devices in a mesh: dp: 4 (over z), seq: 4 (over x, core), blk: 2 (over y).
Axes of the slice: x: 2, y: 2, z: 4, core: 2. Of those that a mesh axis runs over, the one named last changes fastest.
Arguments:
- tokens: bfloat16 [4096, 1024], P(('dp', 'seq', 'blk')), may hold values from -6 to 6
- first_gain: bfloat16 [1024], P(('dp', 'seq', 'blk')), may hold values from 0.099609375 to 1.8984375
- first_shift: bfloat16 [1024], P(('dp', 'seq', 'blk')), may hold values from -3 to 3
- joint_weight: bfloat16 [1024, 3072], P(('dp', 'blk'), 'seq'), may hold values from -0.1875 to 0.1875
- joint_bias: bfloat16 [16, 128], P('seq', ('dp', 'blk')), may hold values from -3 to 3
- output_weight: bfloat16 [1024, 1024], P('seq', ('dp', 'blk')), may hold values from -0.75 to 0.75
- output_bias: bfloat16 [1024], P(('dp', 'seq', 'blk')), may hold values from -3 to 3
- second_gain: bfloat16 [1024], P(('dp', 'seq', 'blk')), may hold values from 0.099609375 to 1.8984375
- second_shift: bfloat16 [1024], P(('dp', 'seq', 'blk')), may hold values from -3 to 3
- expand_weight: bfloat16 [1024, 4096], P(('dp', 'blk'), 'seq'), may hold values from -0.1875 to 0.1875
- expand_bias: bfloat16 [4, 1024], P('seq', ('dp', 'blk')), may hold values from -3 to 3
- reduce_weight: bfloat16 [4096, 1024], P('seq', ('dp', 'blk')), may hold values from -0.1875 to 0.1875
- reduce_bias: bfloat16 [1024], P(('dp', 'seq', 'blk')), may hold values from -3 to 3
- cotangent: bfloat16 [4096, 1024], P(('dp', 'seq', 'blk')), may hold values from -6 to 6
Outputs:
- layer_output: bfloat16 [4096, 1024], P(('dp', 'seq', 'blk'))
- input_grad: bfloat16 [4096, 1024], P(('dp', 'seq', 'blk'))
- first_gain_grad: float32 [1024], P(('dp', 'seq', 'blk'))
- first_shift_grad: float32 [1024], P(('dp', 'seq', 'blk'))
- joint_weight_grad: float32 [1024, 3072], P(('dp', 'blk'), 'seq')
- joint_bias_grad: float32 [16, 128], P('seq', ('dp', 'blk'))
- output_weight_grad: float32 [1024, 1024], P('seq', ('dp', 'blk'))
- output_bias_grad: float32 [1024], P(('dp', 'seq', 'blk'))
- second_gain_grad: float32 [1024], P(('dp', 'seq', 'blk'))
- second_shift_grad: float32 [1024], P(('dp', 'seq', 'blk'))
- expand_weight_grad: float32 [1024, 4096], P(('dp', 'blk'), 'seq')
- expand_bias_grad: float32 [4, 1024], P('seq', ('dp', 'blk'))
- reduce_weight_grad: float32 [4096, 1024], P('seq', ('dp', 'blk'))
- reduce_bias_grad: float32 [1024], P(('dp', 'seq', 'blk'))
The draws below stay inside these ranges and needn't reach their ends.
All inputs are finite; a program needn't handle non-finite values.
Results may differ from the reference program's by a relative error of at most 0.02.
Values may be sent and summed in bfloat16 or wider, within the bound.
No kernel may reach another device: no remote copies, remote signals or barrier semaphores. Data moves between devices by JAX's collectives and lax.ppermute only.
A program may use at most 128 MiB of HBM per device.

```python
import jax
import jax.numpy as jnp
from jax import lax

D = 1024
H = 16
HD = 64
FF = 4096
SEQ_LEN = 1024
SEQS = 4
TOKENS = 4096
N_SEQ = 4


def strengthened(drawn, stream_key, source, target, parts, factor):
    owner, partner = [(jnp.arange(drawn.shape[axis_at]) // (drawn.shape[axis_at] // parts)).reshape([-1 if axis == axis_at else 1 for axis in range(drawn.ndim)]) for axis_at in (source, target)]
    chosen = jax.random.permutation(stream_key, parts)[partner]
    strong = (owner == chosen) | (owner == (partner + parts // 2) % parts)
    return jnp.where(strong, factor * drawn, drawn)


def steps_of(key, shape, cuts, smallest, high):
    factor_of, own = 1.0, jax.random.fold_in(key, 6)
    for axis_at, parts in cuts:
        draws = jnp.exp(jax.random.uniform(jax.random.fold_in(own, axis_at), (parts,), jnp.float32, smallest / len(cuts), high / len(cuts)))
        factor_of = factor_of * jnp.repeat(draws, shape[axis_at] // parts).reshape([-1 if axis == axis_at else 1 for axis in range(len(shape))])
    return factor_of


def noise(rng, dims, spread, bound, split=(), kind=jnp.bfloat16):
    level = steps_of(rng, dims, split, -0.22, 0.18) if split else 1.0
    entries = jax.random.normal(rng, dims, jnp.float32) * spread * level
    return jnp.minimum(jnp.maximum(entries, -bound), bound).astype(kind)


def heavy_noise(rng, shape, width, reach, cuts, heavy, held_as=jnp.bfloat16):
    drawn = width * jax.random.normal(rng, shape, jnp.float32)
    if cuts:
        drawn = drawn * steps_of(rng, shape, cuts, -0.22, 0.18)
    return jnp.clip(strengthened(drawn, jax.random.fold_in(rng, 3), *heavy), -reach, reach).astype(held_as)


def setup_inputs(seed: int = 0) -> dict:
    keys = jax.random.split(jax.random.key(seed), 15)
    return {
        "tokens": heavy_noise(keys[0], (TOKENS, D), 1.0, 6.0, ((0, 32),), (0, 1, 32, 2.75)),
        "first_gain": jnp.clip(1.0 + 0.18 * jax.random.normal(keys[1], (D,), jnp.float32), 0.099609375, 1.8984375).astype(jnp.bfloat16),
        "first_shift": noise(keys[2], (D,), 0.5, 3.0, ((0, 32),)),
        "joint_weight": noise(keys[3], (D, 3 * D), D ** -0.5, 0.1875, ((0, 8), (1, 4))),
        "joint_bias": noise(keys[4], (H, 2 * HD), 0.5, 3.0, ((0, 4), (1, 8))),
        "output_weight": noise(keys[5], (D, D), (D // 16) ** -0.5, 0.75, ((0, 4), (1, 8))),
        "output_bias": noise(keys[6], (D,), 0.5, 3.0, ((0, 32),)),
        "second_gain": jnp.clip(1.0 + 0.18 * jax.random.normal(keys[7], (D,), jnp.float32), 0.099609375, 1.8984375).astype(jnp.bfloat16),
        "second_shift": noise(keys[8], (D,), 0.5, 3.0, ((0, 32),)),
        "expand_weight": noise(keys[9], (D, FF), D ** -0.5, 0.1875, ((0, 8), (1, 4))),
        "expand_bias": noise(keys[10], (N_SEQ, FF // N_SEQ), 0.5, 3.0, ((0, 4), (1, 8))),
        "reduce_weight": noise(keys[11], (FF, D), (FF // 4) ** -0.5, 0.1875, ((0, 4), (1, 8))),
        "reduce_bias": noise(keys[12], (D,), 0.5, 3.0, ((0, 32),)),
        "cotangent": heavy_noise(keys[13], (TOKENS, D), 1.0, 6.0, ((0, 32),), (0, 1, 32, 2.75)),
    }


epsilon = 1e-05
highest = lax.Precision.HIGHEST

@jax.custom_vjp
def low(v):
    return lax.optimization_barrier(v.astype(jnp.bfloat16)).astype(jnp.float32)

@jax.custom_vjp
def low_back(v):
    return v

def low_keep(v):
    return (low(v), None)

def low_pass(kept, grad):
    return (grad,)

def back_keep(v):
    return (v, None)

def back_low(kept, grad):
    return (low(grad),)
low.defvjp(low_keep, low_pass)
low_back.defvjp(back_keep, back_low)

def layer_norm(values, gain_row, shift_row):
    average = lax.optimization_barrier(jnp.mean(values, -1, keepdims=True))
    centred = values - average
    variance = lax.optimization_barrier(jnp.mean(centred * centred, -1, keepdims=True))
    return centred * lax.rsqrt(variance + epsilon) * gain_row + shift_row

def joint_full_bias(joint_bias):
    paired = joint_bias.reshape(H, 2, HD)
    return jnp.stack([paired[:, 0], jnp.zeros_like(paired[:, 0]), paired[:, 1]], axis=1).reshape(3 * D)

def attention(queries, key_inputs, value_inputs):
    seq_rows = queries.shape[0]
    block_rows = min(512, seq_rows)
    scale_factor = HD ** (-0.5)
    slopes = jnp.exp2(-8.0 * (jnp.arange(H) + 1).astype(jnp.float32) / H)
    key_places = jnp.arange(seq_rows, dtype=jnp.int32)
    query_blocks = queries.reshape(seq_rows // block_rows, block_rows, H, HD)
    place_blocks = key_places.reshape(seq_rows // block_rows, block_rows)

    def one_block(block_pair):
        query_block, places = block_pair
        scores = jnp.einsum('qhd,khd->hqk', query_block, key_inputs, precision=highest) * scale_factor
        offsets = (key_places[None, :] - places[:, None]).astype(jnp.float32)
        scores = scores + slopes[:, None, None] * offsets[None]
        allowed = key_places[None, :] <= places[:, None]
        scores = low_back(jnp.where(allowed[None], scores, -1e+30))
        weights = low(jax.nn.softmax(scores, axis=-1))
        return jnp.einsum('hqk,khd->qhd', weights, value_inputs, precision=highest)
    outputs = lax.map(jax.checkpoint(one_block), (query_blocks, place_blocks))
    return outputs.reshape(seq_rows, H, HD)

def layer_forward(inputs, params):
    first_gain, first_shift, joint_weight, joint_bias, output_weight, output_bias, second_gain, second_shift, expand_weight, expand_bias, reduce_weight, reduce_bias = params
    seq_rows = inputs.shape[0]
    normed_one = low(layer_norm(inputs, first_gain, first_shift))
    mixed_cols = jnp.dot(normed_one, joint_weight, precision=highest) + joint_full_bias(joint_bias)
    mixed_cols = mixed_cols.reshape(seq_rows, H, 3, HD)
    queries = low_back(low(mixed_cols[:, :, 0]))
    key_inputs = low_back(low(mixed_cols[:, :, 1]))
    value_inputs = low_back(low(mixed_cols[:, :, 2]))
    attended = low_back(low(attention(queries, key_inputs, value_inputs).reshape(seq_rows, D)))
    branch = low_back(jnp.dot(attended, output_weight, precision=highest) + output_bias)
    middle = inputs + branch
    normed_two = low(layer_norm(middle, second_gain, second_shift))
    hidden = low_back(jnp.dot(normed_two, expand_weight, precision=highest) + expand_bias.reshape(FF))
    activated = low(jax.nn.gelu(hidden, approximate=True))
    result = low_back(jnp.dot(activated, reduce_weight, precision=highest) + reduce_bias)
    return middle + result

def reference(tokens, first_gain, first_shift, joint_weight, joint_bias, output_weight, output_bias, second_gain, second_shift, expand_weight, expand_bias, reduce_weight, reduce_bias, cotangent):
    params = tuple((weight_arg.astype(jnp.float32) for weight_arg in (first_gain, first_shift, joint_weight, joint_bias, output_weight, output_bias, second_gain, second_shift, expand_weight, expand_bias, reduce_weight, reduce_bias)))
    token_seqs = tokens.astype(jnp.float32).reshape(SEQS, SEQ_LEN, D)
    tangent_seqs = cotangent.astype(jnp.float32).reshape(SEQS, SEQ_LEN, D)

    def one_sequence(totals, seq_pair):
        seq_inputs, seq_tangent = seq_pair
        output, pullback = jax.vjp(layer_forward, seq_inputs, params)
        seq_input_grad, param_grads = pullback(seq_tangent)
        totals = jax.tree.map(jnp.add, totals, param_grads)
        return (totals, (output.astype(jnp.bfloat16), seq_input_grad.astype(jnp.bfloat16)))
    zero_grads = tuple((jnp.zeros_like(weight_arg) for weight_arg in params))
    totals, (outputs, input_grads) = lax.scan(one_sequence, zero_grads, (token_seqs, tangent_seqs))
    return (outputs.reshape(TOKENS, D), input_grads.reshape(TOKENS, D), totals[0], totals[1], totals[2], totals[3], totals[4], totals[5], totals[6], totals[7], totals[8], totals[9], totals[10], totals[11])
```

```python
import jax
import jax.numpy as jnp
from jax import lax
from jax.sharding import PartitionSpec as P

H = 16
HD = 64


epsilon = 1e-05


def layer_norm(values, gain_row, shift_row):
    average = jnp.mean(values, -1, keepdims=True)
    centred = values - average
    variance = jnp.mean(centred * centred, -1, keepdims=True)
    return centred * lax.rsqrt(variance + epsilon) * gain_row + shift_row


def local_bias(pair_local, head_local):
    paired = pair_local.reshape(head_local, 2, HD)
    return jnp.stack([paired[:, 0], jnp.zeros_like(paired[:, 0]), paired[:, 1]], axis=1).reshape(
        head_local * 3 * HD
    )


def gelu_tanh(values):
    return jax.nn.gelu(values, approximate=True)


def score_tile(query_block, key_tile, places, tile_start, slopes, scale_factor):
    tile_rows = key_tile.shape[0]
    key_places = tile_start + jnp.arange(tile_rows, dtype=jnp.int32)
    scores = (
        jnp.einsum("qhd,khd->hqk", query_block, key_tile, preferred_element_type=jnp.float32)
        * scale_factor
    )
    offsets = (key_places[None, :] - places[:, None]).astype(jnp.float32)
    scores = scores + slopes[:, None, None] * offsets[None]
    allowed = (key_places[None, :] <= places[:, None])[None]
    return (jnp.where(allowed, scores, -1e30), allowed)


def attend_forward(queries, all_keys, all_values, places, slopes):
    row_count, head_local, head_width = queries.shape
    block_rows = min(512, row_count)
    tile_rows = min(512, all_keys.shape[0])
    scale_factor = head_width ** (-0.5)
    query_blocks = queries.reshape(row_count // block_rows, block_rows, head_local, head_width)
    place_blocks = places.reshape(row_count // block_rows, block_rows)

    def one_block(block_pair):
        query_block, block_places = block_pair
        needed = (block_places[-1] + tile_rows) // tile_rows

        def one_tile(counter, state_carry):
            running_max, running_sum, running_total = state_carry
            tile_start = counter * tile_rows
            key_tile = lax.dynamic_slice_in_dim(all_keys, tile_start, tile_rows, 0)
            value_tile = lax.dynamic_slice_in_dim(all_values, tile_start, tile_rows, 0)
            scores, allowed = score_tile(
                query_block, key_tile, block_places, tile_start, slopes, scale_factor
            )
            new_max = jnp.maximum(running_max, jnp.max(scores, -1))
            weights_tile = jnp.where(allowed, jnp.exp(scores - new_max[..., None]), 0.0)
            factor = jnp.exp(running_max - new_max)
            running_sum = running_sum * factor + jnp.sum(weights_tile, -1)
            running_total = running_total * factor[..., None] + jnp.einsum(
                "hqk,khd->hqd",
                weights_tile.astype(jnp.bfloat16),
                value_tile,
                preferred_element_type=jnp.float32,
            )
            return (new_max, running_sum, running_total)

        start_state = (
            jnp.full((head_local, block_rows), -1e30, jnp.float32),
            jnp.zeros((head_local, block_rows), jnp.float32),
            jnp.zeros((head_local, block_rows, head_width), jnp.float32),
        )
        running_max, running_sum, running_total = lax.fori_loop(0, needed, one_tile, start_state)
        return (running_total / running_sum[..., None], running_max + jnp.log(running_sum))

    outputs, log_sums = lax.map(one_block, (query_blocks, place_blocks))
    outputs = jnp.transpose(outputs, (0, 2, 1, 3)).reshape(row_count, head_local, head_width)
    return (outputs, log_sums)


def attend_backward(queries, all_keys, all_values, places, slopes, grad_out, log_sums, deltas):
    row_count, head_local, head_width = queries.shape
    key_count = all_keys.shape[0]
    block_rows = min(512, row_count)
    tile_rows = min(512, key_count)
    scale_factor = head_width ** (-0.5)
    block_count = row_count // block_rows
    query_blocks = queries.reshape(block_count, block_rows, head_local, head_width)
    grad_blocks = grad_out.reshape(block_count, block_rows, head_local, head_width)
    place_blocks = places.reshape(block_count, block_rows)
    delta_blocks = jnp.transpose(deltas.reshape(block_count, block_rows, head_local), (0, 2, 1))

    def one_block(key_grads, block_inputs):
        query_block, grad_block, block_places, block_lse, block_delta = block_inputs
        needed = (block_places[-1] + tile_rows) // tile_rows

        def one_tile(counter, inner_carry):
            query_grad, key_sums = inner_carry
            tile_start = counter * tile_rows
            key_tile = lax.dynamic_slice_in_dim(all_keys, tile_start, tile_rows, 0)
            value_tile = lax.dynamic_slice_in_dim(all_values, tile_start, tile_rows, 0)
            scores, allowed = score_tile(
                query_block, key_tile, block_places, tile_start, slopes, scale_factor
            )
            probs = jnp.where(allowed, jnp.exp(scores - block_lse[..., None]), 0.0)
            value_grad = jnp.einsum(
                "hqk,qhd->khd",
                probs.astype(jnp.bfloat16),
                grad_block,
                preferred_element_type=jnp.float32,
            )
            prob_grad = jnp.einsum(
                "qhd,khd->hqk", grad_block, value_tile, preferred_element_type=jnp.float32
            )
            score_grad = (probs * (prob_grad - block_delta[..., None])).astype(jnp.bfloat16)
            query_grad = (
                query_grad
                + jnp.einsum(
                    "hqk,khd->qhd", score_grad, key_tile, preferred_element_type=jnp.float32
                )
                * scale_factor
            )
            key_grad = (
                jnp.einsum(
                    "hqk,qhd->khd", score_grad, query_block, preferred_element_type=jnp.float32
                )
                * scale_factor
            )
            current = lax.dynamic_slice_in_dim(key_sums, tile_start, tile_rows, 0)
            update = current + jnp.concatenate([key_grad, value_grad], -1)
            key_sums = lax.dynamic_update_slice_in_dim(key_sums, update, tile_start, 0)
            return (query_grad, key_sums)

        start_grad = jnp.zeros((block_rows, head_local, head_width), jnp.float32)
        query_grad, key_grads = lax.fori_loop(0, needed, one_tile, (start_grad, key_grads))
        return (key_grads, query_grad)

    start_keys = jnp.zeros((key_count, head_local, 2 * head_width), jnp.float32)
    key_grads, query_grads = lax.scan(
        one_block, start_keys, (query_blocks, grad_blocks, place_blocks, log_sums, delta_blocks)
    )
    return (query_grads.reshape(row_count, head_local, head_width), key_grads)


def local(
    tokens,
    first_gain,
    first_shift,
    joint_weight,
    joint_bias,
    output_weight,
    output_bias,
    second_gain,
    second_shift,
    expand_weight,
    expand_bias,
    reduce_weight,
    reduce_bias,
    cotangent,
):
    seq_count = lax.axis_size("seq")
    blk_count = lax.axis_size("blk")
    head_local = H // seq_count
    tok_rows = tokens.shape[0]
    inputs = tokens.astype(jnp.float32)
    small_full = (
        lax.all_gather(first_gain, ("dp", "seq", "blk"), axis=0, tiled=True),
        lax.all_gather(first_shift, ("dp", "seq", "blk"), axis=0, tiled=True),
        lax.all_gather(output_bias, ("dp", "seq", "blk"), axis=0, tiled=True),
        lax.all_gather(second_gain, ("dp", "seq", "blk"), axis=0, tiled=True),
        lax.all_gather(second_shift, ("dp", "seq", "blk"), axis=0, tiled=True),
        lax.all_gather(reduce_bias, ("dp", "seq", "blk"), axis=0, tiled=True),
    )
    gain_one, shift_one, out_shift, gain_two, shift_two, reduce_shift = [
        piece.astype(jnp.float32) for piece in small_full
    ]
    joint_local, pair_local, out_local = (
        lax.all_gather(joint_weight, ("dp", "blk"), axis=0, tiled=True),
        lax.all_gather(joint_bias, ("dp", "blk"), axis=1, tiled=True),
        lax.all_gather(output_weight, ("dp", "blk"), axis=1, tiled=True),
    )
    expand_local, expand_shift, reduce_local = (
        lax.all_gather(expand_weight, ("dp", "blk"), axis=0, tiled=True),
        lax.all_gather(expand_bias, ("dp", "blk"), axis=1, tiled=True),
        lax.all_gather(reduce_weight, ("dp", "blk"), axis=1, tiled=True),
    )
    outgoing = layer_norm(inputs, gain_one, shift_one).astype(jnp.bfloat16)
    arrived = lax.all_gather(outgoing, "seq", axis=0, tiled=True)
    row_count = arrived.shape[0]
    mixed_cols = jnp.dot(arrived, joint_local, preferred_element_type=jnp.float32)
    mixed_cols = mixed_cols + local_bias(pair_local.astype(jnp.float32), head_local)
    by_head = mixed_cols.astype(jnp.bfloat16).reshape(row_count, head_local, 3 * HD)
    queries = by_head[:, :, :HD]
    key_value = by_head[:, :, HD:].reshape(seq_count, tok_rows, head_local, 2 * HD)
    ordered = lax.all_gather(key_value, "blk", axis=1, tiled=True)
    ordered = ordered.reshape(seq_count * blk_count * tok_rows, head_local, 2 * HD)
    all_keys = ordered[:, :, :HD]
    all_values = ordered[:, :, HD:]
    places = (
        (jnp.arange(seq_count, dtype=jnp.int32)[:, None] * blk_count + lax.axis_index("blk"))
        * tok_rows
        + jnp.arange(tok_rows, dtype=jnp.int32)[None, :]
    ).reshape(row_count)
    head_ids = lax.axis_index("seq") * head_local + jnp.arange(head_local, dtype=jnp.int32)
    slopes = jnp.exp2(-8.0 * (head_ids + 1).astype(jnp.float32) / H)
    attended, log_sums = attend_forward(queries, all_keys, all_values, places, slopes)
    attended_low = attended.reshape(row_count, head_local * HD).astype(jnp.bfloat16)
    branch_part = jnp.dot(attended_low, out_local, preferred_element_type=jnp.float32)
    branch_sum = lax.psum_scatter(
        branch_part.astype(jnp.bfloat16), "seq", scatter_dimension=0, tiled=True
    ).astype(jnp.float32)
    middle = inputs + (branch_sum + out_shift)
    normed_two = layer_norm(middle, gain_two, shift_two).astype(jnp.bfloat16)
    normed_two_group, cot_group = (
        lax.all_gather(normed_two, "seq", axis=0, tiled=True),
        lax.all_gather(cotangent, "seq", axis=0, tiled=True),
    )
    hidden = jnp.dot(normed_two_group, expand_local, preferred_element_type=jnp.float32)
    hidden = hidden + expand_shift.astype(jnp.float32).reshape(-1)
    activated, gelu_pull = jax.vjp(gelu_tanh, hidden)
    activated_low = activated.astype(jnp.bfloat16)
    result_part = jnp.dot(activated_low, reduce_local, preferred_element_type=jnp.float32)
    result_sum = lax.psum_scatter(
        result_part.astype(jnp.bfloat16), "seq", scatter_dimension=0, tiled=True
    ).astype(jnp.float32)
    layer_output = (middle + (result_sum + reduce_shift)).astype(jnp.bfloat16)
    upstream = cotangent.astype(jnp.float32)
    reduce_grad = jnp.einsum(
        "tf,td->fd", activated_low, cot_group, preferred_element_type=jnp.float32
    )
    reduce_shift_grad = jnp.sum(upstream, 0)
    activated_grad = jnp.einsum(
        "td,fd->tf", cot_group, reduce_local, preferred_element_type=jnp.float32
    )
    hidden_grad = gelu_pull(activated_grad)[0].astype(jnp.bfloat16)
    expand_grad = jnp.einsum(
        "tc,tf->cf", normed_two_group, hidden_grad, preferred_element_type=jnp.float32
    )
    expand_shift_grad = jnp.sum(hidden_grad.astype(jnp.float32), 0).reshape(
        expand_shift.shape[0], -1
    )
    normed_two_part = jnp.einsum(
        "tf,cf->tc", hidden_grad, expand_local, preferred_element_type=jnp.float32
    )
    normed_two_grad = lax.psum_scatter(
        normed_two_part.astype(jnp.bfloat16), "seq", scatter_dimension=0, tiled=True
    ).astype(jnp.float32)
    unused_value, norm_two_pull = jax.vjp(layer_norm, middle, gain_two, shift_two)
    middle_norm_grad, gain_two_grad, shift_two_grad = norm_two_pull(normed_two_grad)
    middle_grad = upstream + middle_norm_grad
    branch_grad = middle_grad.astype(jnp.bfloat16)
    out_shift_grad = jnp.sum(branch_grad.astype(jnp.float32), 0)
    branch_group = lax.all_gather(branch_grad, "seq", axis=0, tiled=True)
    out_grad = jnp.einsum(
        "tc,td->cd", attended_low, branch_group, preferred_element_type=jnp.float32
    )
    attended_grad = jnp.einsum(
        "td,cd->tc", branch_group, out_local, preferred_element_type=jnp.float32
    ).astype(jnp.bfloat16)
    grad_heads = attended_grad.reshape(row_count, head_local, HD)
    deltas = jnp.sum(grad_heads.astype(jnp.float32) * attended, -1)
    query_grads, key_grads = attend_backward(
        queries, all_keys, all_values, places, slopes, grad_heads, log_sums, deltas
    )
    key_terms = key_grads.reshape(seq_count, blk_count * tok_rows, head_local * 2 * HD)
    key_sums = lax.psum_scatter(
        key_terms.astype(jnp.bfloat16), "blk", scatter_dimension=1, tiled=True
    ).astype(jnp.float32)
    combined = jnp.concatenate(
        [
            query_grads.astype(jnp.bfloat16),
            key_sums.reshape(row_count, head_local, 2 * HD).astype(jnp.bfloat16),
        ],
        -1,
    )
    mixed_grad = combined.reshape(row_count, head_local * 3 * HD)
    joint_grad = jnp.einsum("tc,tk->ck", arrived, mixed_grad, preferred_element_type=jnp.float32)
    bias_sums = jnp.sum(mixed_grad.astype(jnp.float32), 0).reshape(head_local, 3, HD)
    pair_grad = jnp.concatenate([bias_sums[:, 0], bias_sums[:, 2]], -1)
    normed_one_part = jnp.einsum(
        "tk,ck->tc", mixed_grad, joint_local, preferred_element_type=jnp.float32
    )
    normed_one_grad = lax.psum_scatter(
        normed_one_part.astype(jnp.bfloat16), "seq", scatter_dimension=0, tiled=True
    ).astype(jnp.float32)
    unused_first, norm_one_pull = jax.vjp(layer_norm, inputs, gain_one, shift_one)
    input_norm_grad, gain_one_grad, shift_one_grad = norm_one_pull(normed_one_grad)
    input_grad = (middle_grad + input_norm_grad).astype(jnp.bfloat16)
    weight_sums = (
        lax.psum_scatter(
            joint_grad.astype(jnp.bfloat16), ("dp", "blk"), scatter_dimension=0, tiled=True
        ).astype(jnp.float32),
        lax.psum_scatter(
            pair_grad.astype(jnp.bfloat16), ("dp", "blk"), scatter_dimension=1, tiled=True
        ).astype(jnp.float32),
        lax.psum_scatter(
            out_grad.astype(jnp.bfloat16), ("dp", "blk"), scatter_dimension=1, tiled=True
        ).astype(jnp.float32),
        lax.psum_scatter(
            expand_grad.astype(jnp.bfloat16), ("dp", "blk"), scatter_dimension=0, tiled=True
        ).astype(jnp.float32),
        lax.psum_scatter(
            expand_shift_grad.astype(jnp.bfloat16), ("dp", "blk"), scatter_dimension=1, tiled=True
        ).astype(jnp.float32),
        lax.psum_scatter(
            reduce_grad.astype(jnp.bfloat16), ("dp", "blk"), scatter_dimension=1, tiled=True
        ).astype(jnp.float32),
    )
    small_sums = (
        lax.psum_scatter(gain_one_grad, ("dp", "seq", "blk"), scatter_dimension=0, tiled=True),
        lax.psum_scatter(shift_one_grad, ("dp", "seq", "blk"), scatter_dimension=0, tiled=True),
        lax.psum_scatter(out_shift_grad, ("dp", "seq", "blk"), scatter_dimension=0, tiled=True),
        lax.psum_scatter(gain_two_grad, ("dp", "seq", "blk"), scatter_dimension=0, tiled=True),
        lax.psum_scatter(shift_two_grad, ("dp", "seq", "blk"), scatter_dimension=0, tiled=True),
        lax.psum_scatter(reduce_shift_grad, ("dp", "seq", "blk"), scatter_dimension=0, tiled=True),
    )
    return (
        layer_output,
        input_grad,
        small_sums[0],
        small_sums[1],
        weight_sums[0],
        weight_sums[1],
        weight_sums[2],
        small_sums[2],
        small_sums[3],
        small_sums[4],
        weight_sums[3],
        weight_sums[4],
        weight_sums[5],
        small_sums[5],
    )


def swap(value, axes, count, offset):
    return lax.ppermute(value, axes, [(i, i ^ offset) for i in range(count)])


def spread(block, axes, count, offsets):
    return [block] + [swap(block, axes, count, offset) for offset in offsets]


def permute_columns(values, index, parts):
    width = values.shape[-1] // parts
    blocks = [
        lax.dynamic_slice_in_dim(values, (index ^ p) * width, width, values.ndim - 1)
        for p in range(parts)
    ]
    return jnp.concatenate(blocks, -1)


def permute_rows(values, index, parts):
    height = values.shape[0] // parts
    blocks = [
        lax.dynamic_slice_in_dim(values, (index ^ p) * height, height, 0) for p in range(parts)
    ]
    return jnp.concatenate(blocks, 0)


def matmul(spec, left, right):
    return jnp.einsum(spec, left, right, preferred_element_type=jnp.float32)


def low(value):
    return value.astype(jnp.bfloat16)


ALL = ("dp", "seq", "blk")
PLANE = ("seq", "blk")
OWNERS = ("dp", "blk")


def norm_back(grad, xhat, scale, gain_row):
    scaled = grad * gain_row
    mean_scaled = jnp.mean(scaled, -1, keepdims=True)
    mean_product = jnp.mean(scaled * xhat, -1, keepdims=True)
    return scale * (scaled - mean_scaled - xhat * mean_product)


def norm_parts(values):
    average = jnp.mean(values, -1, keepdims=True)
    centred = values - average
    variance = jnp.mean(centred * centred, -1, keepdims=True)
    scale = lax.rsqrt(variance + epsilon)
    return (centred * scale, scale)


def local_heads(
    tokens,
    first_gain,
    first_shift,
    joint_weight,
    joint_bias,
    output_weight,
    output_bias,
    second_gain,
    second_shift,
    expand_weight,
    expand_bias,
    reduce_weight,
    reduce_bias,
    cotangent,
):
    dp_count, seq_count, blk_count = (lax.axis_size(axis) for axis in ALL)
    dp, seq, blk = (lax.axis_index(axis) for axis in ALL)
    plane_count, owner_count = seq_count * blk_count, dp_count * blk_count
    all_count = dp_count * plane_count
    owner = dp * blk_count + blk
    me = (dp * seq_count + seq) * blk_count + blk
    heads = H // plane_count
    tok_rows, width = tokens.shape
    own_width = width // owner_count
    half = heads * 3 * HD
    out_half = heads * HD
    hidden_local = expand_weight.shape[1]
    core = blk_count
    chips = [p for p in range(plane_count) if not p & core]
    seq_chips = [p for p in range(seq_count) if not p & 1]

    def gather_plane(block):
        mine = spread(block, PLANE, plane_count, chips[1:])
        low_part = jnp.concatenate(mine, 0)
        other = swap(low_part, PLANE, plane_count, core)
        rows = block.shape[0]
        pieces = {}
        for place, chip in enumerate(chips):
            pieces[chip] = low_part[place * rows : (place + 1) * rows]
            pieces[chip ^ core] = other[place * rows : (place + 1) * rows]
        return jnp.concatenate([pieces[p] for p in range(plane_count)], 0)

    def scatter_plane(part):
        rows = part.shape[0] // plane_count
        block = [part[p * rows : (p + 1) * rows] for p in range(plane_count)]
        away = low(jnp.concatenate([block[chip ^ core] for chip in chips], 0))
        came = swap(away, PLANE, plane_count, core).astype(jnp.float32)
        total = [block[chip] + came[q * rows : (q + 1) * rows] for q, chip in enumerate(chips)]
        result = total[0]
        for q, chip in enumerate(chips):
            if chip:
                result = result + swap(low(total[q]), PLANE, plane_count, chip).astype(jnp.float32)
        return result

    def gather_seq(block):
        mine = spread(block, "seq", seq_count, seq_chips[1:])
        low_part = jnp.concatenate(mine, 0)
        return jnp.concatenate([low_part, swap(low_part, "seq", seq_count, 1)], 0)

    def scatter_seq(part):
        middle_row = part.shape[0] // 2
        rows = part.shape[0] // seq_count
        came = swap(low(part[middle_row:]), "seq", seq_count, 1).astype(jnp.float32)
        total = part[:middle_row] + came
        result = total[:rows]
        for q, chip in enumerate(seq_chips):
            if chip:
                piece = low(total[q * rows : (q + 1) * rows])
                result = result + swap(piece, "seq", seq_count, chip).astype(jnp.float32)
        return result

    def scatter_small(values):
        values = permute_rows(values, me, all_count)
        count = all_count // 2
        while count:
            values = values[:count] + swap(values[count:], ALL, all_count, count)
            count //= 2
        return values[0]

    packed = jnp.concatenate(
        [first_gain, first_shift, output_bias, second_gain, second_shift, reduce_bias]
        + [joint_bias.reshape(-1), expand_bias.reshape(-1)]
    )[None]
    small = packed
    count = 1
    while count < all_count:
        small = jnp.concatenate([small, swap(small, ALL, all_count, count)], 0)
        count *= 2
    small = permute_rows(small, me, all_count)
    piece = first_gain.shape[0]
    gain_one, shift_one, out_shift, gain_two, shift_two, reduce_shift = [
        small[:, k * piece : (k + 1) * piece].reshape(-1).astype(jnp.float32) for k in range(6)
    ]
    by_place = small[:, 6 * piece :].reshape(dp_count, seq_count, blk_count, -1)
    group = lax.dynamic_index_in_dim(by_place, seq, 1, keepdims=False)
    pair_size = joint_bias.size
    pair = group[:, :, :pair_size].reshape((owner_count,) + joint_bias.shape)
    pair = jnp.transpose(pair, (1, 0, 2)).reshape(joint_bias.shape[0], 2 * HD)
    pair = lax.dynamic_slice_in_dim(pair, blk * heads, heads, 0).astype(jnp.float32)
    expand_shift = group[:, :, pair_size:].reshape(-1).astype(jnp.float32)

    token_group = gather_plane(tokens)
    joint_halves = joint_weight.reshape(own_width, blk_count, half)
    out_halves = output_weight.T.reshape(own_width, blk_count, out_half)
    halves = jnp.concatenate([joint_halves, out_halves], -1)
    pieces = []
    for k in range(owner_count):
        wanted = lax.dynamic_index_in_dim(halves, blk ^ (k % blk_count), 1, keepdims=False)
        pieces.append(swap(wanted, OWNERS, owner_count, k) if k else wanted)
    attention_weights = permute_rows(jnp.concatenate(pieces, 0), owner, owner_count)
    joint_local = attention_weights[:, :half]
    out_local = attention_weights[:, half:]

    def gather_owners(block):
        over_dp = spread(block, "dp", dp_count, range(1, dp_count))
        blocks = []
        for piece_dp in over_dp:
            blocks += spread(piece_dp, "blk", blk_count, range(1, blk_count))
        return jnp.concatenate(blocks, 0)

    expand_local = gather_owners(expand_weight)
    reduce_local = gather_owners(reduce_weight.T)

    def to_relative(values):
        return permute_columns(values, owner, owner_count)

    cot_group = gather_seq(to_relative(cotangent))

    xhat_group, scale_group = norm_parts(token_group.astype(jnp.float32))
    normed_one = low(xhat_group * gain_one + shift_one)
    xhat_low = low(xhat_group)
    mixed = low(matmul("tc,ck->tk", normed_one, joint_local) + local_bias(pair, heads))
    row_count = mixed.shape[0]
    by_head = mixed.reshape(row_count, heads, 3, HD)
    queries, keys, values = by_head[:, :, 0], by_head[:, :, 1], by_head[:, :, 2]
    places = (
        ((seq * blk_count + blk) ^ jnp.arange(plane_count, dtype=jnp.int32))[:, None] * tok_rows
        + jnp.arange(tok_rows, dtype=jnp.int32)[None, :]
    ).reshape(row_count)
    head_ids = (seq * blk_count + blk) * heads + jnp.arange(heads, dtype=jnp.int32)
    slopes = jnp.exp2(-8.0 * (head_ids + 1).astype(jnp.float32) / H)
    offsets = (places[None, :] - places[:, None]).astype(jnp.float32)
    scores = matmul("qhd,khd->hqk", queries, keys) * HD ** (-0.5)
    scores = scores + slopes[:, None, None] * offsets[None]
    scores = jnp.where((offsets <= 0)[None], scores, -1e30)
    weights = jnp.exp(scores - jnp.max(scores, -1, keepdims=True))
    probs = weights / jnp.sum(weights, -1, keepdims=True)
    probs_low = low(probs)
    attended = matmul("hqk,khd->qhd", probs_low, values)
    attended_low = low(attended).reshape(row_count, out_half)
    branch_sum = scatter_plane(matmul("tk,dk->td", attended_low, out_local))

    middle = tokens.astype(jnp.float32) + (branch_sum + out_shift)
    xhat_two, scale_two = norm_parts(middle)
    normed_two = low(xhat_two * gain_two + shift_two)
    normed_group = gather_seq(to_relative(normed_two))
    hidden = matmul("tc,cf->tf", normed_group, expand_local) + expand_shift
    activated, gelu_pull = jax.vjp(gelu_tanh, hidden)
    activated_low = low(activated)
    activated_grad = matmul("td,df->tf", cot_group, reduce_local)
    hidden_grad = low(gelu_pull(activated_grad)[0])
    normed_two_grad = scatter_seq(matmul("tf,cf->tc", hidden_grad, expand_local))
    normed_two_grad = to_relative(normed_two_grad)
    result_sum = to_relative(scatter_seq(matmul("tf,df->td", activated_low, reduce_local)))
    layer_output = low(middle + (result_sum + reduce_shift))

    upstream = cotangent.astype(jnp.float32)
    middle_grad = upstream + norm_back(normed_two_grad, xhat_two, scale_two, gain_two)
    branch_grad = low(middle_grad)

    def scatter_owners(part):
        rows = part.shape[0] // owner_count
        kept = []
        for k in range(0, owner_count, blk_count):
            total = part[k * rows : (k + 1) * rows]
            for b in range(1, blk_count):
                piece = low(part[(k + b) * rows : (k + b + 1) * rows])
                total = total + swap(piece, "blk", blk_count, b).astype(jnp.float32)
            kept.append(total)
        result = kept[0]
        for d in range(1, dp_count):
            result = result + swap(low(kept[d]), "dp", dp_count, d).astype(jnp.float32)
        return result

    reduce_grad = scatter_owners(matmul("td,tf->df", cot_group, activated_low)).T
    expand_grad = scatter_owners(matmul("tc,tf->cf", normed_group, hidden_grad))
    expand_shift_grad = jnp.sum(hidden_grad.astype(jnp.float32), 0)

    def small_rows(vectors, grouped):
        rows = jnp.concatenate([v.reshape(all_count, -1) for v in vectors], -1)
        size = grouped.shape[-1]
        mine = (jnp.arange(seq_count) == seq)[None, :, None, None]
        grouped = jnp.where(mine, grouped.reshape(dp_count, 1, blk_count, size), 0.0)
        return jnp.concatenate([rows, grouped.reshape(all_count, size)], -1)

    early = scatter_small(
        small_rows(
            [
                jnp.sum(branch_grad.astype(jnp.float32), 0),
                jnp.sum(normed_two_grad * xhat_two, 0),
                jnp.sum(normed_two_grad, 0),
                jnp.sum(upstream, 0),
            ],
            expand_shift_grad.reshape(owner_count, -1),
        )
    )

    branch_group = gather_plane(branch_grad)
    grad_heads = low(matmul("td,dk->tk", branch_group, out_local))
    grad_heads = grad_heads.reshape(row_count, heads, HD)
    out_grad = matmul("td,tk->dk", branch_group, attended_low)
    deltas = jnp.sum(grad_heads.astype(jnp.float32) * attended, -1)
    prob_grad = matmul("qhd,khd->hqk", grad_heads, values)
    score_grad = low(probs * (prob_grad - deltas.T[:, :, None]))
    query_grad = matmul("hqk,khd->qhd", score_grad, keys) * HD ** (-0.5)
    key_grad = matmul("hqk,qhd->khd", score_grad, queries) * HD ** (-0.5)
    value_grad = matmul("hqk,qhd->khd", probs_low, grad_heads)
    mixed_grad = low(jnp.stack([query_grad, key_grad, value_grad], 2)).reshape(row_count, half)
    normed_one_grad = scatter_plane(matmul("tk,ck->tc", mixed_grad, joint_local))
    input_norm_grad = norm_back(
        normed_one_grad, xhat_group[:tok_rows], scale_group[:tok_rows], gain_one
    )
    input_grad = low(middle_grad + input_norm_grad)

    plain_grad = matmul("tc,tk->ck", xhat_low, mixed_grad)
    mixed_sums = jnp.sum(mixed_grad.astype(jnp.float32), 0)
    joint_grad = gain_one[:, None] * plain_grad + shift_one[:, None] * mixed_sums
    joint_wide = joint_local.astype(jnp.float32)
    gain_one_part = jnp.sum(joint_wide * plain_grad, -1)
    shift_one_part = jnp.sum(joint_wide * mixed_sums, -1)

    def scatter_heads(part):
        rows = part.shape[0] // dp_count
        total = None
        for d in range(dp_count):
            piece = lax.dynamic_slice_in_dim(part, (dp ^ d) * rows, rows, 0)
            if d:
                piece = swap(low(piece), "dp", dp_count, d).astype(jnp.float32)
            total = piece if total is None else total + piece
        columns = []
        for b in range(blk_count):
            piece = lax.dynamic_slice_in_dim(total, (blk ^ b) * own_width, own_width, 0)
            if b:
                piece = swap(low(piece), "blk", blk_count, b).astype(jnp.float32)
            columns.append(piece)
        return permute_columns(jnp.concatenate(columns, -1), blk, blk_count)

    out_grad = scatter_heads(out_grad).T
    joint_grad = scatter_heads(joint_grad)
    bias_sums = mixed_sums.reshape(heads, 3, HD)
    pair_grad = jnp.concatenate([bias_sums[:, 0], bias_sums[:, 2]], -1)
    pair_rows = jnp.zeros((blk_count, heads, 2 * HD), jnp.float32)
    pair_rows = lax.dynamic_update_slice_in_dim(pair_rows, pair_grad[None], blk, 0)
    pair_rows = pair_rows.reshape(blk_count * heads, owner_count, -1)
    pair_rows = jnp.transpose(pair_rows, (1, 0, 2)).reshape(owner_count, -1)
    late = scatter_small(small_rows([gain_one_part, shift_one_part], pair_rows))
    return (
        layer_output,
        input_grad,
        late[:piece],
        late[piece : 2 * piece],
        joint_grad,
        late[2 * piece :].reshape(joint_bias.shape),
        out_grad,
        early[:piece],
        early[piece : 2 * piece],
        early[2 * piece : 3 * piece],
        expand_grad,
        early[4 * piece :].reshape(expand_bias.shape),
        reduce_grad,
        early[3 * piece : 4 * piece],
    )


def solution(mesh):
    return jax.shard_map(
        local_heads if H % (mesh.shape["seq"] * mesh.shape["blk"]) == 0 else local,
        mesh=mesh,
        in_specs=(
            P(("dp", "seq", "blk"), None),
            P(("dp", "seq", "blk")),
            P(("dp", "seq", "blk")),
            P(("dp", "blk"), "seq"),
            P("seq", ("dp", "blk")),
            P("seq", ("dp", "blk")),
            P(("dp", "seq", "blk")),
            P(("dp", "seq", "blk")),
            P(("dp", "seq", "blk")),
            P(("dp", "blk"), "seq"),
            P("seq", ("dp", "blk")),
            P("seq", ("dp", "blk")),
            P(("dp", "seq", "blk")),
            P(("dp", "seq", "blk"), None),
        ),
        out_specs=(
            P(("dp", "seq", "blk"), None),
            P(("dp", "seq", "blk"), None),
            P(("dp", "seq", "blk")),
            P(("dp", "seq", "blk")),
            P(("dp", "blk"), "seq"),
            P("seq", ("dp", "blk")),
            P("seq", ("dp", "blk")),
            P(("dp", "seq", "blk")),
            P(("dp", "seq", "blk")),
            P(("dp", "seq", "blk")),
            P(("dp", "blk"), "seq"),
            P("seq", ("dp", "blk")),
            P("seq", ("dp", "blk")),
            P(("dp", "seq", "blk")),
        ),
        check_vma=False,
    )
```

```python
import jax
import jax.numpy as jnp
from jax import lax
from jax.sharding import PartitionSpec as P

H = 16
HD = 64


epsilon = 1e-05


def layer_norm(values, gain_row, shift_row):
    average = jnp.mean(values, -1, keepdims=True)
    centred = values - average
    variance = jnp.mean(centred * centred, -1, keepdims=True)
    return centred * lax.rsqrt(variance + epsilon) * gain_row + shift_row


def local_bias(pair_local, head_local):
    paired = pair_local.reshape(head_local, 2, HD)
    return jnp.stack([paired[:, 0], jnp.zeros_like(paired[:, 0]), paired[:, 1]], axis=1).reshape(
        head_local * 3 * HD
    )


def gelu_tanh(values):
    return jax.nn.gelu(values, approximate=True)


def score_tile(query_block, key_tile, places, tile_start, slopes, scale_factor):
    tile_rows = key_tile.shape[0]
    key_places = tile_start + jnp.arange(tile_rows, dtype=jnp.int32)
    scores = (
        jnp.einsum("qhd,khd->hqk", query_block, key_tile, preferred_element_type=jnp.float32)
        * scale_factor
    )
    offsets = (key_places[None, :] - places[:, None]).astype(jnp.float32)
    scores = scores + slopes[:, None, None] * offsets[None]
    allowed = (key_places[None, :] <= places[:, None])[None]
    return (jnp.where(allowed, scores, -1e30), allowed)


def attend_forward(queries, all_keys, all_values, places, slopes):
    row_count, head_local, head_width = queries.shape
    block_rows = min(512, row_count)
    tile_rows = min(512, all_keys.shape[0])
    scale_factor = head_width ** (-0.5)
    query_blocks = queries.reshape(row_count // block_rows, block_rows, head_local, head_width)
    place_blocks = places.reshape(row_count // block_rows, block_rows)

    def one_block(block_pair):
        query_block, block_places = block_pair
        needed = (block_places[-1] + tile_rows) // tile_rows

        def one_tile(counter, state_carry):
            running_max, running_sum, running_total = state_carry
            tile_start = counter * tile_rows
            key_tile = lax.dynamic_slice_in_dim(all_keys, tile_start, tile_rows, 0)
            value_tile = lax.dynamic_slice_in_dim(all_values, tile_start, tile_rows, 0)
            scores, allowed = score_tile(
                query_block, key_tile, block_places, tile_start, slopes, scale_factor
            )
            new_max = jnp.maximum(running_max, jnp.max(scores, -1))
            weights_tile = jnp.where(allowed, jnp.exp(scores - new_max[..., None]), 0.0)
            factor = jnp.exp(running_max - new_max)
            running_sum = running_sum * factor + jnp.sum(weights_tile, -1)
            running_total = running_total * factor[..., None] + jnp.einsum(
                "hqk,khd->hqd",
                weights_tile.astype(jnp.bfloat16),
                value_tile,
                preferred_element_type=jnp.float32,
            )
            return (new_max, running_sum, running_total)

        start_state = (
            jnp.full((head_local, block_rows), -1e30, jnp.float32),
            jnp.zeros((head_local, block_rows), jnp.float32),
            jnp.zeros((head_local, block_rows, head_width), jnp.float32),
        )
        running_max, running_sum, running_total = lax.fori_loop(0, needed, one_tile, start_state)
        return (running_total / running_sum[..., None], running_max + jnp.log(running_sum))

    outputs, log_sums = lax.map(one_block, (query_blocks, place_blocks))
    outputs = jnp.transpose(outputs, (0, 2, 1, 3)).reshape(row_count, head_local, head_width)
    return (outputs, log_sums)


def attend_backward(queries, all_keys, all_values, places, slopes, grad_out, log_sums, deltas):
    row_count, head_local, head_width = queries.shape
    key_count = all_keys.shape[0]
    block_rows = min(512, row_count)
    tile_rows = min(512, key_count)
    scale_factor = head_width ** (-0.5)
    block_count = row_count // block_rows
    query_blocks = queries.reshape(block_count, block_rows, head_local, head_width)
    grad_blocks = grad_out.reshape(block_count, block_rows, head_local, head_width)
    place_blocks = places.reshape(block_count, block_rows)
    delta_blocks = jnp.transpose(deltas.reshape(block_count, block_rows, head_local), (0, 2, 1))

    def one_block(key_grads, block_inputs):
        query_block, grad_block, block_places, block_lse, block_delta = block_inputs
        needed = (block_places[-1] + tile_rows) // tile_rows

        def one_tile(counter, inner_carry):
            query_grad, key_sums = inner_carry
            tile_start = counter * tile_rows
            key_tile = lax.dynamic_slice_in_dim(all_keys, tile_start, tile_rows, 0)
            value_tile = lax.dynamic_slice_in_dim(all_values, tile_start, tile_rows, 0)
            scores, allowed = score_tile(
                query_block, key_tile, block_places, tile_start, slopes, scale_factor
            )
            probs = jnp.where(allowed, jnp.exp(scores - block_lse[..., None]), 0.0)
            value_grad = jnp.einsum(
                "hqk,qhd->khd",
                probs.astype(jnp.bfloat16),
                grad_block,
                preferred_element_type=jnp.float32,
            )
            prob_grad = jnp.einsum(
                "qhd,khd->hqk", grad_block, value_tile, preferred_element_type=jnp.float32
            )
            score_grad = (probs * (prob_grad - block_delta[..., None])).astype(jnp.bfloat16)
            query_grad = (
                query_grad
                + jnp.einsum(
                    "hqk,khd->qhd", score_grad, key_tile, preferred_element_type=jnp.float32
                )
                * scale_factor
            )
            key_grad = (
                jnp.einsum(
                    "hqk,qhd->khd", score_grad, query_block, preferred_element_type=jnp.float32
                )
                * scale_factor
            )
            current = lax.dynamic_slice_in_dim(key_sums, tile_start, tile_rows, 0)
            update = current + jnp.concatenate([key_grad, value_grad], -1)
            key_sums = lax.dynamic_update_slice_in_dim(key_sums, update, tile_start, 0)
            return (query_grad, key_sums)

        start_grad = jnp.zeros((block_rows, head_local, head_width), jnp.float32)
        query_grad, key_grads = lax.fori_loop(0, needed, one_tile, (start_grad, key_grads))
        return (key_grads, query_grad)

    start_keys = jnp.zeros((key_count, head_local, 2 * head_width), jnp.float32)
    key_grads, query_grads = lax.scan(
        one_block, start_keys, (query_blocks, grad_blocks, place_blocks, log_sums, delta_blocks)
    )
    return (query_grads.reshape(row_count, head_local, head_width), key_grads)


def local(
    tokens,
    first_gain,
    first_shift,
    joint_weight,
    joint_bias,
    output_weight,
    output_bias,
    second_gain,
    second_shift,
    expand_weight,
    expand_bias,
    reduce_weight,
    reduce_bias,
    cotangent,
):
    seq_count = lax.axis_size("seq")
    blk_count = lax.axis_size("blk")
    head_local = H // seq_count
    tok_rows = tokens.shape[0]
    inputs = tokens.astype(jnp.float32)
    small_full = (
        lax.all_gather(first_gain, ("dp", "seq", "blk"), axis=0, tiled=True),
        lax.all_gather(first_shift, ("dp", "seq", "blk"), axis=0, tiled=True),
        lax.all_gather(output_bias, ("dp", "seq", "blk"), axis=0, tiled=True),
        lax.all_gather(second_gain, ("dp", "seq", "blk"), axis=0, tiled=True),
        lax.all_gather(second_shift, ("dp", "seq", "blk"), axis=0, tiled=True),
        lax.all_gather(reduce_bias, ("dp", "seq", "blk"), axis=0, tiled=True),
    )
    gain_one, shift_one, out_shift, gain_two, shift_two, reduce_shift = [
        piece.astype(jnp.float32) for piece in small_full
    ]
    joint_local, pair_local, out_local = (
        lax.all_gather(joint_weight, ("dp", "blk"), axis=0, tiled=True),
        lax.all_gather(joint_bias, ("dp", "blk"), axis=1, tiled=True),
        lax.all_gather(output_weight, ("dp", "blk"), axis=1, tiled=True),
    )
    expand_local, expand_shift, reduce_local = (
        lax.all_gather(expand_weight, ("dp", "blk"), axis=0, tiled=True),
        lax.all_gather(expand_bias, ("dp", "blk"), axis=1, tiled=True),
        lax.all_gather(reduce_weight, ("dp", "blk"), axis=1, tiled=True),
    )
    outgoing = layer_norm(inputs, gain_one, shift_one).astype(jnp.bfloat16)
    arrived = lax.all_gather(outgoing, "seq", axis=0, tiled=True)
    row_count = arrived.shape[0]
    mixed_cols = jnp.dot(arrived, joint_local, preferred_element_type=jnp.float32)
    mixed_cols = mixed_cols + local_bias(pair_local.astype(jnp.float32), head_local)
    by_head = mixed_cols.astype(jnp.bfloat16).reshape(row_count, head_local, 3 * HD)
    queries = by_head[:, :, :HD]
    key_value = by_head[:, :, HD:].reshape(seq_count, tok_rows, head_local, 2 * HD)
    ordered = lax.all_gather(key_value, "blk", axis=1, tiled=True)
    ordered = ordered.reshape(seq_count * blk_count * tok_rows, head_local, 2 * HD)
    all_keys = ordered[:, :, :HD]
    all_values = ordered[:, :, HD:]
    places = (
        (jnp.arange(seq_count, dtype=jnp.int32)[:, None] * blk_count + lax.axis_index("blk"))
        * tok_rows
        + jnp.arange(tok_rows, dtype=jnp.int32)[None, :]
    ).reshape(row_count)
    head_ids = lax.axis_index("seq") * head_local + jnp.arange(head_local, dtype=jnp.int32)
    slopes = jnp.exp2(-8.0 * (head_ids + 1).astype(jnp.float32) / H)
    attended, log_sums = attend_forward(queries, all_keys, all_values, places, slopes)
    attended_low = attended.reshape(row_count, head_local * HD).astype(jnp.bfloat16)
    branch_part = jnp.dot(attended_low, out_local, preferred_element_type=jnp.float32)
    branch_sum = lax.psum_scatter(
        branch_part.astype(jnp.bfloat16), "seq", scatter_dimension=0, tiled=True
    ).astype(jnp.float32)
    middle = inputs + (branch_sum + out_shift)
    normed_two = layer_norm(middle, gain_two, shift_two).astype(jnp.bfloat16)
    normed_two_group, cot_group = (
        lax.all_gather(normed_two, "seq", axis=0, tiled=True),
        lax.all_gather(cotangent, "seq", axis=0, tiled=True),
    )
    hidden = jnp.dot(normed_two_group, expand_local, preferred_element_type=jnp.float32)
    hidden = hidden + expand_shift.astype(jnp.float32).reshape(-1)
    activated, gelu_pull = jax.vjp(gelu_tanh, hidden)
    activated_low = activated.astype(jnp.bfloat16)
    result_part = jnp.dot(activated_low, reduce_local, preferred_element_type=jnp.float32)
    result_sum = lax.psum_scatter(
        result_part.astype(jnp.bfloat16), "seq", scatter_dimension=0, tiled=True
    ).astype(jnp.float32)
    layer_output = (middle + (result_sum + reduce_shift)).astype(jnp.bfloat16)
    upstream = cotangent.astype(jnp.float32)
    reduce_grad = jnp.einsum(
        "tf,td->fd", activated_low, cot_group, preferred_element_type=jnp.float32
    )
    reduce_shift_grad = jnp.sum(upstream, 0)
    activated_grad = jnp.einsum(
        "td,fd->tf", cot_group, reduce_local, preferred_element_type=jnp.float32
    )
    hidden_grad = gelu_pull(activated_grad)[0].astype(jnp.bfloat16)
    expand_grad = jnp.einsum(
        "tc,tf->cf", normed_two_group, hidden_grad, preferred_element_type=jnp.float32
    )
    expand_shift_grad = jnp.sum(hidden_grad.astype(jnp.float32), 0).reshape(
        expand_shift.shape[0], -1
    )
    normed_two_part = jnp.einsum(
        "tf,cf->tc", hidden_grad, expand_local, preferred_element_type=jnp.float32
    )
    normed_two_grad = lax.psum_scatter(
        normed_two_part.astype(jnp.bfloat16), "seq", scatter_dimension=0, tiled=True
    ).astype(jnp.float32)
    unused_value, norm_two_pull = jax.vjp(layer_norm, middle, gain_two, shift_two)
    middle_norm_grad, gain_two_grad, shift_two_grad = norm_two_pull(normed_two_grad)
    middle_grad = upstream + middle_norm_grad
    branch_grad = middle_grad.astype(jnp.bfloat16)
    out_shift_grad = jnp.sum(branch_grad.astype(jnp.float32), 0)
    branch_group = lax.all_gather(branch_grad, "seq", axis=0, tiled=True)
    out_grad = jnp.einsum(
        "tc,td->cd", attended_low, branch_group, preferred_element_type=jnp.float32
    )
    attended_grad = jnp.einsum(
        "td,cd->tc", branch_group, out_local, preferred_element_type=jnp.float32
    ).astype(jnp.bfloat16)
    grad_heads = attended_grad.reshape(row_count, head_local, HD)
    deltas = jnp.sum(grad_heads.astype(jnp.float32) * attended, -1)
    query_grads, key_grads = attend_backward(
        queries, all_keys, all_values, places, slopes, grad_heads, log_sums, deltas
    )
    key_terms = key_grads.reshape(seq_count, blk_count * tok_rows, head_local * 2 * HD)
    key_sums = lax.psum_scatter(
        key_terms.astype(jnp.bfloat16), "blk", scatter_dimension=1, tiled=True
    ).astype(jnp.float32)
    combined = jnp.concatenate(
        [
            query_grads.astype(jnp.bfloat16),
            key_sums.reshape(row_count, head_local, 2 * HD).astype(jnp.bfloat16),
        ],
        -1,
    )
    mixed_grad = combined.reshape(row_count, head_local * 3 * HD)
    joint_grad = jnp.einsum("tc,tk->ck", arrived, mixed_grad, preferred_element_type=jnp.float32)
    bias_sums = jnp.sum(mixed_grad.astype(jnp.float32), 0).reshape(head_local, 3, HD)
    pair_grad = jnp.concatenate([bias_sums[:, 0], bias_sums[:, 2]], -1)
    normed_one_part = jnp.einsum(
        "tk,ck->tc", mixed_grad, joint_local, preferred_element_type=jnp.float32
    )
    normed_one_grad = lax.psum_scatter(
        normed_one_part.astype(jnp.bfloat16), "seq", scatter_dimension=0, tiled=True
    ).astype(jnp.float32)
    unused_first, norm_one_pull = jax.vjp(layer_norm, inputs, gain_one, shift_one)
    input_norm_grad, gain_one_grad, shift_one_grad = norm_one_pull(normed_one_grad)
    input_grad = (middle_grad + input_norm_grad).astype(jnp.bfloat16)
    weight_sums = (
        lax.psum_scatter(
            joint_grad.astype(jnp.bfloat16), ("dp", "blk"), scatter_dimension=0, tiled=True
        ).astype(jnp.float32),
        lax.psum_scatter(
            pair_grad.astype(jnp.bfloat16), ("dp", "blk"), scatter_dimension=1, tiled=True
        ).astype(jnp.float32),
        lax.psum_scatter(
            out_grad.astype(jnp.bfloat16), ("dp", "blk"), scatter_dimension=1, tiled=True
        ).astype(jnp.float32),
        lax.psum_scatter(
            expand_grad.astype(jnp.bfloat16), ("dp", "blk"), scatter_dimension=0, tiled=True
        ).astype(jnp.float32),
        lax.psum_scatter(
            expand_shift_grad.astype(jnp.bfloat16), ("dp", "blk"), scatter_dimension=1, tiled=True
        ).astype(jnp.float32),
        lax.psum_scatter(
            reduce_grad.astype(jnp.bfloat16), ("dp", "blk"), scatter_dimension=1, tiled=True
        ).astype(jnp.float32),
    )
    small_sums = (
        lax.psum_scatter(gain_one_grad, ("dp", "seq", "blk"), scatter_dimension=0, tiled=True),
        lax.psum_scatter(shift_one_grad, ("dp", "seq", "blk"), scatter_dimension=0, tiled=True),
        lax.psum_scatter(out_shift_grad, ("dp", "seq", "blk"), scatter_dimension=0, tiled=True),
        lax.psum_scatter(gain_two_grad, ("dp", "seq", "blk"), scatter_dimension=0, tiled=True),
        lax.psum_scatter(shift_two_grad, ("dp", "seq", "blk"), scatter_dimension=0, tiled=True),
        lax.psum_scatter(reduce_shift_grad, ("dp", "seq", "blk"), scatter_dimension=0, tiled=True),
    )
    return (
        layer_output,
        input_grad,
        small_sums[0],
        small_sums[1],
        weight_sums[0],
        weight_sums[1],
        weight_sums[2],
        small_sums[2],
        small_sums[3],
        small_sums[4],
        weight_sums[3],
        weight_sums[4],
        weight_sums[5],
        small_sums[5],
    )


ALL = ("dp", "seq", "blk")
PLANE = ("seq", "blk")


def swap(value, axes, count, offset):
    return lax.ppermute(value, axes, [(i, i ^ offset) for i in range(count)])


def reorder(values, index, parts, axis):
    size = values.shape[axis] // parts
    blocks = [
        lax.dynamic_slice_in_dim(values, (index ^ p) * size, size, axis) for p in range(parts)
    ]
    return jnp.concatenate(blocks, axis)


def matmul(spec, left, right):
    return jnp.einsum(spec, left, right, preferred_element_type=jnp.float32)


def low(value):
    return value.astype(jnp.bfloat16)


def wide(value):
    return value.astype(jnp.float32)


def norm_parts(values):
    average = jnp.mean(values, -1, keepdims=True)
    centred = values - average
    variance = jnp.mean(centred * centred, -1, keepdims=True)
    scale = lax.rsqrt(variance + epsilon)
    return (centred * scale, scale)


def norm_back(grad, xhat, scale, gain_row):
    scaled = grad * gain_row
    mean_scaled = jnp.mean(scaled, -1, keepdims=True)
    mean_product = jnp.mean(scaled * xhat, -1, keepdims=True)
    return scale * (scaled - mean_scaled - xhat * mean_product)


def local_heads(
    tokens,
    first_gain,
    first_shift,
    joint_weight,
    joint_bias,
    output_weight,
    output_bias,
    second_gain,
    second_shift,
    expand_weight,
    expand_bias,
    reduce_weight,
    reduce_bias,
    cotangent,
):
    dp_count, seq_count, blk_count = (lax.axis_size(axis) for axis in ALL)
    dp, seq, blk = (lax.axis_index(axis) for axis in ALL)
    plane_count = seq_count * blk_count
    place = seq * blk_count + blk
    heads = H // plane_count
    tok_rows, width = tokens.shape
    own_width = width // (dp_count * blk_count)
    qkv = heads * 3 * HD
    out_width = heads * HD
    units = expand_weight.shape[1] // blk_count
    core = blk_count
    chips = [p for p in range(plane_count) if not p & core]
    order = chips + [p ^ core for p in chips]

    def gather_plane(block):
        mine = [block] + [swap(block, PLANE, plane_count, chip) for chip in chips[1:]]
        mine = jnp.concatenate(mine, 0)
        return jnp.concatenate([mine, swap(mine, PLANE, plane_count, core)], 0)

    def scatter_plane(part):
        middle_row = part.shape[0] // 2
        came = swap(low(part[middle_row:]), PLANE, plane_count, core)
        total = part[:middle_row] + wide(came)
        rows = middle_row // len(chips)
        pieces = [low(total[q * rows : (q + 1) * rows]) for q in range(1, len(chips))]
        result = total[:rows]
        for chip, piece in zip(chips[1:], pieces):
            result = result + wide(swap(piece, PLANE, plane_count, chip))
        return result

    def exchange_blk(parts):
        rows = parts.shape[0] // blk_count
        taken = []
        for b in range(blk_count):
            piece = lax.dynamic_slice_in_dim(parts, (blk ^ b) * rows, rows, 0)
            taken.append(swap(low(piece), "blk", blk_count, b) if b else piece)
        return taken

    def gather_owners(halves, extra=None):
        taken = []
        for b in range(blk_count):
            piece = lax.dynamic_index_in_dim(halves, blk ^ b, 1, keepdims=False)
            taken.append(swap(piece, "blk", blk_count, b) if b else piece)
        block = reorder(jnp.concatenate(taken, 0), blk, blk_count, 0)
        if extra is not None:
            block = jnp.concatenate([block, extra], 0)
        return [block] + [swap(block, "dp", dp_count, d) for d in range(1, dp_count)]

    def scatter_dp(parts):
        total = parts[0]
        for d in range(1, dp_count):
            total = total + wide(swap(low(parts[d]), "dp", dp_count, d))
        return total

    def in_columns(taken, size):
        return reorder(jnp.concatenate([wide(t) for t in taken], -1), blk, blk_count, 1)

    packed = jnp.concatenate(
        [first_gain, first_shift, output_bias, second_gain, second_shift, reduce_bias]
        + [joint_bias.reshape(-1), expand_bias.reshape(-1)]
    )[None]
    bits = [1 << b for b in range(plane_count.bit_length() - 1)]
    for bit in bits:
        packed = jnp.concatenate([packed, swap(packed, PLANE, plane_count, bit)], 0)
    piece = first_gain.shape[0]
    small_size = packed.shape[1]

    joint_halves = joint_weight.reshape(own_width, blk_count, qkv)
    out_halves = output_weight.T.reshape(own_width, blk_count, out_width)
    columns = qkv + out_width
    small_rows = 16 * -(-plane_count * small_size // (16 * columns))
    flat = jnp.pad(packed.reshape(-1), (0, small_rows * columns - plane_count * small_size))
    blocks = gather_owners(
        jnp.concatenate([joint_halves, out_halves], -1), flat.reshape(small_rows, columns)
    )
    cut = blk_count * own_width
    attention_weights = jnp.concatenate([block[:cut] for block in blocks], 0)
    joint_local, out_local = attention_weights[:, :qkv], attention_weights[:, qkv:]
    small = jnp.stack(
        [
            block[cut:].reshape(-1)[: plane_count * small_size].reshape(plane_count, small_size)
            for block in blocks
        ],
        0,
    )
    small = reorder(small, place, plane_count, 1)
    gain_one, shift_one, out_shift, gain_two, shift_two, reduce_shift = [
        wide(small[:, :, k * piece : (k + 1) * piece]).reshape(-1) for k in range(6)
    ]
    group = small.reshape(dp_count, seq_count, blk_count, small_size)
    group = lax.dynamic_index_in_dim(group, seq, 1, keepdims=False)
    group = reorder(group, dp, dp_count, 0)
    pair_size = joint_bias.size
    pair = group[:, :, 6 * piece : 6 * piece + pair_size]
    pair = jnp.transpose(pair.reshape((-1,) + joint_bias.shape), (1, 0, 2)).reshape(-1, 2 * HD)
    pair = wide(lax.dynamic_slice_in_dim(pair, blk * heads, heads, 0))
    expand_shift = wide(group[:, :, 6 * piece + pair_size :]).reshape(blk_count, units)
    expand_shift = lax.dynamic_index_in_dim(expand_shift, blk, 0, keepdims=False)

    tokens_own = reorder(tokens, dp, dp_count, 1)
    token_group = gather_plane(tokens_own)
    cotangent_own = reorder(cotangent, dp, dp_count, 1)
    cot_group = gather_plane(cotangent_own)

    expand_halves = expand_weight.reshape(own_width, blk_count, units)
    reduce_halves = reduce_weight.T.reshape(own_width, blk_count, units)
    forward_weights = jnp.concatenate(
        gather_owners(jnp.concatenate([expand_halves, reduce_halves], -1)), 0
    )
    expand_local, reduce_local = forward_weights[:, :units], forward_weights[:, units:]

    xhat_group, scale_group = norm_parts(wide(token_group))
    normed_one = low(xhat_group * gain_one + shift_one)
    xhat_low = low(xhat_group)
    mixed = low(matmul("tc,ck->tk", normed_one, joint_local) + local_bias(pair, heads))
    row_count = mixed.shape[0]
    by_head = mixed.reshape(row_count, heads, 3, HD)
    queries, keys, values = by_head[:, :, 0], by_head[:, :, 1], by_head[:, :, 2]
    places = (
        (place ^ jnp.array(order, jnp.int32))[:, None] * tok_rows
        + jnp.arange(tok_rows, dtype=jnp.int32)[None, :]
    ).reshape(row_count)
    head_ids = place * heads + jnp.arange(heads, dtype=jnp.int32)
    slopes = jnp.exp2(-8.0 * (head_ids + 1).astype(jnp.float32) / H)
    offsets = (places[None, :] - places[:, None]).astype(jnp.float32)
    scores = matmul("qhd,khd->hqk", queries, keys) * HD ** (-0.5)
    scores = scores + slopes[:, None, None] * offsets[None]
    scores = jnp.where((offsets <= 0)[None], scores, -1e30)
    weights = jnp.exp(scores - jnp.max(scores, -1, keepdims=True))
    probs = weights / jnp.sum(weights, -1, keepdims=True)
    probs_low = low(probs)
    attended = matmul("hqk,khd->qhd", probs_low, values)
    attended_low = low(attended).reshape(row_count, out_width)
    branch_sum = scatter_plane(matmul("tk,dk->td", attended_low, out_local))

    middle = wide(tokens_own) + (branch_sum + out_shift)
    xhat_two, scale_two = norm_parts(middle)
    normed_group = gather_plane(low(xhat_two * gain_two + shift_two))
    hidden = matmul("tc,cf->tf", normed_group, expand_local) + expand_shift
    activated, gelu_pull = jax.vjp(gelu_tanh, hidden)
    activated_low = low(activated)
    activated_grad = matmul("td,df->tf", cot_group, reduce_local)
    hidden_grad = low(gelu_pull(activated_grad)[0])
    normed_two_grad = scatter_plane(matmul("tf,cf->tc", hidden_grad, expand_local))
    result_sum = scatter_plane(matmul("tf,df->td", activated_low, reduce_local))
    layer_output = reorder(low(middle + (result_sum + reduce_shift)), dp, dp_count, 1)

    upstream = wide(cotangent_own)
    middle_grad = upstream + norm_back(normed_two_grad, xhat_two, scale_two, gain_two)
    branch_grad = low(middle_grad)

    expand_grad = matmul("tc,tf->cf", normed_group, hidden_grad)
    reduce_grad = matmul("td,tf->df", cot_group, activated_low)
    forward_grad = jnp.concatenate([expand_grad, reduce_grad], -1)
    forward_grad = scatter_dp([forward_grad[d * cut : (d + 1) * cut] for d in range(dp_count)])
    forward_grad = exchange_blk(forward_grad)
    expand_grad = in_columns([t[:, :units] for t in forward_grad], units)
    reduce_grad = in_columns([t[:, units:] for t in forward_grad], units).T

    branch_group = gather_plane(branch_grad)
    grad_heads = low(matmul("td,dk->tk", branch_group, out_local))
    grad_heads = grad_heads.reshape(row_count, heads, HD)
    deltas = jnp.sum(wide(grad_heads) * attended, -1)
    prob_grad = matmul("qhd,khd->hqk", grad_heads, values)
    score_grad = low(probs * (prob_grad - deltas.T[:, :, None]))
    query_grad = matmul("hqk,khd->qhd", score_grad, keys) * HD ** (-0.5)
    key_grad = matmul("hqk,qhd->khd", score_grad, queries) * HD ** (-0.5)
    value_grad = matmul("hqk,qhd->khd", probs_low, grad_heads)
    mixed_grad = low(jnp.stack([query_grad, key_grad, value_grad], 2)).reshape(row_count, qkv)
    normed_one_grad = scatter_plane(matmul("tk,ck->tc", mixed_grad, joint_local))
    input_norm_grad = norm_back(
        normed_one_grad, xhat_group[:tok_rows], scale_group[:tok_rows], gain_one
    )
    input_grad = reorder(low(middle_grad + input_norm_grad), dp, dp_count, 1)

    plain_grad = matmul("tc,tk->ck", xhat_low, mixed_grad)
    mixed_sums = jnp.sum(wide(mixed_grad), 0)
    joint_grad = gain_one[:, None] * plain_grad + shift_one[:, None] * mixed_sums
    out_grad = matmul("td,tk->dk", branch_group, attended_low)
    joint_wide = wide(joint_local)
    vectors = [
        jnp.sum(joint_wide * plain_grad, -1),
        jnp.sum(joint_wide * mixed_sums, -1),
        jnp.sum(wide(branch_grad), 0),
        jnp.sum(normed_two_grad * xhat_two, 0),
        jnp.sum(normed_two_grad, 0),
        jnp.sum(upstream, 0),
    ]
    vectors = jnp.concatenate([v.reshape(dp_count, plane_count, piece) for v in vectors], -1)

    bias_sums = mixed_sums.reshape(heads, 3, HD)
    pair_grad = jnp.concatenate([bias_sums[:, 0], bias_sums[:, 2]], -1)
    pair_rows = jnp.zeros((blk_count, heads, 2 * HD), jnp.float32)
    pair_rows = lax.dynamic_update_slice_in_dim(pair_rows, pair_grad[None], blk, 0)
    pair_rows = pair_rows.reshape(blk_count * heads, dp_count * blk_count, -1)
    pair_rows = jnp.transpose(pair_rows, (1, 0, 2)).reshape(dp_count, blk_count, -1)
    unit_rows = jnp.zeros((blk_count, units), jnp.float32)
    unit_rows = lax.dynamic_update_slice_in_dim(
        unit_rows, jnp.sum(wide(hidden_grad), 0)[None], blk, 0
    ).reshape(dp_count, blk_count, -1)
    grouped = reorder(jnp.concatenate([pair_rows, unit_rows], -1), dp, dp_count, 0)
    mine = (jnp.arange(seq_count) == seq)[None, :, None, None]
    grouped = jnp.where(mine, grouped[:, None], 0.0).reshape(dp_count, plane_count, -1)
    small_grad = jnp.concatenate([vectors, grouped], -1).reshape(dp_count, -1)
    small_grad = jnp.pad(
        small_grad, ((0, 0), (0, small_rows * columns - plane_count * small_size))
    ).reshape(dp_count, small_rows, columns)

    attention_grad = jnp.concatenate([joint_grad, out_grad], -1).reshape(dp_count, cut, columns)
    attention_grad = jnp.concatenate([attention_grad, small_grad], 1)
    attention_grad = scatter_dp([attention_grad[d] for d in range(dp_count)])
    small_grad = attention_grad[cut:].reshape(-1)[: plane_count * small_size]
    attention_grad = exchange_blk(attention_grad[:cut])
    joint_grad = in_columns([t[:, :qkv] for t in attention_grad], qkv)
    out_grad = in_columns([t[:, qkv:] for t in attention_grad], out_width).T
    small_grad = reorder(small_grad.reshape(plane_count, small_size), place, plane_count, 0)
    for bit in reversed(bits):
        small_grad = small_grad[:bit] + swap(small_grad[bit:], PLANE, plane_count, bit)
    small_grad = small_grad[0]
    return (
        layer_output,
        input_grad,
        small_grad[:piece],
        small_grad[piece : 2 * piece],
        joint_grad,
        small_grad[6 * piece : 6 * piece + pair_size].reshape(joint_bias.shape),
        out_grad,
        small_grad[2 * piece : 3 * piece],
        small_grad[3 * piece : 4 * piece],
        small_grad[4 * piece : 5 * piece],
        expand_grad,
        small_grad[6 * piece + pair_size :].reshape(expand_bias.shape),
        reduce_grad,
        small_grad[5 * piece : 6 * piece],
    )


def solution(mesh):
    return jax.shard_map(
        local_heads if H % (mesh.shape["seq"] * mesh.shape["blk"]) == 0 else local,
        mesh=mesh,
        in_specs=(
            P(("dp", "seq", "blk"), None),
            P(("dp", "seq", "blk")),
            P(("dp", "seq", "blk")),
            P(("dp", "blk"), "seq"),
            P("seq", ("dp", "blk")),
            P("seq", ("dp", "blk")),
            P(("dp", "seq", "blk")),
            P(("dp", "seq", "blk")),
            P(("dp", "seq", "blk")),
            P(("dp", "blk"), "seq"),
            P("seq", ("dp", "blk")),
            P("seq", ("dp", "blk")),
            P(("dp", "seq", "blk")),
            P(("dp", "seq", "blk"), None),
        ),
        out_specs=(
            P(("dp", "seq", "blk"), None),
            P(("dp", "seq", "blk"), None),
            P(("dp", "seq", "blk")),
            P(("dp", "seq", "blk")),
            P(("dp", "blk"), "seq"),
            P("seq", ("dp", "blk")),
            P("seq", ("dp", "blk")),
            P(("dp", "seq", "blk")),
            P(("dp", "seq", "blk")),
            P(("dp", "seq", "blk")),
            P(("dp", "blk"), "seq"),
            P("seq", ("dp", "blk")),
            P("seq", ("dp", "blk")),
            P(("dp", "seq", "blk")),
        ),
        check_vma=False,
    )
```

```python
import functools

import jax
import jax.numpy as jnp
from jax import lax
from jax.experimental import pallas as pl
from jax.experimental.pallas import tpu as pltpu
from jax.sharding import PartitionSpec as P

H = 16
HD = 64


epsilon = 1e-05


def layer_norm(values, gain_row, shift_row):
    average = jnp.mean(values, -1, keepdims=True)
    centred = values - average
    variance = jnp.mean(centred * centred, -1, keepdims=True)
    return centred * lax.rsqrt(variance + epsilon) * gain_row + shift_row


def local_bias(pair_local, head_local):
    paired = pair_local.reshape(head_local, 2, HD)
    return jnp.stack([paired[:, 0], jnp.zeros_like(paired[:, 0]), paired[:, 1]], axis=1).reshape(
        head_local * 3 * HD
    )


def gelu_tanh(values):
    return jax.nn.gelu(values, approximate=True)


def score_tile(query_block, key_tile, places, tile_start, slopes, scale_factor):
    tile_rows = key_tile.shape[0]
    key_places = tile_start + jnp.arange(tile_rows, dtype=jnp.int32)
    scores = (
        jnp.einsum("qhd,khd->hqk", query_block, key_tile, preferred_element_type=jnp.float32)
        * scale_factor
    )
    offsets = (key_places[None, :] - places[:, None]).astype(jnp.float32)
    scores = scores + slopes[:, None, None] * offsets[None]
    allowed = (key_places[None, :] <= places[:, None])[None]
    return (jnp.where(allowed, scores, -1e30), allowed)


def attend_forward(queries, all_keys, all_values, places, slopes):
    row_count, head_local, head_width = queries.shape
    block_rows = min(512, row_count)
    tile_rows = min(512, all_keys.shape[0])
    scale_factor = head_width ** (-0.5)
    query_blocks = queries.reshape(row_count // block_rows, block_rows, head_local, head_width)
    place_blocks = places.reshape(row_count // block_rows, block_rows)

    def one_block(block_pair):
        query_block, block_places = block_pair
        needed = (block_places[-1] + tile_rows) // tile_rows

        def one_tile(counter, state_carry):
            running_max, running_sum, running_total = state_carry
            tile_start = counter * tile_rows
            key_tile = lax.dynamic_slice_in_dim(all_keys, tile_start, tile_rows, 0)
            value_tile = lax.dynamic_slice_in_dim(all_values, tile_start, tile_rows, 0)
            scores, allowed = score_tile(
                query_block, key_tile, block_places, tile_start, slopes, scale_factor
            )
            new_max = jnp.maximum(running_max, jnp.max(scores, -1))
            weights_tile = jnp.where(allowed, jnp.exp(scores - new_max[..., None]), 0.0)
            factor = jnp.exp(running_max - new_max)
            running_sum = running_sum * factor + jnp.sum(weights_tile, -1)
            running_total = running_total * factor[..., None] + jnp.einsum(
                "hqk,khd->hqd",
                weights_tile.astype(jnp.bfloat16),
                value_tile,
                preferred_element_type=jnp.float32,
            )
            return (new_max, running_sum, running_total)

        start_state = (
            jnp.full((head_local, block_rows), -1e30, jnp.float32),
            jnp.zeros((head_local, block_rows), jnp.float32),
            jnp.zeros((head_local, block_rows, head_width), jnp.float32),
        )
        running_max, running_sum, running_total = lax.fori_loop(0, needed, one_tile, start_state)
        return (running_total / running_sum[..., None], running_max + jnp.log(running_sum))

    outputs, log_sums = lax.map(one_block, (query_blocks, place_blocks))
    outputs = jnp.transpose(outputs, (0, 2, 1, 3)).reshape(row_count, head_local, head_width)
    return (outputs, log_sums)


def attend_backward(queries, all_keys, all_values, places, slopes, grad_out, log_sums, deltas):
    row_count, head_local, head_width = queries.shape
    key_count = all_keys.shape[0]
    block_rows = min(512, row_count)
    tile_rows = min(512, key_count)
    scale_factor = head_width ** (-0.5)
    block_count = row_count // block_rows
    query_blocks = queries.reshape(block_count, block_rows, head_local, head_width)
    grad_blocks = grad_out.reshape(block_count, block_rows, head_local, head_width)
    place_blocks = places.reshape(block_count, block_rows)
    delta_blocks = jnp.transpose(deltas.reshape(block_count, block_rows, head_local), (0, 2, 1))

    def one_block(key_grads, block_inputs):
        query_block, grad_block, block_places, block_lse, block_delta = block_inputs
        needed = (block_places[-1] + tile_rows) // tile_rows

        def one_tile(counter, inner_carry):
            query_grad, key_sums = inner_carry
            tile_start = counter * tile_rows
            key_tile = lax.dynamic_slice_in_dim(all_keys, tile_start, tile_rows, 0)
            value_tile = lax.dynamic_slice_in_dim(all_values, tile_start, tile_rows, 0)
            scores, allowed = score_tile(
                query_block, key_tile, block_places, tile_start, slopes, scale_factor
            )
            probs = jnp.where(allowed, jnp.exp(scores - block_lse[..., None]), 0.0)
            value_grad = jnp.einsum(
                "hqk,qhd->khd",
                probs.astype(jnp.bfloat16),
                grad_block,
                preferred_element_type=jnp.float32,
            )
            prob_grad = jnp.einsum(
                "qhd,khd->hqk", grad_block, value_tile, preferred_element_type=jnp.float32
            )
            score_grad = (probs * (prob_grad - block_delta[..., None])).astype(jnp.bfloat16)
            query_grad = (
                query_grad
                + jnp.einsum(
                    "hqk,khd->qhd", score_grad, key_tile, preferred_element_type=jnp.float32
                )
                * scale_factor
            )
            key_grad = (
                jnp.einsum(
                    "hqk,qhd->khd", score_grad, query_block, preferred_element_type=jnp.float32
                )
                * scale_factor
            )
            current = lax.dynamic_slice_in_dim(key_sums, tile_start, tile_rows, 0)
            update = current + jnp.concatenate([key_grad, value_grad], -1)
            key_sums = lax.dynamic_update_slice_in_dim(key_sums, update, tile_start, 0)
            return (query_grad, key_sums)

        start_grad = jnp.zeros((block_rows, head_local, head_width), jnp.float32)
        query_grad, key_grads = lax.fori_loop(0, needed, one_tile, (start_grad, key_grads))
        return (key_grads, query_grad)

    start_keys = jnp.zeros((key_count, head_local, 2 * head_width), jnp.float32)
    key_grads, query_grads = lax.scan(
        one_block, start_keys, (query_blocks, grad_blocks, place_blocks, log_sums, delta_blocks)
    )
    return (query_grads.reshape(row_count, head_local, head_width), key_grads)


def local(
    tokens,
    first_gain,
    first_shift,
    joint_weight,
    joint_bias,
    output_weight,
    output_bias,
    second_gain,
    second_shift,
    expand_weight,
    expand_bias,
    reduce_weight,
    reduce_bias,
    cotangent,
):
    seq_count = lax.axis_size("seq")
    blk_count = lax.axis_size("blk")
    head_local = H // seq_count
    tok_rows = tokens.shape[0]
    inputs = tokens.astype(jnp.float32)
    small_full = (
        lax.all_gather(first_gain, ("dp", "seq", "blk"), axis=0, tiled=True),
        lax.all_gather(first_shift, ("dp", "seq", "blk"), axis=0, tiled=True),
        lax.all_gather(output_bias, ("dp", "seq", "blk"), axis=0, tiled=True),
        lax.all_gather(second_gain, ("dp", "seq", "blk"), axis=0, tiled=True),
        lax.all_gather(second_shift, ("dp", "seq", "blk"), axis=0, tiled=True),
        lax.all_gather(reduce_bias, ("dp", "seq", "blk"), axis=0, tiled=True),
    )
    gain_one, shift_one, out_shift, gain_two, shift_two, reduce_shift = [
        piece.astype(jnp.float32) for piece in small_full
    ]
    joint_local, pair_local, out_local = (
        lax.all_gather(joint_weight, ("dp", "blk"), axis=0, tiled=True),
        lax.all_gather(joint_bias, ("dp", "blk"), axis=1, tiled=True),
        lax.all_gather(output_weight, ("dp", "blk"), axis=1, tiled=True),
    )
    expand_local, expand_shift, reduce_local = (
        lax.all_gather(expand_weight, ("dp", "blk"), axis=0, tiled=True),
        lax.all_gather(expand_bias, ("dp", "blk"), axis=1, tiled=True),
        lax.all_gather(reduce_weight, ("dp", "blk"), axis=1, tiled=True),
    )
    outgoing = layer_norm(inputs, gain_one, shift_one).astype(jnp.bfloat16)
    arrived = lax.all_gather(outgoing, "seq", axis=0, tiled=True)
    row_count = arrived.shape[0]
    mixed_cols = jnp.dot(arrived, joint_local, preferred_element_type=jnp.float32)
    mixed_cols = mixed_cols + local_bias(pair_local.astype(jnp.float32), head_local)
    by_head = mixed_cols.astype(jnp.bfloat16).reshape(row_count, head_local, 3 * HD)
    queries = by_head[:, :, :HD]
    key_value = by_head[:, :, HD:].reshape(seq_count, tok_rows, head_local, 2 * HD)
    ordered = lax.all_gather(key_value, "blk", axis=1, tiled=True)
    ordered = ordered.reshape(seq_count * blk_count * tok_rows, head_local, 2 * HD)
    all_keys = ordered[:, :, :HD]
    all_values = ordered[:, :, HD:]
    places = (
        (jnp.arange(seq_count, dtype=jnp.int32)[:, None] * blk_count + lax.axis_index("blk"))
        * tok_rows
        + jnp.arange(tok_rows, dtype=jnp.int32)[None, :]
    ).reshape(row_count)
    head_ids = lax.axis_index("seq") * head_local + jnp.arange(head_local, dtype=jnp.int32)
    slopes = jnp.exp2(-8.0 * (head_ids + 1).astype(jnp.float32) / H)
    attended, log_sums = attend_forward(queries, all_keys, all_values, places, slopes)
    attended_low = attended.reshape(row_count, head_local * HD).astype(jnp.bfloat16)
    branch_part = jnp.dot(attended_low, out_local, preferred_element_type=jnp.float32)
    branch_sum = lax.psum_scatter(
        branch_part.astype(jnp.bfloat16), "seq", scatter_dimension=0, tiled=True
    ).astype(jnp.float32)
    middle = inputs + (branch_sum + out_shift)
    normed_two = layer_norm(middle, gain_two, shift_two).astype(jnp.bfloat16)
    normed_two_group, cot_group = (
        lax.all_gather(normed_two, "seq", axis=0, tiled=True),
        lax.all_gather(cotangent, "seq", axis=0, tiled=True),
    )
    hidden = jnp.dot(normed_two_group, expand_local, preferred_element_type=jnp.float32)
    hidden = hidden + expand_shift.astype(jnp.float32).reshape(-1)
    activated, gelu_pull = jax.vjp(gelu_tanh, hidden)
    activated_low = activated.astype(jnp.bfloat16)
    result_part = jnp.dot(activated_low, reduce_local, preferred_element_type=jnp.float32)
    result_sum = lax.psum_scatter(
        result_part.astype(jnp.bfloat16), "seq", scatter_dimension=0, tiled=True
    ).astype(jnp.float32)
    layer_output = (middle + (result_sum + reduce_shift)).astype(jnp.bfloat16)
    upstream = cotangent.astype(jnp.float32)
    reduce_grad = jnp.einsum(
        "tf,td->fd", activated_low, cot_group, preferred_element_type=jnp.float32
    )
    reduce_shift_grad = jnp.sum(upstream, 0)
    activated_grad = jnp.einsum(
        "td,fd->tf", cot_group, reduce_local, preferred_element_type=jnp.float32
    )
    hidden_grad = gelu_pull(activated_grad)[0].astype(jnp.bfloat16)
    expand_grad = jnp.einsum(
        "tc,tf->cf", normed_two_group, hidden_grad, preferred_element_type=jnp.float32
    )
    expand_shift_grad = jnp.sum(hidden_grad.astype(jnp.float32), 0).reshape(
        expand_shift.shape[0], -1
    )
    normed_two_part = jnp.einsum(
        "tf,cf->tc", hidden_grad, expand_local, preferred_element_type=jnp.float32
    )
    normed_two_grad = lax.psum_scatter(
        normed_two_part.astype(jnp.bfloat16), "seq", scatter_dimension=0, tiled=True
    ).astype(jnp.float32)
    unused_value, norm_two_pull = jax.vjp(layer_norm, middle, gain_two, shift_two)
    middle_norm_grad, gain_two_grad, shift_two_grad = norm_two_pull(normed_two_grad)
    middle_grad = upstream + middle_norm_grad
    branch_grad = middle_grad.astype(jnp.bfloat16)
    out_shift_grad = jnp.sum(branch_grad.astype(jnp.float32), 0)
    branch_group = lax.all_gather(branch_grad, "seq", axis=0, tiled=True)
    out_grad = jnp.einsum(
        "tc,td->cd", attended_low, branch_group, preferred_element_type=jnp.float32
    )
    attended_grad = jnp.einsum(
        "td,cd->tc", branch_group, out_local, preferred_element_type=jnp.float32
    ).astype(jnp.bfloat16)
    grad_heads = attended_grad.reshape(row_count, head_local, HD)
    deltas = jnp.sum(grad_heads.astype(jnp.float32) * attended, -1)
    query_grads, key_grads = attend_backward(
        queries, all_keys, all_values, places, slopes, grad_heads, log_sums, deltas
    )
    key_terms = key_grads.reshape(seq_count, blk_count * tok_rows, head_local * 2 * HD)
    key_sums = lax.psum_scatter(
        key_terms.astype(jnp.bfloat16), "blk", scatter_dimension=1, tiled=True
    ).astype(jnp.float32)
    combined = jnp.concatenate(
        [
            query_grads.astype(jnp.bfloat16),
            key_sums.reshape(row_count, head_local, 2 * HD).astype(jnp.bfloat16),
        ],
        -1,
    )
    mixed_grad = combined.reshape(row_count, head_local * 3 * HD)
    joint_grad = jnp.einsum("tc,tk->ck", arrived, mixed_grad, preferred_element_type=jnp.float32)
    bias_sums = jnp.sum(mixed_grad.astype(jnp.float32), 0).reshape(head_local, 3, HD)
    pair_grad = jnp.concatenate([bias_sums[:, 0], bias_sums[:, 2]], -1)
    normed_one_part = jnp.einsum(
        "tk,ck->tc", mixed_grad, joint_local, preferred_element_type=jnp.float32
    )
    normed_one_grad = lax.psum_scatter(
        normed_one_part.astype(jnp.bfloat16), "seq", scatter_dimension=0, tiled=True
    ).astype(jnp.float32)
    unused_first, norm_one_pull = jax.vjp(layer_norm, inputs, gain_one, shift_one)
    input_norm_grad, gain_one_grad, shift_one_grad = norm_one_pull(normed_one_grad)
    input_grad = (middle_grad + input_norm_grad).astype(jnp.bfloat16)
    weight_sums = (
        lax.psum_scatter(
            joint_grad.astype(jnp.bfloat16), ("dp", "blk"), scatter_dimension=0, tiled=True
        ).astype(jnp.float32),
        lax.psum_scatter(
            pair_grad.astype(jnp.bfloat16), ("dp", "blk"), scatter_dimension=1, tiled=True
        ).astype(jnp.float32),
        lax.psum_scatter(
            out_grad.astype(jnp.bfloat16), ("dp", "blk"), scatter_dimension=1, tiled=True
        ).astype(jnp.float32),
        lax.psum_scatter(
            expand_grad.astype(jnp.bfloat16), ("dp", "blk"), scatter_dimension=0, tiled=True
        ).astype(jnp.float32),
        lax.psum_scatter(
            expand_shift_grad.astype(jnp.bfloat16), ("dp", "blk"), scatter_dimension=1, tiled=True
        ).astype(jnp.float32),
        lax.psum_scatter(
            reduce_grad.astype(jnp.bfloat16), ("dp", "blk"), scatter_dimension=1, tiled=True
        ).astype(jnp.float32),
    )
    small_sums = (
        lax.psum_scatter(gain_one_grad, ("dp", "seq", "blk"), scatter_dimension=0, tiled=True),
        lax.psum_scatter(shift_one_grad, ("dp", "seq", "blk"), scatter_dimension=0, tiled=True),
        lax.psum_scatter(out_shift_grad, ("dp", "seq", "blk"), scatter_dimension=0, tiled=True),
        lax.psum_scatter(gain_two_grad, ("dp", "seq", "blk"), scatter_dimension=0, tiled=True),
        lax.psum_scatter(shift_two_grad, ("dp", "seq", "blk"), scatter_dimension=0, tiled=True),
        lax.psum_scatter(reduce_shift_grad, ("dp", "seq", "blk"), scatter_dimension=0, tiled=True),
    )
    return (
        layer_output,
        input_grad,
        small_sums[0],
        small_sums[1],
        weight_sums[0],
        weight_sums[1],
        weight_sums[2],
        small_sums[2],
        small_sums[3],
        small_sums[4],
        weight_sums[3],
        weight_sums[4],
        weight_sums[5],
        small_sums[5],
    )


ALL = ("dp", "seq", "blk")
PLANE = ("seq", "blk")


def swap(value, axes, count, offset):
    return lax.ppermute(value, axes, [(i, i ^ offset) for i in range(count)])


def low(value):
    return value.astype(jnp.bfloat16)


def wide(value):
    return value.astype(jnp.float32)


ANY = pl.BlockSpec(memory_space=pl.ANY)
VMEM = pl.BlockSpec(memory_space=pltpu.VMEM)
SMEM = pl.BlockSpec(memory_space=pltpu.SMEM)
STEP = 256
PAIR = 2 * HD
QKV = 3 * PAIR
COLUMNS = QKV + PAIR
SMALL = 16
LANES = 128


def struct(rows, columns, dtype):
    return jax.ShapeDtypeStruct((rows, columns), dtype)


def contract(left, right, left_dim, right_dim):
    return lax.dot_general(
        left, right, (((left_dim,), (right_dim,)), ((), ())), preferred_element_type=jnp.float32
    )


def call(kernel, outs, specs, operands, scratch=(), cost=1.0, room=24):
    return pl.pallas_call(
        kernel,
        out_shape=outs,
        in_specs=specs,
        out_specs=[VMEM] * len(outs),
        scratch_shapes=list(scratch),
        compiler_params=pltpu.CompilerParams(vmem_limit_bytes=room * 2**20),
        cost_estimate=pl.CostEstimate(flops=int(cost * 1.1e9), bytes_accessed=0, transcendentals=0),
    )(*operands)


def fetch(pairs, sems):
    copies = [
        pltpu.make_async_copy(source, target, sems.at[k])
        for k, (source, target) in enumerate(pairs)
    ]
    for copy in copies:
        copy.start()
    for copy in copies:
        copy.wait()


def row_starts(place, order, rows):
    return [pl.multiple_of((place ^ offset) * rows, rows) for offset in order]


def head_lanes(shape):
    return lax.broadcasted_iota(jnp.int32, shape, 1) // HD


def normalise(values):
    average = jnp.mean(values, -1, keepdims=True)
    centred = values - average
    variance = jnp.mean(centred * centred, -1, keepdims=True)
    scale = lax.rsqrt(variance + epsilon)
    return (centred * scale, scale)


def norm_back(grad, xhat, scale, gain_row):
    scaled = grad * gain_row
    mean_scaled = jnp.mean(scaled, -1, keepdims=True)
    mean_product = jnp.mean(scaled * xhat, -1, keepdims=True)
    return scale * (scaled - mean_scaled - xhat * mean_product)


def normalise_kernel(order, spots, *refs):
    pieces, (xhat_ref, held, sems) = refs[: len(order)], refs[len(order) :]
    rows = pieces[0].shape[0]
    starts = row_starts(spots[3], order, rows)
    fetch([(p, held.at[pl.ds(s, rows)]) for p, s in zip(pieces, starts)], sems)

    @pl.loop(0, held.shape[0] // STEP)
    def _(step):
        block = pl.ds(pl.multiple_of(step * STEP, STEP), STEP)
        xhat_ref[block] = normalise(wide(held[block]))[0]


def reorder_columns(spots, source_ref, out_ref, count):
    size = out_ref.shape[1] // count
    for p in range(count):
        start = pl.multiple_of((spots[0] ^ p) * size, size)
        out_ref[:, p * size : (p + 1) * size] = source_ref[:, pl.ds(start, size)]


def prepare_attention_kernel(dp_count, blk_count, spots, *refs):
    joint_ref, output_ref, tokens_ref = refs[:3]
    vectors, (pair_ref, expand_ref) = refs[3:9], refs[9:11]
    outs = refs[11:]
    blocks, (own_ref, small_ref, turned) = outs[:blk_count], outs[blk_count:]
    turned[...] = low(wide(joint_ref[...]).T)
    for b, block in enumerate(blocks):
        first = (spots[2] ^ b) * 2
        for head in range(2):
            for part in range(3):
                start = pl.multiple_of(((first + head) * 3 + part) * HD, HD)
                row = part * PAIR + head * HD
                block[row : row + HD] = turned[pl.ds(start, HD)]
        start = pl.multiple_of(first * HD, PAIR)
        block[QKV:] = output_ref[pl.ds(start, PAIR)]
    reorder_columns(spots, tokens_ref, own_ref, dp_count)
    small = jnp.zeros(small_ref.shape, jnp.float32)
    row = lax.broadcasted_iota(jnp.int32, small.shape, 0)
    for k, vector in enumerate(vectors):
        piece = wide(vector[...])
        line = jnp.concatenate([piece, jnp.zeros((1, LANES - piece.shape[1]), jnp.float32)], 1)
        small = jnp.where(row == k, line, small)
    pair = wide(pair_ref[...])
    pair = jnp.concatenate([pair, jnp.zeros((pair.shape[0], LANES - pair.shape[1]), jnp.float32)], 1)
    for k in range(pair.shape[0]):
        small = jnp.where(row == 6 + k, pair[k : k + 1], small)
    small = jnp.where(row == 6 + pair.shape[0], wide(expand_ref[...]), small)
    small_ref[...] = low(small)


def prepare_forward_kernel(dp_count, blk_count, spots, *refs):
    expand_ref, reduce_ref, cot_ref, _ = refs[:4]
    blocks, (own_ref, turned) = refs[4 : 4 + blk_count], refs[4 + blk_count :]
    turned[...] = low(wide(expand_ref[...]).T)
    units = turned.shape[0] // blk_count
    for b, block in enumerate(blocks):
        start = pl.multiple_of((spots[2] ^ b) * units, units)
        block[:units] = turned[pl.ds(start, units)]
        block[units:] = reduce_ref[pl.ds(start, units)]
    reorder_columns(spots, cot_ref, own_ref, dp_count)


def pack_kernel(blk_count, has_small, spots, *refs):
    blocks, out_ref = refs[:blk_count], refs[-1]
    rows = blocks[0].shape[0]
    for b, block in enumerate(blocks):
        start = pl.multiple_of((spots[2] ^ b) * LANES, LANES)
        out_ref[:rows, pl.ds(start, LANES)] = block[...]
    if has_small:
        small_ref = refs[blk_count]
        count = small_ref.shape[0] // SMALL
        deep = count // blk_count
        for m in range(count):
            start = pl.multiple_of((spots[3] ^ m) * SMALL, SMALL)
            row, lane = rows + m % deep * SMALL, m // deep * LANES
            out_ref[row : row + SMALL, lane : lane + LANES] = small_ref[pl.ds(start, SMALL)]


def unpack_kernel(dp_count, plane_count, blk_count, pair_rows, spots, *refs):
    blocks = refs[:dp_count]
    vector_ref, joint_ref, expand_ref, held, small, sems = refs[dp_count:]
    dp, seq, blk = spots[0], spots[1], spots[2]
    deep = held.shape[1]
    fetch([(b.at[pl.ds(COLUMNS, deep)], held.at[d]) for d, b in enumerate(blocks)], sems)
    for d in range(dp_count):
        for b in range(blk_count):
            start = (d * blk_count + b) * deep
            small[start : start + deep] = wide(held[d, :, b * LANES : (b + 1) * LANES])
    piece = vector_ref.shape[1] // (dp_count * plane_count)
    group = LANES // piece
    for first in range(0, dp_count * plane_count, group):
        parts = [
            small[(first + k) * SMALL : (first + k) * SMALL + 8, :piece] for k in range(group)
        ]
        vector_ref[:, first * piece : (first + group) * piece] = jnp.concatenate(parts, 1)

    def line(owner, row):
        start = ((dp ^ (owner // blk_count)) * plane_count + seq * blk_count + owner % blk_count)
        return small[pl.ds(start * SMALL + row, 1)]

    owners = dp_count * blk_count
    width = 2 * HD // owners
    pairs = [
        jnp.concatenate([line(o, 6 + blk * 2 + head)[:, :width] for o in range(owners)], 1)
        for head in range(2)
    ]
    joint = jnp.concatenate(
        [pairs[0][:, :HD], pairs[1][:, :HD], jnp.zeros((1, PAIR), jnp.float32)]
        + [pairs[0][:, HD:], pairs[1][:, HD:]],
        1,
    )
    joint_ref[...] = jnp.broadcast_to(joint, joint_ref.shape)
    mine = owners // blk_count
    hidden = jnp.concatenate([line(blk * mine + k, 6 + pair_rows) for k in range(mine)], 1)
    expand_ref[...] = jnp.broadcast_to(hidden, expand_ref.shape)


def score_block(queries, keys, slope, first):
    scores = contract(queries, keys, 1, 1)
    column = lax.broadcasted_iota(jnp.int32, scores.shape, 1)
    row = lax.broadcasted_iota(jnp.int32, scores.shape, 0) + first
    places = lax.broadcasted_iota(jnp.int32, (1, scores.shape[1]), 1) - (first + STEP - 1)
    return jnp.where(column <= row, scores + slope * wide(places), -1e30)


def split_rows(part_of, order, starts, rows, own_ref, away_ref):
    half = len(order) // 2
    for k, start in enumerate(starts):
        part = part_of(start)
        if k < half:
            own_ref[k * rows : (k + 1) * rows] = part
        else:
            away_ref[(k - half) * rows : (k - half + 1) * rows] = low(part)


def attend_kernel(order, dp_count, spots, slope_ref, *refs):
    blocks = refs[:dp_count]
    xhat_ref, vector_ref, bias_ref = refs[dp_count : dp_count + 3]
    mixed_ref, att_ref, lse_ref, weight_ref, own_ref, away_ref, sems = refs[dp_count + 3 :]
    cut = weight_ref.shape[1] // dp_count
    fetch(
        [
            (b.at[pl.ds(0, COLUMNS)], weight_ref.at[:, pl.ds(d * cut, cut)])
            for d, b in enumerate(blocks)
        ],
        sems,
    )
    count = xhat_ref.shape[0]

    @pl.loop(0, count // STEP)
    def _(step):
        block = pl.ds(pl.multiple_of(step * STEP, STEP), STEP)
        normed = low(xhat_ref[block] * vector_ref[:1] + vector_ref[1:2])
        mixed_ref[block] = low(contract(normed, weight_ref[:QKV], 1, 1) + bias_ref[:1])

    lanes = head_lanes((STEP, PAIR))
    for first in range(0, count, STEP):
        stop = first + STEP
        queries = mixed_ref[first:stop, :PAIR] * jnp.bfloat16(HD**-0.5)
        keys, values = mixed_ref[:stop, PAIR : 2 * PAIR], mixed_ref[:stop, 2 * PAIR :]
        attended = log_sums = None
        for head in range(2):
            chosen = jnp.where(lanes == head, queries, 0)
            scores = score_block(chosen, keys, slope_ref[head], first)
            top = jnp.max(scores, -1, keepdims=True)
            weights = jnp.exp(scores - top)
            total = jnp.sum(weights, -1, keepdims=True)
            result = contract(low(weights), values, 1, 0) / total
            log_sum = jnp.broadcast_to(top + jnp.log(total), result.shape)
            attended = result if head == 0 else jnp.where(lanes == 1, result, attended)
            log_sums = log_sum if head == 0 else jnp.where(lanes == 1, log_sum, log_sums)
        att_ref[first:stop] = attended
        lse_ref[first:stop] = log_sums
    rows = count // len(order)
    starts = row_starts(spots[3], order, rows)
    split_rows(
        lambda start: contract(low(att_ref[pl.ds(start, rows)]), weight_ref[QKV:], 1, 0),
        order, starts, rows, own_ref, away_ref,
    )


def attend_back_kernel(order, spots, slope_ref, *refs):
    pieces = refs[: len(order)]
    mixed_ref, att_ref, lse_ref, weight_ref, _ = refs[len(order) : len(order) + 5]
    grad_ref, own_ref, away_ref, held, pulled, key_sum, value_sum, sems = refs[len(order) + 5 :]
    rows = pieces[0].shape[0]
    starts = row_starts(spots[3], order, rows)
    fetch([(p, held.at[pl.ds(s, rows)]) for p, s in zip(pieces, starts)], sems)
    count = held.shape[0]

    @pl.loop(0, count // STEP)
    def _(step):
        block = pl.ds(pl.multiple_of(step * STEP, STEP), STEP)
        pulled[block] = low(contract(held[block], weight_ref[QKV:], 1, 1))

    key_sum[...] = jnp.zeros_like(key_sum)
    value_sum[...] = jnp.zeros_like(value_sum)
    lanes = head_lanes((STEP, PAIR))
    for first in range(0, count, STEP):
        stop = first + STEP
        queries = mixed_ref[first:stop, :PAIR] * jnp.bfloat16(HD**-0.5)
        keys, values = mixed_ref[:stop, PAIR : 2 * PAIR], mixed_ref[:stop, 2 * PAIR :]
        key_lanes = head_lanes(keys.shape)
        grads = pulled[first:stop]
        products = wide(grads) * att_ref[first:stop]
        query_grad = None
        for head in range(2):
            chosen = jnp.where(lanes == head, queries, 0)
            chosen_grads = jnp.where(lanes == head, grads, 0)
            delta = jnp.sum(jnp.where(lanes == head, products, 0.0), -1, keepdims=True)
            scores = score_block(chosen, keys, slope_ref[head], first)
            probs = jnp.exp(scores - lse_ref[first:stop, head * HD : head * HD + 1])
            prob_grad = contract(chosen_grads, values, 1, 1)
            score_grad = low(probs * (prob_grad - delta))
            term = contract(score_grad, jnp.where(key_lanes == head, keys, 0), 1, 0)
            query_grad = term if head == 0 else query_grad + term
            key_sum[:stop] += contract(score_grad, chosen, 0, 0)
            value_sum[:stop] += contract(low(probs), chosen_grads, 0, 0)
        grad_ref[first:stop, :PAIR] = low(query_grad * HD**-0.5)
    grad_ref[:, PAIR : 2 * PAIR] = low(key_sum[...])
    grad_ref[:, 2 * PAIR :] = low(value_sum[...])
    split_rows(
        lambda start: contract(grad_ref[pl.ds(start, rows)], weight_ref[:QKV], 1, 0),
        order, starts, rows, own_ref, away_ref,
    )


def pack_small(spots, dp_count, blk_count, vectors, pairs, hidden, small):
    dp, seq, blk = spots[0], spots[1], spots[2]
    small[...] = jnp.zeros_like(small)
    count = small.shape[0] // SMALL
    plane_count = count // dp_count
    width = vectors.shape[1]
    piece = width // count
    empty = jnp.zeros((8, LANES - piece), jnp.float32)
    for k in range(count):
        part = jnp.concatenate([vectors[:, k * piece : (k + 1) * piece], empty], 1)
        small[k * SMALL : k * SMALL + 8] = part
    owners = dp_count * blk_count
    size = 2 * HD // owners
    lane = lax.broadcasted_iota(jnp.int32, (1, LANES), 1)
    mine = owners // blk_count
    for owner in range(owners):
        spot = (dp ^ (owner // blk_count)) * plane_count + seq * blk_count + owner % blk_count
        for head in range(2):
            part = pairs[head]
            if owner:
                part = jnp.concatenate([part[:, owner * size :], part[:, : owner * size]], 1)
            row = spot * SMALL + 6 + blk * 2 + head
            small[pl.ds(row, 1)] = jnp.where(lane < size, part, 0.0)
        part = hidden[:, owner % mine * LANES : (owner % mine + 1) * LANES]
        row = spot * SMALL + 6 + 2 * blk_count
        small[pl.ds(row, 1)] = jnp.where(blk == owner // mine, part, 0.0)


def attend_weights_kernel(order, dp_count, blk_count, spots, *refs):
    pieces = refs[: len(order)]
    xhat_ref, grad_ref, att_ref, weight_ref, vector_ref = refs[len(order) : len(order) + 5]
    sums_ref, hidden_ref = refs[len(order) + 5 : len(order) + 7]
    outs = refs[len(order) + 7 :]
    parts, (held, small, sems) = outs[:dp_count], outs[dp_count:]
    rows = pieces[0].shape[0]
    starts = row_starts(spots[3], order, rows)
    fetch([(p, held.at[pl.ds(s, rows)]) for p, s in zip(pieces, starts)], sems)
    mixed_grad, attended = grad_ref[...], low(att_ref[...])
    sums = jnp.sum(wide(mixed_grad), 0, keepdims=True)
    column = jnp.broadcast_to(sums, (8, QKV)).T[:, :1]
    cut = weight_ref.shape[1] // dp_count
    lines = [[], []]
    for d, part in enumerate(parts):
        block = slice(d * cut, (d + 1) * cut)
        plain = contract(mixed_grad, low(xhat_ref[:, block]), 0, 0)
        joint_grad = vector_ref[:1, block] * plain + vector_ref[1:2, block] * column
        part[:QKV] = joint_grad.astype(part.dtype)
        part[QKV:COLUMNS] = contract(attended, held[:, block], 0, 0).astype(part.dtype)
        weights = wide(weight_ref[:QKV, block])
        for k, product in enumerate((weights * plain, weights * column)):
            lines[k].append(jnp.sum(product, 0, keepdims=True))
    lines = [jnp.concatenate(line, 1) for line in lines]
    vectors = jnp.concatenate(lines + [sums_ref[:4], jnp.zeros_like(sums_ref[:2])], 0)
    pairs = [
        jnp.concatenate([sums[:, h * HD : (h + 1) * HD], sums[:, 2 * PAIR + h * HD : 2 * PAIR + (h + 1) * HD]], 1)
        for h in range(2)
    ]
    pack_small(spots, dp_count, blk_count, vectors, pairs, hidden_ref[:1], small)
    plane_rows = small.shape[0] // dp_count
    deep = plane_rows // blk_count
    for d, part in enumerate(parts):
        for b in range(blk_count):
            start = d * plane_rows + b * deep
            part[COLUMNS:, b * LANES : (b + 1) * LANES] = small[start : start + deep].astype(part.dtype)


def split_kernel(count, blk_count, has_small, spots, total_ref, *refs):
    came, outs = refs[:count], refs[count:]
    total = outs[-1]
    total[...] = wide(summed(total_ref, came))
    rows = outs[0].shape[0]
    for b in range(blk_count):
        start = pl.multiple_of((spots[2] ^ b) * LANES, LANES)
        outs[b][...] = total[:rows, pl.ds(start, LANES)].astype(outs[b].dtype)
    if has_small:
        small_ref = outs[blk_count]
        devices = small_ref.shape[0] // SMALL
        deep = devices // blk_count
        for m in range(devices):
            start = pl.multiple_of((spots[3] ^ m) * SMALL, SMALL)
            row, lane = rows + m % deep * SMALL, m // deep * LANES
            small_ref[pl.ds(start, SMALL)] = total[row : row + SMALL, lane : lane + LANES]


def attend_final_kernel(blk_count, spots, *refs):
    blocks, (joint_ref, output_ref) = refs[:blk_count], refs[blk_count:]
    for b, block in enumerate(blocks):
        other = spots[2] ^ b
        values = wide(block[...])
        turned = values[:QKV].T
        ordered = jnp.concatenate(
            [turned[:, part * PAIR + h * HD : part * PAIR + (h + 1) * HD] for h in range(2) for part in range(3)],
            1,
        )
        joint_ref[:, pl.ds(pl.multiple_of(other * QKV, LANES), QKV)] = ordered
        output_ref[pl.ds(pl.multiple_of(other * PAIR, PAIR), PAIR)] = values[QKV:]


def forward_final_kernel(blk_count, spots, *refs):
    blocks, (expand_ref, reduce_ref) = refs[:blk_count], refs[blk_count:]
    units = reduce_ref.shape[0] // blk_count
    for b, block in enumerate(blocks):
        start = pl.multiple_of((spots[2] ^ b) * units, units)
        expand_ref[:, pl.ds(start, units)] = wide(block[:units]).T
        reduce_ref[pl.ds(start, units)] = wide(block[units:])


def forward_fetch(count, dp_count, spots, pieces, weights, left, right, held, sems):
    rows, cut = pieces[0].shape[0], weights.shape[2]
    fetch(
        [(p, left.at[pl.ds(k * rows, rows)]) for k, p in enumerate(pieces[:count])]
        + [(p, right.at[pl.ds(k * rows, rows)]) for k, p in enumerate(pieces[count:])]
        + [
            (weights.at[spots[0] ^ d], held.at[:, pl.ds(d * cut, cut)]) for d in range(dp_count)
        ],
        sems,
    )


def forward_kernel(count, dp_count, spots, *refs):
    pieces, weights = refs[: 2 * count], refs[2 * count]
    bias_ref, act_ref, grad_ref, own_ref, away_ref, sum_ref, left, right, held, sems = refs[2 * count + 1 :]
    forward_fetch(count, dp_count, spots, pieces, weights, left, right, held, sems)
    units = act_ref.shape[1]
    half = left.shape[0] // 2
    sum_ref[...] = jnp.zeros_like(sum_ref)
    root = (2.0 / jnp.pi) ** 0.5
    for first in range(0, left.shape[0], STEP):
        stop = first + STEP
        hidden = contract(left[first:stop], held[:units], 1, 1) + bias_ref[:1]
        square = hidden * hidden
        bend = jnp.tanh(root * hidden * (1.0 + 0.044715 * square))
        act_ref[first:stop] = low(0.5 * hidden * (1.0 + bend))
        slope = 0.5 * (1.0 + bend) + 0.5 * hidden * (1.0 - bend * bend) * root * (
            1.0 + 3 * 0.044715 * square
        )
        hidden_grad = low(contract(right[first:stop], held[units:], 1, 1) * slope)
        grad_ref[first:stop] = hidden_grad
        sum_ref[...] += jnp.sum(wide(hidden_grad), 0, keepdims=True)
        part = contract(hidden_grad, held[:units], 1, 0)
        if first < half:
            own_ref[first:stop] = part
        else:
            away_ref[first - half : stop - half] = low(part)


def forward_weights_kernel(count, dp_count, spots, *refs):
    pieces, weights = refs[: 2 * count], refs[2 * count]
    act_ref, grad_ref, _ = refs[2 * count + 1 : 2 * count + 4]
    part_ref, own_ref, away_ref, left, right, held, sems = refs[2 * count + 4 :]
    forward_fetch(count, dp_count, spots, pieces, weights, left, right, held, sems)
    units, cut = act_ref.shape[1], weights.shape[2]
    for d in range(dp_count):
        block = slice(d * cut, (d + 1) * cut)
        spot = spots[0] ^ d
        part_ref[spot, :units] = low(contract(grad_ref[...], left[:, block], 0, 0))
        part_ref[spot, units:] = low(contract(act_ref[...], right[:, block], 0, 0))
    half = left.shape[0] // 2
    for first in range(0, left.shape[0], STEP):
        stop = first + STEP
        result = contract(act_ref[first:stop], held[units:], 1, 0)
        if first < half:
            own_ref[first:stop] = result
        else:
            away_ref[first - half : stop - half] = low(result)


def add_kernel(own_ref, came_ref, after, total_ref, *pieces):
    rows = total_ref.shape[0]
    total_ref[...] = own_ref[:rows] + wide(came_ref[:rows])
    for k, piece in enumerate(pieces):
        block = slice((k + 1) * rows, (k + 2) * rows)
        piece[...] = low(own_ref[block] + wide(came_ref[block]))


def summed(total_ref, came):
    total = total_ref[...]
    for piece in came:
        total = total + wide(piece[...])
    return total


def middle_kernel(count, total_ref, *refs):
    came = refs[:count]
    tokens_ref, vector_ref, middle_ref, normed_ref = refs[count:]
    middle = wide(tokens_ref[...]) + (summed(total_ref, came) + vector_ref[2:3])
    middle_ref[...] = middle
    normed_ref[...] = low(normalise(middle)[0] * vector_ref[3:4] + vector_ref[4:5])


def middle_back_kernel(count, total_ref, *refs):
    came = refs[:count]
    middle_ref, cot_ref, vector_ref, grad_ref, branch_ref, sums_ref = refs[count:]
    grad = summed(total_ref, came)
    xhat, scale = normalise(middle_ref[...])
    upstream = wide(cot_ref[...])
    total = upstream + norm_back(grad, xhat, scale, vector_ref[3:4])
    grad_ref[...] = total
    branch = low(total)
    branch_ref[...] = branch
    sums_ref[...] = jnp.zeros_like(sums_ref)
    for k, values in enumerate((wide(branch), grad * xhat, grad, upstream)):
        sums_ref[k : k + 1] = jnp.sum(values, 0, keepdims=True)


def place_columns(spots, dp_count, values, out_ref):
    size = out_ref.shape[1] // dp_count
    for d in range(dp_count):
        start = pl.multiple_of((spots[0] ^ d) * size, size)
        out_ref[:, pl.ds(start, size)] = values[:, d * size : (d + 1) * size]


def output_kernel(count, dp_count, spots, total_ref, *refs):
    came = refs[:count]
    middle_ref, vector_ref, out_ref = refs[count:]
    result = middle_ref[...] + (summed(total_ref, came) + vector_ref[5:6])
    place_columns(spots, dp_count, low(result), out_ref)


def input_kernel(count, dp_count, spots, total_ref, *refs):
    came = refs[:count]
    grad_ref, tokens_ref, vector_ref, out_ref = refs[count:]
    xhat, scale = normalise(wide(tokens_ref[...]))
    result = grad_ref[...] + norm_back(summed(total_ref, came), xhat, scale, vector_ref[:1])
    place_columns(spots, dp_count, low(result), out_ref)


def local_heads(
    tokens,
    first_gain,
    first_shift,
    joint_weight,
    joint_bias,
    output_weight,
    output_bias,
    second_gain,
    second_shift,
    expand_weight,
    expand_bias,
    reduce_weight,
    reduce_bias,
    cotangent,
):
    dp_count, seq_count, blk_count = (lax.axis_size(axis) for axis in ALL)
    dp, seq, blk = (lax.axis_index(axis) for axis in ALL)
    plane_count = seq_count * blk_count
    place = seq * blk_count + blk
    spots = jnp.stack([dp, seq, blk, place]).astype(jnp.int32)
    tok_rows, width = tokens.shape
    units = expand_weight.shape[1] // blk_count
    cut = width // dp_count
    piece = first_gain.shape[0]
    core = blk_count
    chips = [p for p in range(plane_count) if not p & core]
    order = chips + [p ^ core for p in chips]
    chip_count = len(chips)
    row_count, half_rows = plane_count * tok_rows, chip_count * tok_rows
    f32, bf16 = jnp.float32, jnp.bfloat16
    halves_out = [struct(half_rows, width, f32), struct(half_rows, width, bf16)]
    own_out = [struct(tok_rows, width, f32)]
    low_out = [struct(tok_rows, width, bf16)]
    dma = lambda count: pltpu.SemaphoreType.DMA((count,))
    held = lambda columns: pltpu.VMEM((row_count, columns), bf16)
    kernel = functools.partial

    def gather_plane(block):
        mine = [block] + [swap(block, PLANE, plane_count, chip) for chip in chips[1:]]
        return mine + [swap(p, PLANE, plane_count, core) for p in mine]

    def scatter_plane(own, away, after=None):
        came = swap(away, PLANE, plane_count, core)
        after = own if after is None else after
        outs = own_out + low_out * (chip_count - 1)
        total, *pieces = call(add_kernel, outs, [VMEM, VMEM, ANY], [own, came, after])
        pieces = [swap(p, PLANE, plane_count, chip) for chip, p in zip(chips[1:], pieces)]
        return [total] + pieces

    def exchange_blk(blocks):
        return [swap(p, "blk", blk_count, b) if b else p for b, p in enumerate(blocks)]

    *blocks, tokens_own, small = call(
        kernel(prepare_attention_kernel, dp_count, blk_count),
        [struct(COLUMNS, LANES, bf16)] * blk_count + low_out + [struct(SMALL, LANES, bf16)],
        [SMEM] + [VMEM] * 11,
        [spots, joint_weight, output_weight, tokens]
        + [
            v.reshape(1, -1)
            for v in (first_gain, first_shift, output_bias, second_gain, second_shift, reduce_bias)
        ]
        + [joint_bias, expand_bias],
        [pltpu.VMEM((joint_weight.shape[1], LANES), bf16)],
        2,
    )
    bits = [1 << b for b in range(plane_count.bit_length() - 1)]
    blocks = exchange_blk(blocks)
    for bit in bits:
        small = jnp.concatenate([small, swap(small, PLANE, plane_count, bit)], 0)
    small_deep = plane_count * SMALL // blk_count
    block = call(
        kernel(pack_kernel, blk_count, True),
        [struct(COLUMNS + small_deep, cut, bf16)],
        [SMEM] + [VMEM] * (blk_count + 1),
        [spots] + blocks + [small],
    )[0]
    blocks = [block] + [swap(block, "dp", dp_count, d) for d in range(1, dp_count)]
    token_group = gather_plane(tokens_own)

    *forward_blocks, cotangent_own = call(
        kernel(prepare_forward_kernel, dp_count, blk_count),
        [struct(2 * units, LANES, bf16)] * blk_count + low_out,
        [SMEM] + [VMEM] * 3 + [ANY],
        [spots, expand_weight, reduce_weight, cotangent, block],
        [pltpu.VMEM((expand_weight.shape[1], LANES), bf16)],
        2,
    )
    forward_block = call(
        kernel(pack_kernel, blk_count, False),
        [struct(2 * units, cut, bf16)],
        [SMEM] + [VMEM] * blk_count,
        [spots] + exchange_blk(forward_blocks),
    )[0]
    forward_weights = lax.all_gather(forward_block, "dp", axis=0, tiled=False)
    cot_group = gather_plane(cotangent_own)

    xhat = call(
        kernel(normalise_kernel, order),
        [struct(row_count, width, f32)],
        [SMEM] + [ANY] * plane_count,
        [spots] + token_group,
        [held(width), dma(plane_count)],
        2,
    )[0]
    vectors, joint_row, expand_row = call(
        kernel(unpack_kernel, dp_count, plane_count, blk_count, joint_bias.shape[0]),
        [struct(8, width, f32), struct(8, QKV, f32), struct(8, units, f32)],
        [SMEM] + [ANY] * dp_count,
        [spots] + blocks,
        [
            pltpu.VMEM((dp_count, small_deep, cut), bf16),
            pltpu.VMEM((dp_count * plane_count * SMALL, LANES), f32),
            dma(dp_count),
        ],
    )
    head_ids = place * 2 + jnp.arange(2, dtype=jnp.int32)
    slopes = jnp.exp2(-8.0 * (head_ids + 1).astype(f32) / H)
    mixed, attended, log_sums, weights, own, away = call(
        kernel(attend_kernel, order, dp_count),
        [struct(row_count, QKV, bf16), struct(row_count, PAIR, f32)]
        + [struct(row_count, PAIR, f32), struct(COLUMNS, width, bf16)]
        + halves_out,
        [SMEM, SMEM] + [ANY] * dp_count + [VMEM] * 3,
        [spots, slopes] + blocks + [xhat, vectors, joint_row],
        [dma(dp_count)],
        10,
    )
    branch = scatter_plane(own, away)

    middle, normed_two = call(
        kernel(middle_kernel, chip_count - 1),
        own_out + low_out,
        [VMEM] * (chip_count + 2),
        branch + [tokens_own, vectors],
    )
    normed_group = gather_plane(normed_two)
    forward_operands = [spots] + normed_group + cot_group + [forward_weights]
    forward_specs = [SMEM] + [ANY] * (2 * plane_count + 1)
    forward_scratch = [held(width), held(width), pltpu.VMEM((2 * units, width), bf16)]
    forward_scratch.append(dma(2 * plane_count + dp_count))
    activated, hidden_grad, own, away, hidden_sums = call(
        kernel(forward_kernel, plane_count, dp_count),
        [struct(row_count, units, bf16)] * 2 + halves_out + [struct(8, units, f32)],
        forward_specs + [VMEM],
        forward_operands + [expand_row],
        forward_scratch,
        8,
    )
    normed_two_grad = scatter_plane(own, away)
    middle_grad, branch_grad, middle_sums = call(
        kernel(middle_back_kernel, chip_count - 1),
        own_out + low_out + [struct(8, width, f32)],
        [VMEM] * (chip_count + 3),
        normed_two_grad + [middle, cotangent_own, vectors],
    )
    forward_grad, own, away = call(
        kernel(forward_weights_kernel, plane_count, dp_count),
        [jax.ShapeDtypeStruct((dp_count, 2 * units, cut), bf16)] + halves_out,
        forward_specs + [VMEM, VMEM, ANY],
        forward_operands + [activated, hidden_grad, normed_two_grad[0]],
        forward_scratch,
        8,
    )
    forward_grad = lax.psum_scatter(forward_grad, "dp", scatter_dimension=0, tiled=False)
    forward_grad = call(
        kernel(split_kernel, 0, blk_count, False),
        [struct(2 * units, LANES, f32)] + [struct(2 * units, LANES, bf16)] * (blk_count - 1),
        [SMEM, VMEM],
        [spots, forward_grad],
        [pltpu.VMEM((2 * units, cut), f32)],
    )
    expand_grad, reduce_grad = call(
        kernel(forward_final_kernel, blk_count),
        [struct(LANES, blk_count * units, f32), struct(blk_count * units, LANES, f32)],
        [SMEM] + [VMEM] * blk_count,
        [spots] + exchange_blk(forward_grad),
    )

    branch_group = gather_plane(branch_grad)
    result = scatter_plane(own, away, branch_group[-1])
    layer_output = call(
        kernel(output_kernel, chip_count - 1, dp_count),
        low_out,
        [SMEM] + [VMEM] * (chip_count + 2),
        [spots] + result + [middle, vectors],
    )[0]
    mixed_grad, own, away = call(
        kernel(attend_back_kernel, order),
        [struct(row_count, QKV, bf16)] + halves_out,
        [SMEM, SMEM] + [ANY] * plane_count + [VMEM] * 4 + [ANY],
        [spots, slopes] + branch_group + [mixed, attended, log_sums, weights, result[0]],
        [held(width), held(PAIR)]
        + [pltpu.VMEM((row_count, PAIR), f32)] * 2
        + [dma(plane_count)],
        10,
    )
    block_out = lambda dtype: struct(COLUMNS + small_deep, cut, dtype)
    attention_grad = call(
        kernel(attend_weights_kernel, order, dp_count, blk_count),
        [block_out(f32)] + [block_out(bf16)] * (dp_count - 1),
        [SMEM] + [ANY] * plane_count + [VMEM] * 7,
        [spots]
        + branch_group
        + [xhat, mixed_grad, attended, weights, vectors, middle_sums, hidden_sums],
        [held(width), pltpu.VMEM((dp_count * plane_count * SMALL, LANES), f32), dma(plane_count)],
        8,
    )
    normed_one_grad = scatter_plane(own, away)
    input_grad = call(
        kernel(input_kernel, chip_count - 1, dp_count),
        low_out,
        [SMEM] + [VMEM] * (chip_count + 3),
        [spots] + normed_one_grad + [middle_grad, tokens_own, vectors],
    )[0]
    attention_grad = [attention_grad[0]] + [
        swap(attention_grad[d], "dp", dp_count, d) for d in range(1, dp_count)
    ]
    *attention_grad, small = call(
        kernel(split_kernel, dp_count - 1, blk_count, True),
        [struct(COLUMNS, LANES, f32)]
        + [struct(COLUMNS, LANES, bf16)] * (blk_count - 1)
        + [struct(plane_count * SMALL, LANES, f32)],
        [SMEM] + [VMEM] * dp_count,
        [spots] + attention_grad,
        [pltpu.VMEM((COLUMNS + small_deep, cut), f32)],
    )
    joint_grad, output_grad = call(
        kernel(attend_final_kernel, blk_count),
        [struct(LANES, blk_count * QKV, f32), struct(blk_count * PAIR, LANES, f32)],
        [SMEM] + [VMEM] * blk_count,
        [spots] + exchange_blk(attention_grad),
    )
    for bit in reversed(bits):
        small = small[: bit * SMALL] + swap(small[bit * SMALL :], PLANE, plane_count, bit)
    pair_rows, pair_columns = joint_bias.shape
    return (
        layer_output,
        input_grad,
        small[0, :piece],
        small[1, :piece],
        joint_grad,
        small[6 : 6 + pair_rows, :pair_columns],
        output_grad,
        small[2, :piece],
        small[3, :piece],
        small[4, :piece],
        expand_grad,
        small[6 + pair_rows : 7 + pair_rows],
        reduce_grad,
        small[5, :piece],
    )


def local_any(*arrays):
    dp_count, seq_count, blk_count = (lax.axis_size(axis) for axis in ALL)
    own_width = arrays[0].shape[1] // (dp_count * blk_count)
    if H == 2 * seq_count * blk_count and own_width == LANES and blk_count == 2:
        return local_heads(*arrays)
    return local(*arrays)


def solution(mesh):
    return jax.shard_map(
        local_heads if H == 2 * mesh.shape["seq"] * mesh.shape["blk"] else local,
        mesh=mesh,
        in_specs=(
            P(("dp", "seq", "blk"), None),
            P(("dp", "seq", "blk")),
            P(("dp", "seq", "blk")),
            P(("dp", "blk"), "seq"),
            P("seq", ("dp", "blk")),
            P("seq", ("dp", "blk")),
            P(("dp", "seq", "blk")),
            P(("dp", "seq", "blk")),
            P(("dp", "seq", "blk")),
            P(("dp", "blk"), "seq"),
            P("seq", ("dp", "blk")),
            P("seq", ("dp", "blk")),
            P(("dp", "seq", "blk")),
            P(("dp", "seq", "blk"), None),
        ),
        out_specs=(
            P(("dp", "seq", "blk"), None),
            P(("dp", "seq", "blk"), None),
            P(("dp", "seq", "blk")),
            P(("dp", "seq", "blk")),
            P(("dp", "blk"), "seq"),
            P("seq", ("dp", "blk")),
            P("seq", ("dp", "blk")),
            P(("dp", "seq", "blk")),
            P(("dp", "seq", "blk")),
            P(("dp", "seq", "blk")),
            P(("dp", "blk"), "seq"),
            P("seq", ("dp", "blk")),
            P("seq", ("dp", "blk")),
            P(("dp", "seq", "blk")),
        ),
        check_vma=False,
    )
```

```python
import functools

import jax
import jax.numpy as jnp
from jax import lax
from jax.experimental import pallas as pl
from jax.experimental.pallas import tpu as pltpu
from jax.sharding import PartitionSpec as P

H = 16
HD = 64


epsilon = 1e-05


def layer_norm(values, gain_row, shift_row):
    average = jnp.mean(values, -1, keepdims=True)
    centred = values - average
    variance = jnp.mean(centred * centred, -1, keepdims=True)
    return centred * lax.rsqrt(variance + epsilon) * gain_row + shift_row


def local_bias(pair_local, head_local):
    paired = pair_local.reshape(head_local, 2, HD)
    return jnp.stack([paired[:, 0], jnp.zeros_like(paired[:, 0]), paired[:, 1]], axis=1).reshape(
        head_local * 3 * HD
    )


def gelu_tanh(values):
    return jax.nn.gelu(values, approximate=True)


def score_tile(query_block, key_tile, places, tile_start, slopes, scale_factor):
    tile_rows = key_tile.shape[0]
    key_places = tile_start + jnp.arange(tile_rows, dtype=jnp.int32)
    scores = (
        jnp.einsum("qhd,khd->hqk", query_block, key_tile, preferred_element_type=jnp.float32)
        * scale_factor
    )
    offsets = (key_places[None, :] - places[:, None]).astype(jnp.float32)
    scores = scores + slopes[:, None, None] * offsets[None]
    allowed = (key_places[None, :] <= places[:, None])[None]
    return (jnp.where(allowed, scores, -1e30), allowed)


def attend_forward(queries, all_keys, all_values, places, slopes):
    row_count, head_local, head_width = queries.shape
    block_rows = min(512, row_count)
    tile_rows = min(512, all_keys.shape[0])
    scale_factor = head_width ** (-0.5)
    query_blocks = queries.reshape(row_count // block_rows, block_rows, head_local, head_width)
    place_blocks = places.reshape(row_count // block_rows, block_rows)

    def one_block(block_pair):
        query_block, block_places = block_pair
        needed = (block_places[-1] + tile_rows) // tile_rows

        def one_tile(counter, state_carry):
            running_max, running_sum, running_total = state_carry
            tile_start = counter * tile_rows
            key_tile = lax.dynamic_slice_in_dim(all_keys, tile_start, tile_rows, 0)
            value_tile = lax.dynamic_slice_in_dim(all_values, tile_start, tile_rows, 0)
            scores, allowed = score_tile(
                query_block, key_tile, block_places, tile_start, slopes, scale_factor
            )
            new_max = jnp.maximum(running_max, jnp.max(scores, -1))
            weights_tile = jnp.where(allowed, jnp.exp(scores - new_max[..., None]), 0.0)
            factor = jnp.exp(running_max - new_max)
            running_sum = running_sum * factor + jnp.sum(weights_tile, -1)
            running_total = running_total * factor[..., None] + jnp.einsum(
                "hqk,khd->hqd",
                weights_tile.astype(jnp.bfloat16),
                value_tile,
                preferred_element_type=jnp.float32,
            )
            return (new_max, running_sum, running_total)

        start_state = (
            jnp.full((head_local, block_rows), -1e30, jnp.float32),
            jnp.zeros((head_local, block_rows), jnp.float32),
            jnp.zeros((head_local, block_rows, head_width), jnp.float32),
        )
        running_max, running_sum, running_total = lax.fori_loop(0, needed, one_tile, start_state)
        return (running_total / running_sum[..., None], running_max + jnp.log(running_sum))

    outputs, log_sums = lax.map(one_block, (query_blocks, place_blocks))
    outputs = jnp.transpose(outputs, (0, 2, 1, 3)).reshape(row_count, head_local, head_width)
    return (outputs, log_sums)


def attend_backward(queries, all_keys, all_values, places, slopes, grad_out, log_sums, deltas):
    row_count, head_local, head_width = queries.shape
    key_count = all_keys.shape[0]
    block_rows = min(512, row_count)
    tile_rows = min(512, key_count)
    scale_factor = head_width ** (-0.5)
    block_count = row_count // block_rows
    query_blocks = queries.reshape(block_count, block_rows, head_local, head_width)
    grad_blocks = grad_out.reshape(block_count, block_rows, head_local, head_width)
    place_blocks = places.reshape(block_count, block_rows)
    delta_blocks = jnp.transpose(deltas.reshape(block_count, block_rows, head_local), (0, 2, 1))

    def one_block(key_grads, block_inputs):
        query_block, grad_block, block_places, block_lse, block_delta = block_inputs
        needed = (block_places[-1] + tile_rows) // tile_rows

        def one_tile(counter, inner_carry):
            query_grad, key_sums = inner_carry
            tile_start = counter * tile_rows
            key_tile = lax.dynamic_slice_in_dim(all_keys, tile_start, tile_rows, 0)
            value_tile = lax.dynamic_slice_in_dim(all_values, tile_start, tile_rows, 0)
            scores, allowed = score_tile(
                query_block, key_tile, block_places, tile_start, slopes, scale_factor
            )
            probs = jnp.where(allowed, jnp.exp(scores - block_lse[..., None]), 0.0)
            value_grad = jnp.einsum(
                "hqk,qhd->khd",
                probs.astype(jnp.bfloat16),
                grad_block,
                preferred_element_type=jnp.float32,
            )
            prob_grad = jnp.einsum(
                "qhd,khd->hqk", grad_block, value_tile, preferred_element_type=jnp.float32
            )
            score_grad = (probs * (prob_grad - block_delta[..., None])).astype(jnp.bfloat16)
            query_grad = (
                query_grad
                + jnp.einsum(
                    "hqk,khd->qhd", score_grad, key_tile, preferred_element_type=jnp.float32
                )
                * scale_factor
            )
            key_grad = (
                jnp.einsum(
                    "hqk,qhd->khd", score_grad, query_block, preferred_element_type=jnp.float32
                )
                * scale_factor
            )
            current = lax.dynamic_slice_in_dim(key_sums, tile_start, tile_rows, 0)
            update = current + jnp.concatenate([key_grad, value_grad], -1)
            key_sums = lax.dynamic_update_slice_in_dim(key_sums, update, tile_start, 0)
            return (query_grad, key_sums)

        start_grad = jnp.zeros((block_rows, head_local, head_width), jnp.float32)
        query_grad, key_grads = lax.fori_loop(0, needed, one_tile, (start_grad, key_grads))
        return (key_grads, query_grad)

    start_keys = jnp.zeros((key_count, head_local, 2 * head_width), jnp.float32)
    key_grads, query_grads = lax.scan(
        one_block, start_keys, (query_blocks, grad_blocks, place_blocks, log_sums, delta_blocks)
    )
    return (query_grads.reshape(row_count, head_local, head_width), key_grads)


def local(
    tokens,
    first_gain,
    first_shift,
    joint_weight,
    joint_bias,
    output_weight,
    output_bias,
    second_gain,
    second_shift,
    expand_weight,
    expand_bias,
    reduce_weight,
    reduce_bias,
    cotangent,
):
    seq_count = lax.axis_size("seq")
    blk_count = lax.axis_size("blk")
    head_local = H // seq_count
    tok_rows = tokens.shape[0]
    inputs = tokens.astype(jnp.float32)
    small_full = (
        lax.all_gather(first_gain, ("dp", "seq", "blk"), axis=0, tiled=True),
        lax.all_gather(first_shift, ("dp", "seq", "blk"), axis=0, tiled=True),
        lax.all_gather(output_bias, ("dp", "seq", "blk"), axis=0, tiled=True),
        lax.all_gather(second_gain, ("dp", "seq", "blk"), axis=0, tiled=True),
        lax.all_gather(second_shift, ("dp", "seq", "blk"), axis=0, tiled=True),
        lax.all_gather(reduce_bias, ("dp", "seq", "blk"), axis=0, tiled=True),
    )
    gain_one, shift_one, out_shift, gain_two, shift_two, reduce_shift = [
        piece.astype(jnp.float32) for piece in small_full
    ]
    joint_local, pair_local, out_local = (
        lax.all_gather(joint_weight, ("dp", "blk"), axis=0, tiled=True),
        lax.all_gather(joint_bias, ("dp", "blk"), axis=1, tiled=True),
        lax.all_gather(output_weight, ("dp", "blk"), axis=1, tiled=True),
    )
    expand_local, expand_shift, reduce_local = (
        lax.all_gather(expand_weight, ("dp", "blk"), axis=0, tiled=True),
        lax.all_gather(expand_bias, ("dp", "blk"), axis=1, tiled=True),
        lax.all_gather(reduce_weight, ("dp", "blk"), axis=1, tiled=True),
    )
    outgoing = layer_norm(inputs, gain_one, shift_one).astype(jnp.bfloat16)
    arrived = lax.all_gather(outgoing, "seq", axis=0, tiled=True)
    row_count = arrived.shape[0]
    mixed_cols = jnp.dot(arrived, joint_local, preferred_element_type=jnp.float32)
    mixed_cols = mixed_cols + local_bias(pair_local.astype(jnp.float32), head_local)
    by_head = mixed_cols.astype(jnp.bfloat16).reshape(row_count, head_local, 3 * HD)
    queries = by_head[:, :, :HD]
    key_value = by_head[:, :, HD:].reshape(seq_count, tok_rows, head_local, 2 * HD)
    ordered = lax.all_gather(key_value, "blk", axis=1, tiled=True)
    ordered = ordered.reshape(seq_count * blk_count * tok_rows, head_local, 2 * HD)
    all_keys = ordered[:, :, :HD]
    all_values = ordered[:, :, HD:]
    places = (
        (jnp.arange(seq_count, dtype=jnp.int32)[:, None] * blk_count + lax.axis_index("blk"))
        * tok_rows
        + jnp.arange(tok_rows, dtype=jnp.int32)[None, :]
    ).reshape(row_count)
    head_ids = lax.axis_index("seq") * head_local + jnp.arange(head_local, dtype=jnp.int32)
    slopes = jnp.exp2(-8.0 * (head_ids + 1).astype(jnp.float32) / H)
    attended, log_sums = attend_forward(queries, all_keys, all_values, places, slopes)
    attended_low = attended.reshape(row_count, head_local * HD).astype(jnp.bfloat16)
    branch_part = jnp.dot(attended_low, out_local, preferred_element_type=jnp.float32)
    branch_sum = lax.psum_scatter(
        branch_part.astype(jnp.bfloat16), "seq", scatter_dimension=0, tiled=True
    ).astype(jnp.float32)
    middle = inputs + (branch_sum + out_shift)
    normed_two = layer_norm(middle, gain_two, shift_two).astype(jnp.bfloat16)
    normed_two_group, cot_group = (
        lax.all_gather(normed_two, "seq", axis=0, tiled=True),
        lax.all_gather(cotangent, "seq", axis=0, tiled=True),
    )
    hidden = jnp.dot(normed_two_group, expand_local, preferred_element_type=jnp.float32)
    hidden = hidden + expand_shift.astype(jnp.float32).reshape(-1)
    activated, gelu_pull = jax.vjp(gelu_tanh, hidden)
    activated_low = activated.astype(jnp.bfloat16)
    result_part = jnp.dot(activated_low, reduce_local, preferred_element_type=jnp.float32)
    result_sum = lax.psum_scatter(
        result_part.astype(jnp.bfloat16), "seq", scatter_dimension=0, tiled=True
    ).astype(jnp.float32)
    layer_output = (middle + (result_sum + reduce_shift)).astype(jnp.bfloat16)
    upstream = cotangent.astype(jnp.float32)
    reduce_grad = jnp.einsum(
        "tf,td->fd", activated_low, cot_group, preferred_element_type=jnp.float32
    )
    reduce_shift_grad = jnp.sum(upstream, 0)
    activated_grad = jnp.einsum(
        "td,fd->tf", cot_group, reduce_local, preferred_element_type=jnp.float32
    )
    hidden_grad = gelu_pull(activated_grad)[0].astype(jnp.bfloat16)
    expand_grad = jnp.einsum(
        "tc,tf->cf", normed_two_group, hidden_grad, preferred_element_type=jnp.float32
    )
    expand_shift_grad = jnp.sum(hidden_grad.astype(jnp.float32), 0).reshape(
        expand_shift.shape[0], -1
    )
    normed_two_part = jnp.einsum(
        "tf,cf->tc", hidden_grad, expand_local, preferred_element_type=jnp.float32
    )
    normed_two_grad = lax.psum_scatter(
        normed_two_part.astype(jnp.bfloat16), "seq", scatter_dimension=0, tiled=True
    ).astype(jnp.float32)
    unused_value, norm_two_pull = jax.vjp(layer_norm, middle, gain_two, shift_two)
    middle_norm_grad, gain_two_grad, shift_two_grad = norm_two_pull(normed_two_grad)
    middle_grad = upstream + middle_norm_grad
    branch_grad = middle_grad.astype(jnp.bfloat16)
    out_shift_grad = jnp.sum(branch_grad.astype(jnp.float32), 0)
    branch_group = lax.all_gather(branch_grad, "seq", axis=0, tiled=True)
    out_grad = jnp.einsum(
        "tc,td->cd", attended_low, branch_group, preferred_element_type=jnp.float32
    )
    attended_grad = jnp.einsum(
        "td,cd->tc", branch_group, out_local, preferred_element_type=jnp.float32
    ).astype(jnp.bfloat16)
    grad_heads = attended_grad.reshape(row_count, head_local, HD)
    deltas = jnp.sum(grad_heads.astype(jnp.float32) * attended, -1)
    query_grads, key_grads = attend_backward(
        queries, all_keys, all_values, places, slopes, grad_heads, log_sums, deltas
    )
    key_terms = key_grads.reshape(seq_count, blk_count * tok_rows, head_local * 2 * HD)
    key_sums = lax.psum_scatter(
        key_terms.astype(jnp.bfloat16), "blk", scatter_dimension=1, tiled=True
    ).astype(jnp.float32)
    combined = jnp.concatenate(
        [
            query_grads.astype(jnp.bfloat16),
            key_sums.reshape(row_count, head_local, 2 * HD).astype(jnp.bfloat16),
        ],
        -1,
    )
    mixed_grad = combined.reshape(row_count, head_local * 3 * HD)
    joint_grad = jnp.einsum("tc,tk->ck", arrived, mixed_grad, preferred_element_type=jnp.float32)
    bias_sums = jnp.sum(mixed_grad.astype(jnp.float32), 0).reshape(head_local, 3, HD)
    pair_grad = jnp.concatenate([bias_sums[:, 0], bias_sums[:, 2]], -1)
    normed_one_part = jnp.einsum(
        "tk,ck->tc", mixed_grad, joint_local, preferred_element_type=jnp.float32
    )
    normed_one_grad = lax.psum_scatter(
        normed_one_part.astype(jnp.bfloat16), "seq", scatter_dimension=0, tiled=True
    ).astype(jnp.float32)
    unused_first, norm_one_pull = jax.vjp(layer_norm, inputs, gain_one, shift_one)
    input_norm_grad, gain_one_grad, shift_one_grad = norm_one_pull(normed_one_grad)
    input_grad = (middle_grad + input_norm_grad).astype(jnp.bfloat16)
    weight_sums = (
        lax.psum_scatter(
            joint_grad.astype(jnp.bfloat16), ("dp", "blk"), scatter_dimension=0, tiled=True
        ).astype(jnp.float32),
        lax.psum_scatter(
            pair_grad.astype(jnp.bfloat16), ("dp", "blk"), scatter_dimension=1, tiled=True
        ).astype(jnp.float32),
        lax.psum_scatter(
            out_grad.astype(jnp.bfloat16), ("dp", "blk"), scatter_dimension=1, tiled=True
        ).astype(jnp.float32),
        lax.psum_scatter(
            expand_grad.astype(jnp.bfloat16), ("dp", "blk"), scatter_dimension=0, tiled=True
        ).astype(jnp.float32),
        lax.psum_scatter(
            expand_shift_grad.astype(jnp.bfloat16), ("dp", "blk"), scatter_dimension=1, tiled=True
        ).astype(jnp.float32),
        lax.psum_scatter(
            reduce_grad.astype(jnp.bfloat16), ("dp", "blk"), scatter_dimension=1, tiled=True
        ).astype(jnp.float32),
    )
    small_sums = (
        lax.psum_scatter(gain_one_grad, ("dp", "seq", "blk"), scatter_dimension=0, tiled=True),
        lax.psum_scatter(shift_one_grad, ("dp", "seq", "blk"), scatter_dimension=0, tiled=True),
        lax.psum_scatter(out_shift_grad, ("dp", "seq", "blk"), scatter_dimension=0, tiled=True),
        lax.psum_scatter(gain_two_grad, ("dp", "seq", "blk"), scatter_dimension=0, tiled=True),
        lax.psum_scatter(shift_two_grad, ("dp", "seq", "blk"), scatter_dimension=0, tiled=True),
        lax.psum_scatter(reduce_shift_grad, ("dp", "seq", "blk"), scatter_dimension=0, tiled=True),
    )
    return (
        layer_output,
        input_grad,
        small_sums[0],
        small_sums[1],
        weight_sums[0],
        weight_sums[1],
        weight_sums[2],
        small_sums[2],
        small_sums[3],
        small_sums[4],
        weight_sums[3],
        weight_sums[4],
        weight_sums[5],
        small_sums[5],
    )


ALL = ("dp", "seq", "blk")
PLANE = ("seq", "blk")


def swap(value, axes, count, offset):
    return lax.ppermute(value, axes, [(i, i ^ offset) for i in range(count)])


def low(value):
    return value.astype(jnp.bfloat16)


def wide(value):
    return value.astype(jnp.float32)


ANY = pl.BlockSpec(memory_space=pl.ANY)
HBM = pl.BlockSpec(memory_space=pltpu.HBM)
VMEM = pl.BlockSpec(memory_space=pltpu.VMEM)
SMEM = pl.BlockSpec(memory_space=pltpu.SMEM)
STEP = 256
PAIR = 2 * HD
QKV = 3 * PAIR
COLUMNS = QKV + PAIR
SMALL = 16
LANES = 128


def struct(rows, columns, dtype):
    return jax.ShapeDtypeStruct((rows, columns), dtype)


def contract(left, right, left_dim, right_dim):
    return lax.dot_general(
        left, right, (((left_dim,), (right_dim,)), ((), ())), preferred_element_type=jnp.float32
    )


def call(kernel, outs, specs, operands, scratch=(), cost=1.0, room=16):
    return pl.pallas_call(
        kernel,
        out_shape=outs,
        in_specs=specs,
        out_specs=[VMEM] * len(outs),
        scratch_shapes=list(scratch),
        compiler_params=pltpu.CompilerParams(vmem_limit_bytes=room * 2**20),
        cost_estimate=pl.CostEstimate(flops=int(cost * 1.0 * 1.1e9), bytes_accessed=0, transcendentals=0),
    )(*operands)


def fetch(pairs, sems):
    copies = [
        pltpu.make_async_copy(source, target, sems.at[k])
        for k, (source, target) in enumerate(pairs)
    ]
    for copy in copies:
        copy.start()
    for copy in copies:
        copy.wait()


def gathered(spots, pieces, order, target):
    half = len(order) // 2
    rows = target.shape[0] // len(order)
    pairs = []
    for k in range(len(order)):
        source = pl.multiple_of((spots[4] ^ (k % half)) * rows, rows)
        pairs.append((pieces[k // half].at[pl.ds(source, rows)], target.at[pl.ds(k * rows, rows)]))
    return pairs


def copies(out_ref, values):
    rows = values.shape[0]
    for k in range(out_ref.shape[0] // rows):
        out_ref[k * rows : (k + 1) * rows] = values


def row_starts(place, order, rows):
    return [pl.multiple_of((place ^ offset) * rows, rows) for offset in order]


def head_lanes(shape):
    return lax.broadcasted_iota(jnp.int32, shape, 1) // HD


def normalise(values):
    average = jnp.mean(values, -1, keepdims=True)
    centred = values - average
    variance = jnp.mean(centred * centred, -1, keepdims=True)
    scale = lax.rsqrt(variance + epsilon)
    return (centred * scale, scale)


def norm_back(grad, xhat, scale, gain_row):
    scaled = grad * gain_row
    mean_scaled = jnp.mean(scaled, -1, keepdims=True)
    mean_product = jnp.mean(scaled * xhat, -1, keepdims=True)
    return scale * (scaled - mean_scaled - xhat * mean_product)


def normalise_kernel(order, spots, *refs):
    pieces, (xhat_ref, held, sems) = refs[: len(order)], refs[len(order) :]
    rows = held.shape[0] // len(order)
    starts = row_starts(spots[3], order, rows)
    fetch([(p, held.at[pl.ds(s, rows)]) for p, s in zip(pieces, starts)], sems)

    @pl.loop(0, held.shape[0] // STEP)
    def _(step):
        block = pl.ds(pl.multiple_of(step * STEP, STEP), STEP)
        xhat_ref[block] = normalise(wide(held[block]))[0]


def reorder_columns(spots, source_ref, out_ref, count):
    size = out_ref.shape[1] // count
    for p in range(count):
        start = pl.multiple_of((spots[0] ^ p) * size, size)
        out_ref[:, p * size : (p + 1) * size] = source_ref[:, pl.ds(start, size)]


def prepare_attention_kernel(dp_count, blk_count, spots, *refs):
    count = 11
    sources, outs = refs[:count], refs[count:]
    blocks, (own_ref, small_ref) = outs[:blk_count], outs[blk_count : blk_count + 2]
    turned, *kept, sems = outs[blk_count + 2 :]
    fetch(list(zip(sources, kept)), sems)
    joint_ref, output_ref, tokens_ref = kept[:3]
    vectors, (pair_ref, shift_ref) = kept[3:9], kept[9:]
    turned[...] = low(wide(joint_ref[...]).T)
    for b, block in enumerate(blocks):
        first = (spots[2] ^ b) * 2
        for head in range(2):
            for part in range(3):
                start = pl.multiple_of(((first + head) * 3 + part) * HD, HD)
                row = part * PAIR + head * HD
                block[row : row + HD] = turned[pl.ds(start, HD)]
        start = pl.multiple_of(first * HD, PAIR)
        block[QKV:] = output_ref[pl.ds(start, PAIR)]
    reorder_columns(spots, tokens_ref, own_ref, dp_count)
    small = jnp.zeros(small_ref.shape, jnp.float32)
    row = lax.broadcasted_iota(jnp.int32, small.shape, 0)
    for k, vector in enumerate(vectors):
        piece = wide(vector[...])
        line = jnp.concatenate([piece, jnp.zeros((1, LANES - piece.shape[1]), jnp.float32)], 1)
        small = jnp.where(row == k, line, small)
    pair = wide(pair_ref[...])
    pair = jnp.concatenate([pair, jnp.zeros((pair.shape[0], LANES - pair.shape[1]), jnp.float32)], 1)
    for k in range(pair.shape[0]):
        small = jnp.where(row == 6 + k, pair[k : k + 1], small)
    small = jnp.where(row == 6 + pair.shape[0], wide(shift_ref[...]), small)
    small_ref[...] = low(small)


def cotangent_kernel(dp_count, spots, cot_ref, *refs):
    own_ref, rows = refs[-1], cot_ref.shape[0]
    for first in range(0, own_ref.shape[0], rows):
        reorder_columns(spots, cot_ref, own_ref.at[first : first + rows], dp_count)


def prepare_forward_kernel(blk_count, spots, *refs):
    expand_ref, reduce_ref = refs[:2]
    blocks, turned = refs[-blk_count - 1 : -1], refs[-1]
    turned[...] = low(wide(expand_ref[...]).T)
    units = turned.shape[0] // blk_count
    for b, block in enumerate(blocks):
        start = pl.multiple_of((spots[2] ^ b) * units, units)
        block[:units] = turned[pl.ds(start, units)]
        block[units:] = reduce_ref[pl.ds(start, units)]


def pack_kernel(blk_count, has_small, spots, *refs):
    blocks, out_ref = refs[:blk_count], refs[-1]
    rows = blocks[0].shape[0]
    for b, block in enumerate(blocks):
        start = pl.multiple_of((spots[2] ^ b) * LANES, LANES)
        out_ref[:rows, pl.ds(start, LANES)] = block[...]
    if has_small:
        small_ref = refs[blk_count]
        count = small_ref.shape[0] // SMALL
        deep = count // blk_count
        for m in range(count):
            start = pl.multiple_of((spots[3] ^ m) * SMALL, SMALL)
            row, lane = rows + m % deep * SMALL, m // deep * LANES
            out_ref[row : row + SMALL, lane : lane + LANES] = small_ref[pl.ds(start, SMALL)]


def unpack_kernel(dp_count, plane_count, blk_count, pair_rows, spots, *refs):
    blocks = refs[:dp_count]
    vector_ref, joint_ref, expand_ref, held, small, sems = refs[dp_count + 2 :]
    dp, seq, blk = spots[0], spots[1], spots[2]
    deep = held.shape[1]
    fetch([(b.at[pl.ds(COLUMNS, deep)], held.at[d]) for d, b in enumerate(blocks)], sems)
    for d in range(dp_count):
        for b in range(blk_count):
            start = (d * blk_count + b) * deep
            small[start : start + deep] = wide(held[d, :, b * LANES : (b + 1) * LANES])
    piece = vector_ref.shape[1] // (dp_count * plane_count)
    group = LANES // piece
    for first in range(0, dp_count * plane_count, group):
        parts = [
            small[(first + k) * SMALL : (first + k) * SMALL + 8, :piece] for k in range(group)
        ]
        vector_ref[:, first * piece : (first + group) * piece] = jnp.concatenate(parts, 1)

    def line(owner, row):
        start = ((dp ^ (owner // blk_count)) * plane_count + seq * blk_count + owner % blk_count)
        return small[pl.ds(start * SMALL + row, 1)]

    owners = dp_count * blk_count
    width = 2 * HD // owners
    pairs = [
        jnp.concatenate([line(o, 6 + blk * 2 + head)[:, :width] for o in range(owners)], 1)
        for head in range(2)
    ]
    joint = jnp.concatenate(
        [pairs[0][:, :HD], pairs[1][:, :HD], jnp.zeros((1, PAIR), jnp.float32)]
        + [pairs[0][:, HD:], pairs[1][:, HD:]],
        1,
    )
    joint_ref[...] = jnp.broadcast_to(joint, joint_ref.shape)
    mine = owners // blk_count
    hidden = jnp.concatenate([line(blk * mine + k, 6 + pair_rows) for k in range(mine)], 1)
    expand_ref[...] = jnp.broadcast_to(hidden, expand_ref.shape)


def score_block(queries, keys, slope, first):
    scores = contract(queries, keys, 1, 1)
    column = lax.broadcasted_iota(jnp.int32, scores.shape, 1)
    row = lax.broadcasted_iota(jnp.int32, scores.shape, 0) + first
    places = lax.broadcasted_iota(jnp.int32, (1, scores.shape[1]), 1) - (first + STEP - 1)
    return jnp.where(column <= row, scores + slope * wide(places), -1e30)


def split_rows(part_of, order, starts, rows, own_ref, away_ref):
    half = len(order) // 2
    for k, start in enumerate(starts):
        part = part_of(start)
        if k < half:
            own_ref[k * rows : (k + 1) * rows] = part
        else:
            away_ref[(k - half) * rows : (k - half + 1) * rows] = low(part)


def attend_kernel(order, dp_count, spots, slope_ref, *refs):
    blocks = refs[:dp_count]
    xhat_ref, vector_ref, bias_ref = refs[dp_count : dp_count + 3]
    mixed_ref, att_ref, lse_ref, weight_ref, own_ref, away_ref, sems = refs[dp_count + 5 :]
    cut = weight_ref.shape[1] // dp_count
    fetch(
        [
            (b.at[pl.ds(0, COLUMNS)], weight_ref.at[:, pl.ds(d * cut, cut)])
            for d, b in enumerate(blocks)
        ],
        sems,
    )
    count = xhat_ref.shape[0]

    @pl.loop(0, count // STEP)
    def _(step):
        block = pl.ds(pl.multiple_of(step * STEP, STEP), STEP)
        normed = low(xhat_ref[block] * vector_ref[:1] + vector_ref[1:2])
        mixed_ref[block] = low(contract(normed, weight_ref[:QKV], 1, 1) + bias_ref[:1])

    lanes = head_lanes((STEP, PAIR))
    for first in range(0, count, STEP):
        stop = first + STEP
        queries = mixed_ref[first:stop, :PAIR] * jnp.bfloat16(HD**-0.5)
        keys, values = mixed_ref[:stop, PAIR : 2 * PAIR], mixed_ref[:stop, 2 * PAIR :]
        attended = log_sums = None
        for head in range(2):
            chosen = jnp.where(lanes == head, queries, 0)
            scores = score_block(chosen, keys, slope_ref[head], first)
            top = jnp.max(scores, -1, keepdims=True)
            weights = jnp.exp(scores - top)
            total = jnp.sum(weights, -1, keepdims=True)
            result = contract(low(weights), values, 1, 0) / total
            log_sum = jnp.broadcast_to(top + jnp.log(total), result.shape)
            attended = result if head == 0 else jnp.where(lanes == 1, result, attended)
            log_sums = log_sum if head == 0 else jnp.where(lanes == 1, log_sum, log_sums)
        att_ref[first:stop] = attended
        lse_ref[first:stop] = log_sums
    rows = count // len(order)
    starts = row_starts(spots[3], order, rows)
    split_rows(
        lambda start: contract(low(att_ref[pl.ds(start, rows)]), weight_ref[QKV:], 1, 0),
        order, starts, rows, own_ref, away_ref,
    )


def attend_back_kernel(order, spots, slope_ref, *refs):
    pieces = refs[: len(order)]
    mixed_ref, att_ref, lse_ref, weight_ref, _ = refs[len(order) : len(order) + 5]
    grad_ref, own_ref, away_ref, held, pulled, key_sum, value_sum, sems = refs[len(order) + 5 :]
    rows = pieces[0].shape[0]
    starts = row_starts(spots[3], order, rows)
    fetch([(p, held.at[pl.ds(s, rows)]) for p, s in zip(pieces, starts)], sems)
    count = held.shape[0]

    @pl.loop(0, count // STEP)
    def _(step):
        block = pl.ds(pl.multiple_of(step * STEP, STEP), STEP)
        pulled[block] = low(contract(held[block], weight_ref[QKV:], 1, 1))

    key_sum[...] = jnp.zeros_like(key_sum)
    value_sum[...] = jnp.zeros_like(value_sum)
    lanes = head_lanes((STEP, PAIR))
    for first in range(0, count, STEP):
        stop = first + STEP
        queries = mixed_ref[first:stop, :PAIR] * jnp.bfloat16(HD**-0.5)
        keys, values = mixed_ref[:stop, PAIR : 2 * PAIR], mixed_ref[:stop, 2 * PAIR :]
        key_lanes = head_lanes(keys.shape)
        grads = pulled[first:stop]
        products = wide(grads) * att_ref[first:stop]
        query_grad = None
        for head in range(2):
            chosen = jnp.where(lanes == head, queries, 0)
            chosen_grads = jnp.where(lanes == head, grads, 0)
            delta = jnp.sum(jnp.where(lanes == head, products, 0.0), -1, keepdims=True)
            scores = score_block(chosen, keys, slope_ref[head], first)
            probs = jnp.exp(scores - lse_ref[first:stop, head * HD : head * HD + 1])
            prob_grad = contract(chosen_grads, values, 1, 1)
            score_grad = low(probs * (prob_grad - delta))
            term = contract(score_grad, jnp.where(key_lanes == head, keys, 0), 1, 0)
            query_grad = term if head == 0 else query_grad + term
            key_sum[:stop] += contract(score_grad, chosen, 0, 0)
            value_sum[:stop] += contract(low(probs), chosen_grads, 0, 0)
        grad_ref[first:stop, :PAIR] = low(query_grad * HD**-0.5)
    grad_ref[:, PAIR : 2 * PAIR] = low(key_sum[...])
    grad_ref[:, 2 * PAIR :] = low(value_sum[...])
    split_rows(
        lambda start: contract(grad_ref[pl.ds(start, rows)], weight_ref[:QKV], 1, 0),
        order, starts, rows, own_ref, away_ref,
    )


def pack_small(spots, dp_count, blk_count, vectors, pairs, hidden, small):
    dp, seq, blk = spots[0], spots[1], spots[2]
    small[...] = jnp.zeros_like(small)
    count = small.shape[0] // SMALL
    plane_count = count // dp_count
    width = vectors.shape[1]
    piece = width // count
    empty = jnp.zeros((8, LANES - piece), jnp.float32)
    for k in range(count):
        part = jnp.concatenate([vectors[:, k * piece : (k + 1) * piece], empty], 1)
        small[k * SMALL : k * SMALL + 8] = part
    owners = dp_count * blk_count
    size = 2 * HD // owners
    lane = lax.broadcasted_iota(jnp.int32, (1, LANES), 1)
    mine = owners // blk_count
    for owner in range(owners):
        spot = (dp ^ (owner // blk_count)) * plane_count + seq * blk_count + owner % blk_count
        for head in range(2):
            part = pairs[head]
            if owner:
                part = jnp.concatenate([part[:, owner * size :], part[:, : owner * size]], 1)
            row = spot * SMALL + 6 + blk * 2 + head
            small[pl.ds(row, 1)] = jnp.where(lane < size, part, 0.0)
        part = hidden[:, owner % mine * LANES : (owner % mine + 1) * LANES]
        row = spot * SMALL + 6 + 2 * blk_count
        small[pl.ds(row, 1)] = jnp.where(blk == owner // mine, part, 0.0)


def attend_weights_kernel(order, dp_count, blk_count, spots, *refs):
    pieces = refs[: len(order)]
    xhat_ref, grad_ref, att_ref, weight_ref, vector_ref = refs[len(order) : len(order) + 5]
    sums_ref, hidden_ref = refs[len(order) + 5 : len(order) + 7]
    outs = refs[len(order) + 7 :]
    parts, (held, small, sems) = outs[:dp_count], outs[dp_count:]
    rows = pieces[0].shape[0]
    starts = row_starts(spots[3], order, rows)
    fetch([(p, held.at[pl.ds(s, rows)]) for p, s in zip(pieces, starts)], sems)
    mixed_grad, attended = grad_ref[...], low(att_ref[...])
    sums = jnp.sum(wide(mixed_grad), 0, keepdims=True)
    column = jnp.broadcast_to(sums, (8, QKV)).T[:, :1]
    cut = weight_ref.shape[1] // dp_count
    lines = [[], []]
    for d, part in enumerate(parts):
        block = slice(d * cut, (d + 1) * cut)
        plain = contract(mixed_grad, low(xhat_ref[:, block]), 0, 0)
        joint_grad = vector_ref[:1, block] * plain + vector_ref[1:2, block] * column
        part[:QKV] = joint_grad.astype(part.dtype)
        part[QKV:COLUMNS] = contract(attended, held[:, block], 0, 0).astype(part.dtype)
        weights = wide(weight_ref[:QKV, block])
        for k, product in enumerate((weights * plain, weights * column)):
            lines[k].append(jnp.sum(product, 0, keepdims=True))
    lines = [jnp.concatenate(line, 1) for line in lines]
    vectors = jnp.concatenate(lines + [sums_ref[:4], jnp.zeros_like(sums_ref[:2])], 0)
    pairs = [
        jnp.concatenate([sums[:, h * HD : (h + 1) * HD], sums[:, 2 * PAIR + h * HD : 2 * PAIR + (h + 1) * HD]], 1)
        for h in range(2)
    ]
    pack_small(spots, dp_count, blk_count, vectors, pairs, hidden_ref[:1], small)
    plane_rows = small.shape[0] // dp_count
    deep = plane_rows // blk_count
    for d, part in enumerate(parts):
        for b in range(blk_count):
            start = d * plane_rows + b * deep
            part[COLUMNS:, b * LANES : (b + 1) * LANES] = small[start : start + deep].astype(part.dtype)


def split_kernel(count, blk_count, has_small, after, spots, *refs):
    parts, outs = refs[:count], refs[count + after :]
    total = outs[-1]
    total[...] = wide(summed(parts[0], parts[1:]))
    rows = outs[0].shape[0]
    for b in range(blk_count):
        start = pl.multiple_of((spots[2] ^ b) * LANES, LANES)
        outs[b][...] = total[:rows, pl.ds(start, LANES)].astype(outs[b].dtype)
    if has_small:
        small_ref = outs[blk_count]
        devices = small_ref.shape[0] // SMALL
        deep = devices // blk_count
        for m in range(devices):
            start = pl.multiple_of((spots[3] ^ m) * SMALL, SMALL)
            row, lane = rows + m % deep * SMALL, m // deep * LANES
            small_ref[pl.ds(start, SMALL)] = total[row : row + SMALL, lane : lane + LANES]


def attend_final_kernel(blk_count, spots, *refs):
    blocks, (joint_ref, output_ref) = refs[:blk_count], refs[blk_count:]
    for b, block in enumerate(blocks):
        other = spots[2] ^ b
        values = wide(block[...])
        turned = values[:QKV].T
        ordered = jnp.concatenate(
            [turned[:, part * PAIR + h * HD : part * PAIR + (h + 1) * HD] for h in range(2) for part in range(3)],
            1,
        )
        joint_ref[:, pl.ds(pl.multiple_of(other * QKV, LANES), QKV)] = ordered
        output_ref[pl.ds(pl.multiple_of(other * PAIR, PAIR), PAIR)] = values[QKV:]


def forward_final_kernel(blk_count, spots, *refs):
    blocks, (expand_ref, reduce_ref) = refs[:blk_count], refs[blk_count:]
    units = reduce_ref.shape[0] // blk_count
    for b, block in enumerate(blocks):
        start = pl.multiple_of((spots[2] ^ b) * units, units)
        expand_ref[:, pl.ds(start, units)] = wide(block[:units]).T
        reduce_ref[pl.ds(start, units)] = wide(block[units:])


def forward_fetch(order, dp_count, spots, pieces, weights, left, right, held, sems):
    cut = weights.shape[2]
    fetch(
        gathered(spots, pieces[:2], order, left)
        + gathered(spots, pieces[2:], order, right)
        + [
            (weights.at[spots[0] ^ d], held.at[:, pl.ds(d * cut, cut)]) for d in range(dp_count)
        ],
        sems,
    )


def forward_kernel(order, dp_count, spots, *refs):
    pieces, weights = refs[:4], refs[4]
    bias_ref, act_ref, grad_ref, own_ref, away_ref, sum_ref, left, right, held, sems = refs[5:]
    forward_fetch(order, dp_count, spots, pieces, weights, left, right, held, sems)
    units = act_ref.shape[1]
    half = left.shape[0] // 2
    sum_ref[...] = jnp.zeros_like(sum_ref)
    root = (2.0 / jnp.pi) ** 0.5
    for first in range(0, left.shape[0], STEP):
        stop = first + STEP
        hidden = contract(left[first:stop], held[:units], 1, 1) + bias_ref[:1]
        square = hidden * hidden
        bend = jnp.tanh(root * hidden * (1.0 + 0.044715 * square))
        act_ref[first:stop] = low(0.5 * hidden * (1.0 + bend))
        slope = 0.5 * (1.0 + bend) + 0.5 * hidden * (1.0 - bend * bend) * root * (
            1.0 + 3 * 0.044715 * square
        )
        hidden_grad = low(contract(right[first:stop], held[units:], 1, 1) * slope)
        grad_ref[first:stop] = hidden_grad
        sum_ref[...] += jnp.sum(wide(hidden_grad), 0, keepdims=True)
        part = contract(hidden_grad, held[:units], 1, 0)
        if first < half:
            own_ref[first:stop] = part
        else:
            away_ref[first - half : stop - half] = low(part)


def forward_weights_kernel(order, dp_count, spots, *refs):
    pieces, weights = refs[:4], refs[4]
    act_ref, grad_ref, _ = refs[5:8]
    part_ref, own_ref, away_ref, left, right, held, sems = refs[8:]
    forward_fetch(order, dp_count, spots, pieces, weights, left, right, held, sems)
    units, cut = act_ref.shape[1], weights.shape[2]
    for d in range(dp_count):
        block = slice(d * cut, (d + 1) * cut)
        spot = spots[0] ^ d
        part_ref[spot, :units] = low(contract(grad_ref[...], left[:, block], 0, 0))
        part_ref[spot, units:] = low(contract(act_ref[...], right[:, block], 0, 0))
    half = left.shape[0] // 2
    for first in range(0, left.shape[0], STEP):
        stop = first + STEP
        result = contract(act_ref[first:stop], held[units:], 1, 0)
        if first < half:
            own_ref[first:stop] = result
        else:
            away_ref[first - half : stop - half] = low(result)


def add_kernel(count, own_ref, came_ref, *refs):
    total_ref, *pieces = refs[count:]
    rows = total_ref.shape[0]
    total_ref[...] = own_ref[:rows] + wide(came_ref[:rows])
    for k, piece in enumerate(pieces):
        block = slice((k + 1) * rows, (k + 2) * rows)
        piece[...] = low(own_ref[block] + wide(came_ref[block]))


def summed(total_ref, came):
    total = total_ref[...]
    for piece in came:
        total = total + wide(piece[...])
    return total


def middle_kernel(count, total_ref, *refs):
    came = refs[:count]
    tokens_ref, vector_ref, middle_ref, normed_ref = refs[count:]
    middle = wide(tokens_ref[...]) + (summed(total_ref, came) + vector_ref[2:3])
    middle_ref[...] = middle
    copies(normed_ref, low(normalise(middle)[0] * vector_ref[3:4] + vector_ref[4:5]))


def middle_back_kernel(count, total_ref, *refs):
    came = refs[:count]
    middle_ref, cot_ref, vector_ref, grad_ref, branch_ref, sums_ref = refs[count:]
    grad = summed(total_ref, came)
    xhat, scale = normalise(middle_ref[...])
    upstream = wide(cot_ref[: grad_ref.shape[0]])
    total = upstream + norm_back(grad, xhat, scale, vector_ref[3:4])
    grad_ref[...] = total
    branch = low(total)
    branch_ref[...] = branch
    sums_ref[...] = jnp.zeros_like(sums_ref)
    for k, values in enumerate((wide(branch), grad * xhat, grad, upstream)):
        sums_ref[k : k + 1] = jnp.sum(values, 0, keepdims=True)


def place_columns(spots, dp_count, values, out_ref):
    size = out_ref.shape[1] // dp_count
    for d in range(dp_count):
        start = pl.multiple_of((spots[0] ^ d) * size, size)
        out_ref[:, pl.ds(start, size)] = values[:, d * size : (d + 1) * size]


def add_rows_kernel(count, spots, own_ref, came_ref, result_own, result_came, _, out_ref):
    rows, width = own_ref.shape[0] // count, own_ref.shape[1]
    for k in range(count):
        block = slice(k * rows, (k + 1) * rows)
        start = pl.multiple_of((spots[4] ^ k) * rows, rows)
        out_ref[pl.ds(start, rows), :width] = low(own_ref[block] + wide(came_ref[block]))
        out_ref[pl.ds(start, rows), width:] = low(result_own[block] + wide(result_came[block]))


def final_kernel(dp_count, spots, parts_ref, grad_ref, tokens_ref, middle_ref, vector_ref, input_ref, output_ref):
    width = grad_ref.shape[1]
    grad = jnp.sum(wide(parts_ref[:, :, :width]), 0)
    xhat, scale = normalise(wide(tokens_ref[...]))
    result = grad_ref[...] + norm_back(grad, xhat, scale, vector_ref[:1])
    place_columns(spots, dp_count, low(result), input_ref)
    result = jnp.sum(wide(parts_ref[:, :, width:]), 0)
    result = middle_ref[...] + (result + vector_ref[5:6])
    place_columns(spots, dp_count, low(result), output_ref)


def local_heads(
    tokens,
    first_gain,
    first_shift,
    joint_weight,
    joint_bias,
    output_weight,
    output_bias,
    second_gain,
    second_shift,
    expand_weight,
    expand_bias,
    reduce_weight,
    reduce_bias,
    cotangent,
):
    dp_count, seq_count, blk_count = (lax.axis_size(axis) for axis in ALL)
    dp, seq, blk = (lax.axis_index(axis) for axis in ALL)
    plane_count = seq_count * blk_count
    place = seq * blk_count + blk
    chip = seq // 2 * blk_count + blk
    spots = jnp.stack([dp, seq, blk, place, chip]).astype(jnp.int32)
    tok_rows, width = tokens.shape
    units = expand_weight.shape[1] // blk_count
    cut = width // dp_count
    piece = first_gain.shape[0]
    core = blk_count
    chips = [p for p in range(plane_count) if not p & core]
    order = chips + [p ^ core for p in chips]
    chip_count = len(chips)
    row_count, half_rows = plane_count * tok_rows, chip_count * tok_rows
    f32, bf16 = jnp.float32, jnp.bfloat16
    halves_out = [struct(half_rows, width, f32), struct(half_rows, width, bf16)]
    own_out = [struct(tok_rows, width, f32)]
    low_out = [struct(tok_rows, width, bf16)]
    copies_out = [struct(half_rows, width, bf16)]
    dma = lambda count: pltpu.SemaphoreType.DMA((count,))
    held = lambda columns: pltpu.VMEM((row_count, columns), bf16)
    kernel = functools.partial

    def gather_plane(block):
        mine = [block] + [swap(block, PLANE, plane_count, chip) for chip in chips[1:]]
        return mine + [swap(p, PLANE, plane_count, core) for p in mine]

    groups = [[p ^ side for p in chips] for side in (0, core)]

    def between_chips(blocks):
        blocks = blocks.reshape(chip_count, tok_rows, blocks.shape[1])
        return lax.all_to_all(blocks, PLANE, 0, 0, axis_index_groups=groups, tiled=True)

    def gather_copies(copies):
        mine = between_chips(copies).reshape(half_rows, width)
        return [mine, swap(mine, PLANE, plane_count, core)]

    def scatter_plane(own, away, after=()):
        came = swap(away, PLANE, plane_count, core)
        outs = own_out + low_out * (chip_count - 1)
        total, *pieces = call(
            kernel(add_kernel, len(after)),
            outs,
            [VMEM, VMEM] + [ANY] * len(after),
            [own, came] + list(after),
        )
        pieces = [swap(p, PLANE, plane_count, chip) for chip, p in zip(chips[1:], pieces)]
        return [total] + pieces

    def exchange_blk(blocks):
        return [swap(p, "blk", blk_count, b) if b else p for b, p in enumerate(blocks)]

    sources = [joint_weight, output_weight, tokens]
    sources += [
        v.reshape(1, -1)
        for v in (first_gain, first_shift, output_bias, second_gain, second_shift, reduce_bias)
    ]
    sources += [joint_bias, expand_bias]
    *blocks, tokens_own, small = call(
        kernel(prepare_attention_kernel, dp_count, blk_count),
        [struct(COLUMNS, LANES, bf16)] * blk_count + low_out + [struct(SMALL, LANES, bf16)],
        [SMEM] + [HBM] * len(sources),
        [spots] + sources,
        [pltpu.VMEM((joint_weight.shape[1], LANES), bf16)]
        + [pltpu.VMEM(v.shape, v.dtype) for v in sources]
        + [dma(len(sources))],
        room=60,
    )
    bits = [1 << b for b in range(plane_count.bit_length() - 1)]
    blocks = exchange_blk(blocks)
    for bit in bits:
        small = jnp.concatenate([small, swap(small, PLANE, plane_count, bit)], 0)
    small_deep = plane_count * SMALL // blk_count
    block = call(
        kernel(pack_kernel, blk_count, True),
        [struct(COLUMNS + small_deep, cut, bf16)],
        [SMEM] + [VMEM] * (blk_count + 1),
        [spots] + blocks + [small],
    )[0]
    blocks = [block] + [swap(block, "dp", dp_count, d) for d in range(1, dp_count)]
    token_group = gather_plane(tokens_own)

    cotangent_own = call(
        kernel(cotangent_kernel, dp_count),
        copies_out,
        [SMEM, VMEM] + [ANY] * 2,
        [spots, cotangent] + blocks[1:3],
    )[0]
    forward_blocks = call(
        kernel(prepare_forward_kernel, blk_count),
        [struct(2 * units, LANES, bf16)] * blk_count,
        [SMEM] + [VMEM] * 2 + [ANY],
        [spots, expand_weight, reduce_weight, blocks[1]],
        [pltpu.VMEM((expand_weight.shape[1], LANES), bf16)],
    )
    forward_block = call(
        kernel(pack_kernel, blk_count, False),
        [struct(2 * units, cut, bf16)],
        [SMEM] + [VMEM] * blk_count,
        [spots] + exchange_blk(forward_blocks),
    )[0]
    forward_weights = lax.all_gather(forward_block, "dp", axis=0, tiled=False)
    cot_group = gather_copies(cotangent_own)

    xhat = call(
        kernel(normalise_kernel, order),
        [struct(row_count, width, f32)],
        [SMEM] + [HBM] * plane_count,
        [spots] + token_group,
        [held(width), dma(plane_count)],
        2,
    )[0]
    vectors, joint_row, expand_row = call(
        kernel(unpack_kernel, dp_count, plane_count, blk_count, joint_bias.shape[0]),
        [struct(8, width, f32), struct(8, QKV, f32), struct(8, units, f32)],
        [SMEM] + [HBM] * dp_count + [ANY] * 2,
        [spots] + blocks + [xhat, tokens_own],
        [
            pltpu.VMEM((dp_count, small_deep, cut), bf16),
            pltpu.VMEM((dp_count * plane_count * SMALL, LANES), f32),
            dma(dp_count),
        ],
    )
    head_ids = place * 2 + jnp.arange(2, dtype=jnp.int32)
    slopes = jnp.exp2(-8.0 * (head_ids + 1).astype(f32) / H)
    mixed, attended, log_sums, weights, own, away = call(
        kernel(attend_kernel, order, dp_count),
        [struct(row_count, QKV, bf16), struct(row_count, PAIR, f32)]
        + [struct(row_count, PAIR, f32), struct(COLUMNS, width, bf16)]
        + halves_out,
        [SMEM, SMEM] + [HBM] * dp_count + [VMEM] * 3 + [ANY] * 2,
        [spots, slopes] + blocks + [xhat, vectors, joint_row, cot_group[0], forward_block],
        [dma(dp_count)],
        10,
        24,
    )
    branch = scatter_plane(own, away)

    middle, normed_two = call(
        kernel(middle_kernel, chip_count - 1),
        own_out + copies_out,
        [VMEM] * (chip_count + 2),
        branch + [tokens_own, vectors],
    )
    normed_group = gather_copies(normed_two)
    forward_operands = [spots] + normed_group + cot_group + [forward_weights]
    forward_specs = [SMEM] + [HBM] * 5
    forward_scratch = [held(width), held(width), pltpu.VMEM((2 * units, width), bf16)]
    forward_scratch.append(dma(2 * plane_count + dp_count))
    activated, hidden_grad, own, away, hidden_sums = call(
        kernel(forward_kernel, order, dp_count),
        [struct(row_count, units, bf16)] * 2 + halves_out + [struct(8, units, f32)],
        forward_specs + [VMEM],
        forward_operands + [expand_row],
        forward_scratch,
        8,
        24,
    )
    normed_two_grad = scatter_plane(own, away)
    middle_grad, branch_grad, middle_sums = call(
        kernel(middle_back_kernel, chip_count - 1),
        own_out + low_out + [struct(8, width, f32)],
        [VMEM] * (chip_count + 3),
        normed_two_grad + [middle, cotangent_own, vectors],
    )
    forward_grad, own, away = call(
        kernel(forward_weights_kernel, order, dp_count),
        [jax.ShapeDtypeStruct((dp_count, 2 * units, cut), bf16)] + halves_out,
        forward_specs + [VMEM, VMEM, ANY],
        forward_operands + [activated, hidden_grad, normed_two_grad[0]],
        forward_scratch,
        8,
        24,
    )
    forward_grad = lax.psum_scatter(forward_grad, "dp", scatter_dimension=0, tiled=False)
    forward_grad = call(
        kernel(split_kernel, 1, blk_count, False, 0),
        [struct(2 * units, LANES, f32)] + [struct(2 * units, LANES, bf16)] * (blk_count - 1),
        [SMEM, VMEM],
        [spots, forward_grad],
        [pltpu.VMEM((2 * units, cut), f32)],
    )
    forward_grad = exchange_blk(forward_grad)
    expand_grad, reduce_grad = call(
        kernel(forward_final_kernel, blk_count),
        [struct(LANES, blk_count * units, f32), struct(blk_count * units, LANES, f32)],
        [SMEM] + [VMEM] * blk_count,
        [spots] + forward_grad,
    )

    branch_group = gather_plane(branch_grad)
    result_own, result_came = own, swap(away, PLANE, plane_count, core)
    mixed_grad, own, away = call(
        kernel(attend_back_kernel, order),
        [struct(row_count, QKV, bf16)] + halves_out,
        [SMEM, SMEM] + [HBM] * plane_count + [VMEM] * 4 + [ANY],
        [spots, slopes] + branch_group + [mixed, attended, log_sums, weights, spots],
        [held(width), held(PAIR)]
        + [pltpu.VMEM((row_count, PAIR), f32)] * 2
        + [dma(plane_count)],
        10,
        24,
    )
    block_out = lambda dtype: struct(COLUMNS + small_deep, cut, dtype)
    attention_grad = call(
        kernel(attend_weights_kernel, order, dp_count, blk_count),
        [block_out(f32)] + [block_out(bf16)] * (dp_count - 1),
        [SMEM] + [HBM] * plane_count + [VMEM] * 7,
        [spots]
        + branch_group
        + [xhat, mixed_grad, attended, weights, vectors, middle_sums, hidden_sums],
        [held(width), pltpu.VMEM((dp_count * plane_count * SMALL, LANES), f32), dma(plane_count)],
        3,
        24,
    )
    pieces = call(
        kernel(add_rows_kernel, chip_count),
        [struct(half_rows, 2 * width, bf16)],
        [SMEM] + [VMEM] * 4 + [ANY],
        [spots, own, swap(away, PLANE, plane_count, core), result_own, result_came]
        + list(attention_grad[1:2]),
    )[0]
    pieces = between_chips(pieces)
    input_grad, layer_output = call(
        kernel(final_kernel, dp_count),
        low_out * 2,
        [SMEM] + [VMEM] * 5,
        [spots, pieces, middle_grad, tokens_own, middle, vectors],
    )
    attention_grad = [attention_grad[0]] + [
        swap(attention_grad[d], "dp", dp_count, d) for d in range(1, dp_count)
    ]
    *attention_grad, small = call(
        kernel(split_kernel, dp_count, blk_count, True, 2),
        [struct(COLUMNS, LANES, f32)]
        + [struct(COLUMNS, LANES, bf16)] * (blk_count - 1)
        + [struct(plane_count * SMALL, LANES, f32)],
        [SMEM] + [VMEM] * dp_count + [ANY] * 2,
        [spots] + attention_grad + [pieces, forward_grad[-1]],
        [pltpu.VMEM((COLUMNS + small_deep, cut), f32)],
    )
    joint_grad, output_grad = call(
        kernel(attend_final_kernel, blk_count),
        [struct(LANES, blk_count * QKV, f32), struct(blk_count * PAIR, LANES, f32)],
        [SMEM] + [VMEM] * blk_count,
        [spots] + exchange_blk(attention_grad),
    )
    for bit in reversed(bits):
        small = small[: bit * SMALL] + swap(small[bit * SMALL :], PLANE, plane_count, bit)
    pair_rows, pair_columns = joint_bias.shape
    return (
        layer_output,
        input_grad,
        small[0, :piece],
        small[1, :piece],
        joint_grad,
        small[6 : 6 + pair_rows, :pair_columns],
        output_grad,
        small[2, :piece],
        small[3, :piece],
        small[4, :piece],
        expand_grad,
        small[6 + pair_rows : 7 + pair_rows],
        reduce_grad,
        small[5, :piece],
    )


def local_any(*arrays):
    dp_count, seq_count, blk_count = (lax.axis_size(axis) for axis in ALL)
    own_width = arrays[0].shape[1] // (dp_count * blk_count)
    if H == 2 * seq_count * blk_count and own_width == LANES and blk_count == 2:
        return local_heads(*arrays)
    return local(*arrays)


def solution(mesh):
    return jax.shard_map(
        local_heads if H == 2 * mesh.shape["seq"] * mesh.shape["blk"] else local,
        mesh=mesh,
        in_specs=(
            P(("dp", "seq", "blk"), None),
            P(("dp", "seq", "blk")),
            P(("dp", "seq", "blk")),
            P(("dp", "blk"), "seq"),
            P("seq", ("dp", "blk")),
            P("seq", ("dp", "blk")),
            P(("dp", "seq", "blk")),
            P(("dp", "seq", "blk")),
            P(("dp", "seq", "blk")),
            P(("dp", "blk"), "seq"),
            P("seq", ("dp", "blk")),
            P("seq", ("dp", "blk")),
            P(("dp", "seq", "blk")),
            P(("dp", "seq", "blk"), None),
        ),
        out_specs=(
            P(("dp", "seq", "blk"), None),
            P(("dp", "seq", "blk"), None),
            P(("dp", "seq", "blk")),
            P(("dp", "seq", "blk")),
            P(("dp", "blk"), "seq"),
            P("seq", ("dp", "blk")),
            P("seq", ("dp", "blk")),
            P(("dp", "seq", "blk")),
            P(("dp", "seq", "blk")),
            P(("dp", "seq", "blk")),
            P(("dp", "blk"), "seq"),
            P("seq", ("dp", "blk")),
            P("seq", ("dp", "blk")),
            P(("dp", "seq", "blk")),
        ),
        check_vma=False,
    )
```

```python
import functools

import jax
import jax.numpy as jnp
from jax import lax
from jax.experimental import pallas as pl
from jax.experimental.pallas import tpu as pltpu
from jax.sharding import PartitionSpec as P

H = 16
HD = 64


epsilon = 1e-05


def layer_norm(values, gain_row, shift_row):
    average = jnp.mean(values, -1, keepdims=True)
    centred = values - average
    variance = jnp.mean(centred * centred, -1, keepdims=True)
    return centred * lax.rsqrt(variance + epsilon) * gain_row + shift_row


def local_bias(pair_local, head_local):
    paired = pair_local.reshape(head_local, 2, HD)
    return jnp.stack([paired[:, 0], jnp.zeros_like(paired[:, 0]), paired[:, 1]], axis=1).reshape(
        head_local * 3 * HD
    )


def gelu_tanh(values):
    return jax.nn.gelu(values, approximate=True)


def score_tile(query_block, key_tile, places, tile_start, slopes, scale_factor):
    tile_rows = key_tile.shape[0]
    key_places = tile_start + jnp.arange(tile_rows, dtype=jnp.int32)
    scores = (
        jnp.einsum("qhd,khd->hqk", query_block, key_tile, preferred_element_type=jnp.float32)
        * scale_factor
    )
    offsets = (key_places[None, :] - places[:, None]).astype(jnp.float32)
    scores = scores + slopes[:, None, None] * offsets[None]
    allowed = (key_places[None, :] <= places[:, None])[None]
    return (jnp.where(allowed, scores, -1e30), allowed)


def attend_forward(queries, all_keys, all_values, places, slopes):
    row_count, head_local, head_width = queries.shape
    block_rows = min(512, row_count)
    tile_rows = min(512, all_keys.shape[0])
    scale_factor = head_width ** (-0.5)
    query_blocks = queries.reshape(row_count // block_rows, block_rows, head_local, head_width)
    place_blocks = places.reshape(row_count // block_rows, block_rows)

    def one_block(block_pair):
        query_block, block_places = block_pair
        needed = (block_places[-1] + tile_rows) // tile_rows

        def one_tile(counter, state_carry):
            running_max, running_sum, running_total = state_carry
            tile_start = counter * tile_rows
            key_tile = lax.dynamic_slice_in_dim(all_keys, tile_start, tile_rows, 0)
            value_tile = lax.dynamic_slice_in_dim(all_values, tile_start, tile_rows, 0)
            scores, allowed = score_tile(
                query_block, key_tile, block_places, tile_start, slopes, scale_factor
            )
            new_max = jnp.maximum(running_max, jnp.max(scores, -1))
            weights_tile = jnp.where(allowed, jnp.exp(scores - new_max[..., None]), 0.0)
            factor = jnp.exp(running_max - new_max)
            running_sum = running_sum * factor + jnp.sum(weights_tile, -1)
            running_total = running_total * factor[..., None] + jnp.einsum(
                "hqk,khd->hqd",
                weights_tile.astype(jnp.bfloat16),
                value_tile,
                preferred_element_type=jnp.float32,
            )
            return (new_max, running_sum, running_total)

        start_state = (
            jnp.full((head_local, block_rows), -1e30, jnp.float32),
            jnp.zeros((head_local, block_rows), jnp.float32),
            jnp.zeros((head_local, block_rows, head_width), jnp.float32),
        )
        running_max, running_sum, running_total = lax.fori_loop(0, needed, one_tile, start_state)
        return (running_total / running_sum[..., None], running_max + jnp.log(running_sum))

    outputs, log_sums = lax.map(one_block, (query_blocks, place_blocks))
    outputs = jnp.transpose(outputs, (0, 2, 1, 3)).reshape(row_count, head_local, head_width)
    return (outputs, log_sums)


def attend_backward(queries, all_keys, all_values, places, slopes, grad_out, log_sums, deltas):
    row_count, head_local, head_width = queries.shape
    key_count = all_keys.shape[0]
    block_rows = min(512, row_count)
    tile_rows = min(512, key_count)
    scale_factor = head_width ** (-0.5)
    block_count = row_count // block_rows
    query_blocks = queries.reshape(block_count, block_rows, head_local, head_width)
    grad_blocks = grad_out.reshape(block_count, block_rows, head_local, head_width)
    place_blocks = places.reshape(block_count, block_rows)
    delta_blocks = jnp.transpose(deltas.reshape(block_count, block_rows, head_local), (0, 2, 1))

    def one_block(key_grads, block_inputs):
        query_block, grad_block, block_places, block_lse, block_delta = block_inputs
        needed = (block_places[-1] + tile_rows) // tile_rows

        def one_tile(counter, inner_carry):
            query_grad, key_sums = inner_carry
            tile_start = counter * tile_rows
            key_tile = lax.dynamic_slice_in_dim(all_keys, tile_start, tile_rows, 0)
            value_tile = lax.dynamic_slice_in_dim(all_values, tile_start, tile_rows, 0)
            scores, allowed = score_tile(
                query_block, key_tile, block_places, tile_start, slopes, scale_factor
            )
            probs = jnp.where(allowed, jnp.exp(scores - block_lse[..., None]), 0.0)
            value_grad = jnp.einsum(
                "hqk,qhd->khd",
                probs.astype(jnp.bfloat16),
                grad_block,
                preferred_element_type=jnp.float32,
            )
            prob_grad = jnp.einsum(
                "qhd,khd->hqk", grad_block, value_tile, preferred_element_type=jnp.float32
            )
            score_grad = (probs * (prob_grad - block_delta[..., None])).astype(jnp.bfloat16)
            query_grad = (
                query_grad
                + jnp.einsum(
                    "hqk,khd->qhd", score_grad, key_tile, preferred_element_type=jnp.float32
                )
                * scale_factor
            )
            key_grad = (
                jnp.einsum(
                    "hqk,qhd->khd", score_grad, query_block, preferred_element_type=jnp.float32
                )
                * scale_factor
            )
            current = lax.dynamic_slice_in_dim(key_sums, tile_start, tile_rows, 0)
            update = current + jnp.concatenate([key_grad, value_grad], -1)
            key_sums = lax.dynamic_update_slice_in_dim(key_sums, update, tile_start, 0)
            return (query_grad, key_sums)

        start_grad = jnp.zeros((block_rows, head_local, head_width), jnp.float32)
        query_grad, key_grads = lax.fori_loop(0, needed, one_tile, (start_grad, key_grads))
        return (key_grads, query_grad)

    start_keys = jnp.zeros((key_count, head_local, 2 * head_width), jnp.float32)
    key_grads, query_grads = lax.scan(
        one_block, start_keys, (query_blocks, grad_blocks, place_blocks, log_sums, delta_blocks)
    )
    return (query_grads.reshape(row_count, head_local, head_width), key_grads)


def local(
    tokens,
    first_gain,
    first_shift,
    joint_weight,
    joint_bias,
    output_weight,
    output_bias,
    second_gain,
    second_shift,
    expand_weight,
    expand_bias,
    reduce_weight,
    reduce_bias,
    cotangent,
):
    seq_count = lax.axis_size("seq")
    blk_count = lax.axis_size("blk")
    head_local = H // seq_count
    tok_rows = tokens.shape[0]
    inputs = tokens.astype(jnp.float32)
    small_full = (
        lax.all_gather(first_gain, ("dp", "seq", "blk"), axis=0, tiled=True),
        lax.all_gather(first_shift, ("dp", "seq", "blk"), axis=0, tiled=True),
        lax.all_gather(output_bias, ("dp", "seq", "blk"), axis=0, tiled=True),
        lax.all_gather(second_gain, ("dp", "seq", "blk"), axis=0, tiled=True),
        lax.all_gather(second_shift, ("dp", "seq", "blk"), axis=0, tiled=True),
        lax.all_gather(reduce_bias, ("dp", "seq", "blk"), axis=0, tiled=True),
    )
    gain_one, shift_one, out_shift, gain_two, shift_two, reduce_shift = [
        piece.astype(jnp.float32) for piece in small_full
    ]
    joint_local, pair_local, out_local = (
        lax.all_gather(joint_weight, ("dp", "blk"), axis=0, tiled=True),
        lax.all_gather(joint_bias, ("dp", "blk"), axis=1, tiled=True),
        lax.all_gather(output_weight, ("dp", "blk"), axis=1, tiled=True),
    )
    expand_local, expand_shift, reduce_local = (
        lax.all_gather(expand_weight, ("dp", "blk"), axis=0, tiled=True),
        lax.all_gather(expand_bias, ("dp", "blk"), axis=1, tiled=True),
        lax.all_gather(reduce_weight, ("dp", "blk"), axis=1, tiled=True),
    )
    outgoing = layer_norm(inputs, gain_one, shift_one).astype(jnp.bfloat16)
    arrived = lax.all_gather(outgoing, "seq", axis=0, tiled=True)
    row_count = arrived.shape[0]
    mixed_cols = jnp.dot(arrived, joint_local, preferred_element_type=jnp.float32)
    mixed_cols = mixed_cols + local_bias(pair_local.astype(jnp.float32), head_local)
    by_head = mixed_cols.astype(jnp.bfloat16).reshape(row_count, head_local, 3 * HD)
    queries = by_head[:, :, :HD]
    key_value = by_head[:, :, HD:].reshape(seq_count, tok_rows, head_local, 2 * HD)
    ordered = lax.all_gather(key_value, "blk", axis=1, tiled=True)
    ordered = ordered.reshape(seq_count * blk_count * tok_rows, head_local, 2 * HD)
    all_keys = ordered[:, :, :HD]
    all_values = ordered[:, :, HD:]
    places = (
        (jnp.arange(seq_count, dtype=jnp.int32)[:, None] * blk_count + lax.axis_index("blk"))
        * tok_rows
        + jnp.arange(tok_rows, dtype=jnp.int32)[None, :]
    ).reshape(row_count)
    head_ids = lax.axis_index("seq") * head_local + jnp.arange(head_local, dtype=jnp.int32)
    slopes = jnp.exp2(-8.0 * (head_ids + 1).astype(jnp.float32) / H)
    attended, log_sums = attend_forward(queries, all_keys, all_values, places, slopes)
    attended_low = attended.reshape(row_count, head_local * HD).astype(jnp.bfloat16)
    branch_part = jnp.dot(attended_low, out_local, preferred_element_type=jnp.float32)
    branch_sum = lax.psum_scatter(
        branch_part.astype(jnp.bfloat16), "seq", scatter_dimension=0, tiled=True
    ).astype(jnp.float32)
    middle = inputs + (branch_sum + out_shift)
    normed_two = layer_norm(middle, gain_two, shift_two).astype(jnp.bfloat16)
    normed_two_group, cot_group = (
        lax.all_gather(normed_two, "seq", axis=0, tiled=True),
        lax.all_gather(cotangent, "seq", axis=0, tiled=True),
    )
    hidden = jnp.dot(normed_two_group, expand_local, preferred_element_type=jnp.float32)
    hidden = hidden + expand_shift.astype(jnp.float32).reshape(-1)
    activated, gelu_pull = jax.vjp(gelu_tanh, hidden)
    activated_low = activated.astype(jnp.bfloat16)
    result_part = jnp.dot(activated_low, reduce_local, preferred_element_type=jnp.float32)
    result_sum = lax.psum_scatter(
        result_part.astype(jnp.bfloat16), "seq", scatter_dimension=0, tiled=True
    ).astype(jnp.float32)
    layer_output = (middle + (result_sum + reduce_shift)).astype(jnp.bfloat16)
    upstream = cotangent.astype(jnp.float32)
    reduce_grad = jnp.einsum(
        "tf,td->fd", activated_low, cot_group, preferred_element_type=jnp.float32
    )
    reduce_shift_grad = jnp.sum(upstream, 0)
    activated_grad = jnp.einsum(
        "td,fd->tf", cot_group, reduce_local, preferred_element_type=jnp.float32
    )
    hidden_grad = gelu_pull(activated_grad)[0].astype(jnp.bfloat16)
    expand_grad = jnp.einsum(
        "tc,tf->cf", normed_two_group, hidden_grad, preferred_element_type=jnp.float32
    )
    expand_shift_grad = jnp.sum(hidden_grad.astype(jnp.float32), 0).reshape(
        expand_shift.shape[0], -1
    )
    normed_two_part = jnp.einsum(
        "tf,cf->tc", hidden_grad, expand_local, preferred_element_type=jnp.float32
    )
    normed_two_grad = lax.psum_scatter(
        normed_two_part.astype(jnp.bfloat16), "seq", scatter_dimension=0, tiled=True
    ).astype(jnp.float32)
    unused_value, norm_two_pull = jax.vjp(layer_norm, middle, gain_two, shift_two)
    middle_norm_grad, gain_two_grad, shift_two_grad = norm_two_pull(normed_two_grad)
    middle_grad = upstream + middle_norm_grad
    branch_grad = middle_grad.astype(jnp.bfloat16)
    out_shift_grad = jnp.sum(branch_grad.astype(jnp.float32), 0)
    branch_group = lax.all_gather(branch_grad, "seq", axis=0, tiled=True)
    out_grad = jnp.einsum(
        "tc,td->cd", attended_low, branch_group, preferred_element_type=jnp.float32
    )
    attended_grad = jnp.einsum(
        "td,cd->tc", branch_group, out_local, preferred_element_type=jnp.float32
    ).astype(jnp.bfloat16)
    grad_heads = attended_grad.reshape(row_count, head_local, HD)
    deltas = jnp.sum(grad_heads.astype(jnp.float32) * attended, -1)
    query_grads, key_grads = attend_backward(
        queries, all_keys, all_values, places, slopes, grad_heads, log_sums, deltas
    )
    key_terms = key_grads.reshape(seq_count, blk_count * tok_rows, head_local * 2 * HD)
    key_sums = lax.psum_scatter(
        key_terms.astype(jnp.bfloat16), "blk", scatter_dimension=1, tiled=True
    ).astype(jnp.float32)
    combined = jnp.concatenate(
        [
            query_grads.astype(jnp.bfloat16),
            key_sums.reshape(row_count, head_local, 2 * HD).astype(jnp.bfloat16),
        ],
        -1,
    )
    mixed_grad = combined.reshape(row_count, head_local * 3 * HD)
    joint_grad = jnp.einsum("tc,tk->ck", arrived, mixed_grad, preferred_element_type=jnp.float32)
    bias_sums = jnp.sum(mixed_grad.astype(jnp.float32), 0).reshape(head_local, 3, HD)
    pair_grad = jnp.concatenate([bias_sums[:, 0], bias_sums[:, 2]], -1)
    normed_one_part = jnp.einsum(
        "tk,ck->tc", mixed_grad, joint_local, preferred_element_type=jnp.float32
    )
    normed_one_grad = lax.psum_scatter(
        normed_one_part.astype(jnp.bfloat16), "seq", scatter_dimension=0, tiled=True
    ).astype(jnp.float32)
    unused_first, norm_one_pull = jax.vjp(layer_norm, inputs, gain_one, shift_one)
    input_norm_grad, gain_one_grad, shift_one_grad = norm_one_pull(normed_one_grad)
    input_grad = (middle_grad + input_norm_grad).astype(jnp.bfloat16)
    weight_sums = (
        lax.psum_scatter(
            joint_grad.astype(jnp.bfloat16), ("dp", "blk"), scatter_dimension=0, tiled=True
        ).astype(jnp.float32),
        lax.psum_scatter(
            pair_grad.astype(jnp.bfloat16), ("dp", "blk"), scatter_dimension=1, tiled=True
        ).astype(jnp.float32),
        lax.psum_scatter(
            out_grad.astype(jnp.bfloat16), ("dp", "blk"), scatter_dimension=1, tiled=True
        ).astype(jnp.float32),
        lax.psum_scatter(
            expand_grad.astype(jnp.bfloat16), ("dp", "blk"), scatter_dimension=0, tiled=True
        ).astype(jnp.float32),
        lax.psum_scatter(
            expand_shift_grad.astype(jnp.bfloat16), ("dp", "blk"), scatter_dimension=1, tiled=True
        ).astype(jnp.float32),
        lax.psum_scatter(
            reduce_grad.astype(jnp.bfloat16), ("dp", "blk"), scatter_dimension=1, tiled=True
        ).astype(jnp.float32),
    )
    small_sums = (
        lax.psum_scatter(gain_one_grad, ("dp", "seq", "blk"), scatter_dimension=0, tiled=True),
        lax.psum_scatter(shift_one_grad, ("dp", "seq", "blk"), scatter_dimension=0, tiled=True),
        lax.psum_scatter(out_shift_grad, ("dp", "seq", "blk"), scatter_dimension=0, tiled=True),
        lax.psum_scatter(gain_two_grad, ("dp", "seq", "blk"), scatter_dimension=0, tiled=True),
        lax.psum_scatter(shift_two_grad, ("dp", "seq", "blk"), scatter_dimension=0, tiled=True),
        lax.psum_scatter(reduce_shift_grad, ("dp", "seq", "blk"), scatter_dimension=0, tiled=True),
    )
    return (
        layer_output,
        input_grad,
        small_sums[0],
        small_sums[1],
        weight_sums[0],
        weight_sums[1],
        weight_sums[2],
        small_sums[2],
        small_sums[3],
        small_sums[4],
        weight_sums[3],
        weight_sums[4],
        weight_sums[5],
        small_sums[5],
    )


ALL = ("dp", "seq", "blk")
PLANE = ("seq", "blk")


def swap(value, axes, count, offset):
    return lax.ppermute(value, axes, [(i, i ^ offset) for i in range(count)])


def low(value):
    return value.astype(jnp.bfloat16)


def wide(value):
    return value.astype(jnp.float32)


ANY = pl.BlockSpec(memory_space=pl.ANY)
HBM = pl.BlockSpec(memory_space=pltpu.HBM)
VMEM = pl.BlockSpec(memory_space=pltpu.VMEM)
SMEM = pl.BlockSpec(memory_space=pltpu.SMEM)
STEP = 256
PAIR = 2 * HD
QKV = 3 * PAIR
COLUMNS = QKV + PAIR
SMALL = 16
LANES = 128


def struct(rows, columns, dtype):
    return jax.ShapeDtypeStruct((rows, columns), dtype)


def contract(left, right, left_dim, right_dim):
    return lax.dot_general(
        left, right, (((left_dim,), (right_dim,)), ((), ())), preferred_element_type=jnp.float32
    )


def call(kernel, outs, specs, operands, scratch=(), cost=1.0, room=16):
    return pl.pallas_call(
        kernel,
        out_shape=outs,
        in_specs=specs,
        out_specs=[VMEM] * len(outs),
        scratch_shapes=list(scratch),
        compiler_params=pltpu.CompilerParams(vmem_limit_bytes=room * 2**20),
        cost_estimate=pl.CostEstimate(flops=int(cost * 1.0 * 1.1e9), bytes_accessed=0, transcendentals=0),
    )(*operands)


def fetch(pairs, sems):
    copies = [
        pltpu.make_async_copy(source, target, sems.at[k])
        for k, (source, target) in enumerate(pairs)
    ]
    for copy in copies:
        copy.start()
    for copy in copies:
        copy.wait()


def gathered(spots, pieces, order, target):
    half = len(order) // 2
    rows = target.shape[0] // len(order)
    pairs = []
    for k in range(len(order)):
        source = pl.multiple_of((spots[4] ^ (k % half)) * rows, rows)
        pairs.append((pieces[k // half].at[pl.ds(source, rows)], target.at[pl.ds(k * rows, rows)]))
    return pairs


def halves(pieces, target):
    rows = pieces[0].shape[0]
    return [(p, target.at[pl.ds(k * rows, rows)]) for k, p in enumerate(pieces)]


def row_starts(place, order, rows):
    return [pl.multiple_of((place ^ offset) * rows, rows) for offset in order]


def head_lanes(shape):
    return lax.broadcasted_iota(jnp.int32, shape, 1) // HD


def normalise(values):
    average = jnp.mean(values, -1, keepdims=True)
    centred = values - average
    variance = jnp.mean(centred * centred, -1, keepdims=True)
    scale = lax.rsqrt(variance + epsilon)
    return (centred * scale, scale)


def norm_back(grad, xhat, scale, gain_row):
    scaled = grad * gain_row
    mean_scaled = jnp.mean(scaled, -1, keepdims=True)
    mean_product = jnp.mean(scaled * xhat, -1, keepdims=True)
    return scale * (scaled - mean_scaled - xhat * mean_product)


def normalise_kernel(order, spots, *refs):
    pieces, (xhat_ref, held, sems) = refs[: len(order)], refs[len(order) :]
    rows = held.shape[0] // len(order)
    starts = row_starts(spots[3], order, rows)
    fetch([(p, held.at[pl.ds(s, rows)]) for p, s in zip(pieces, starts)], sems)

    @pl.loop(0, held.shape[0] // STEP)
    def _(step):
        block = pl.ds(pl.multiple_of(step * STEP, STEP), STEP)
        xhat_ref[block] = normalise(wide(held[block]))[0]


def reorder_columns(spots, source_ref, out_ref, count):
    size = out_ref.shape[1] // count
    for p in range(count):
        start = pl.multiple_of((spots[0] ^ p) * size, size)
        out_ref[:, p * size : (p + 1) * size] = source_ref[:, pl.ds(start, size)]


def prepare_attention_kernel(dp_count, blk_count, spots, *refs):
    count = 11
    sources, outs = refs[:count], refs[count:]
    blocks, (own_ref, small_ref) = outs[:blk_count], outs[blk_count : blk_count + 2]
    turned, *kept, sems = outs[blk_count + 2 :]
    fetch(list(zip(sources, kept)), sems)
    joint_ref, output_ref, tokens_ref = kept[:3]
    vectors, (pair_ref, shift_ref) = kept[3:9], kept[9:]
    turned[...] = low(wide(joint_ref[...]).T)
    for b, block in enumerate(blocks):
        first = (spots[2] ^ b) * 2
        for head in range(2):
            for part in range(3):
                start = pl.multiple_of(((first + head) * 3 + part) * HD, HD)
                row = part * PAIR + head * HD
                block[row : row + HD] = turned[pl.ds(start, HD)]
        start = pl.multiple_of(first * HD, PAIR)
        block[QKV:] = output_ref[pl.ds(start, PAIR)]
    reorder_columns(spots, tokens_ref, own_ref, dp_count)
    small = jnp.zeros(small_ref.shape, jnp.float32)
    row = lax.broadcasted_iota(jnp.int32, small.shape, 0)
    for k, vector in enumerate(vectors):
        piece = wide(vector[...])
        line = jnp.concatenate([piece, jnp.zeros((1, LANES - piece.shape[1]), jnp.float32)], 1)
        small = jnp.where(row == k, line, small)
    pair = wide(pair_ref[...])
    pair = jnp.concatenate([pair, jnp.zeros((pair.shape[0], LANES - pair.shape[1]), jnp.float32)], 1)
    for k in range(pair.shape[0]):
        small = jnp.where(row == 6 + k, pair[k : k + 1], small)
    small = jnp.where(row == 6 + pair.shape[0], wide(shift_ref[...]), small)
    small_ref[...] = low(small)


def cotangent_kernel(dp_count, spots, cot_ref, *refs):
    own_ref, rows = refs[-1], cot_ref.shape[0]
    for first in range(0, own_ref.shape[0], rows):
        reorder_columns(spots, cot_ref, own_ref.at[first : first + rows], dp_count)


def prepare_forward_kernel(blk_count, spots, *refs):
    expand_ref, reduce_ref = refs[:2]
    blocks, turned = refs[-blk_count - 1 : -1], refs[-1]
    turned[...] = low(wide(expand_ref[...]).T)
    units = turned.shape[0] // blk_count
    for b, block in enumerate(blocks):
        start = pl.multiple_of((spots[2] ^ b) * units, units)
        block[:units] = turned[pl.ds(start, units)]
        block[units:] = reduce_ref[pl.ds(start, units)]


def pack_kernel(blk_count, has_small, spots, *refs):
    blocks, out_ref = refs[:blk_count], refs[-1]
    rows = blocks[0].shape[0]
    for b, block in enumerate(blocks):
        start = pl.multiple_of((spots[2] ^ b) * LANES, LANES)
        for first in range(0, out_ref.shape[0], out_ref.shape[0] if has_small else rows):
            out_ref[first : first + rows, pl.ds(start, LANES)] = block[...]
    if has_small:
        small_ref = refs[blk_count]
        count = small_ref.shape[0] // SMALL
        deep = count // blk_count
        for m in range(count):
            start = pl.multiple_of((spots[3] ^ m) * SMALL, SMALL)
            row, lane = rows + m % deep * SMALL, m // deep * LANES
            out_ref[row : row + SMALL, lane : lane + LANES] = small_ref[pl.ds(start, SMALL)]


def unpack_kernel(dp_count, plane_count, blk_count, pair_rows, spots, *refs):
    blocks = refs[:dp_count]
    vector_ref, joint_ref, expand_ref, held, small, sems = refs[dp_count + 2 :]
    dp, seq, blk = spots[0], spots[1], spots[2]
    deep = held.shape[1]
    fetch([(b.at[pl.ds(COLUMNS, deep)], held.at[d]) for d, b in enumerate(blocks)], sems)
    for d in range(dp_count):
        for b in range(blk_count):
            start = (d * blk_count + b) * deep
            small[start : start + deep] = wide(held[d, :, b * LANES : (b + 1) * LANES])
    piece = vector_ref.shape[1] // (dp_count * plane_count)
    group = LANES // piece
    for first in range(0, dp_count * plane_count, group):
        parts = [
            small[(first + k) * SMALL : (first + k) * SMALL + 8, :piece] for k in range(group)
        ]
        vector_ref[:, first * piece : (first + group) * piece] = jnp.concatenate(parts, 1)

    def line(owner, row):
        start = ((dp ^ (owner // blk_count)) * plane_count + seq * blk_count + owner % blk_count)
        return small[pl.ds(start * SMALL + row, 1)]

    owners = dp_count * blk_count
    width = 2 * HD // owners
    pairs = [
        jnp.concatenate([line(o, 6 + blk * 2 + head)[:, :width] for o in range(owners)], 1)
        for head in range(2)
    ]
    joint = jnp.concatenate(
        [pairs[0][:, :HD], pairs[1][:, :HD], jnp.zeros((1, PAIR), jnp.float32)]
        + [pairs[0][:, HD:], pairs[1][:, HD:]],
        1,
    )
    joint_ref[...] = jnp.broadcast_to(joint, joint_ref.shape)
    mine = owners // blk_count
    hidden = jnp.concatenate([line(blk * mine + k, 6 + pair_rows) for k in range(mine)], 1)
    expand_ref[...] = jnp.broadcast_to(hidden, expand_ref.shape)


def score_block(queries, keys, slope, first):
    scores = contract(queries, keys, 1, 1)
    column = lax.broadcasted_iota(jnp.int32, scores.shape, 1)
    row = lax.broadcasted_iota(jnp.int32, scores.shape, 0) + first
    places = lax.broadcasted_iota(jnp.int32, (1, scores.shape[1]), 1) - (first + STEP - 1)
    return jnp.where(column <= row, scores + slope * wide(places), -1e30)


def split_rows(part_of, order, starts, rows, own_ref, away_ref):
    half = len(order) // 2
    for k, start in enumerate(starts):
        part = part_of(start)
        if k < half:
            own_ref[k * rows : (k + 1) * rows] = part
        else:
            away_ref[(k - half) * rows : (k - half + 1) * rows] = low(part)


def attend_kernel(order, dp_count, spots, slope_ref, *refs):
    blocks = refs[:dp_count]
    xhat_ref, vector_ref, bias_ref = refs[dp_count : dp_count + 3]
    mixed_ref, att_ref, lse_ref, weight_ref, own_ref, away_ref, sems = refs[dp_count + 5 :]
    cut = weight_ref.shape[1] // dp_count
    fetch(
        [
            (b.at[pl.ds(0, COLUMNS)], weight_ref.at[:, pl.ds(d * cut, cut)])
            for d, b in enumerate(blocks)
        ],
        sems,
    )
    count = xhat_ref.shape[0]

    @pl.loop(0, count // STEP)
    def _(step):
        block = pl.ds(pl.multiple_of(step * STEP, STEP), STEP)
        normed = low(xhat_ref[block] * vector_ref[:1] + vector_ref[1:2])
        mixed_ref[block] = low(contract(normed, weight_ref[:QKV], 1, 1) + bias_ref[:1])

    lanes = head_lanes((STEP, PAIR))
    for first in range(0, count, STEP):
        stop = first + STEP
        queries = mixed_ref[first:stop, :PAIR] * jnp.bfloat16(HD**-0.5)
        keys, values = mixed_ref[:stop, PAIR : 2 * PAIR], mixed_ref[:stop, 2 * PAIR :]
        attended = log_sums = None
        for head in range(2):
            chosen = jnp.where(lanes == head, queries, 0)
            scores = score_block(chosen, keys, slope_ref[head], first)
            top = jnp.max(scores, -1, keepdims=True)
            weights = jnp.exp(scores - top)
            total = jnp.sum(weights, -1, keepdims=True)
            result = contract(low(weights), values, 1, 0) / total
            log_sum = jnp.broadcast_to(top + jnp.log(total), result.shape)
            attended = result if head == 0 else jnp.where(lanes == 1, result, attended)
            log_sums = log_sum if head == 0 else jnp.where(lanes == 1, log_sum, log_sums)
        att_ref[first:stop] = attended
        lse_ref[first:stop] = log_sums
    rows = count // len(order)
    starts = row_starts(spots[3], order, rows)
    split_rows(
        lambda start: contract(low(att_ref[pl.ds(start, rows)]), weight_ref[QKV:], 1, 0),
        order, starts, rows, own_ref, away_ref,
    )


def attend_back_kernel(order, spots, slope_ref, *refs):
    pieces = refs[: len(order)]
    mixed_ref, att_ref, lse_ref, weight_ref, _ = refs[len(order) : len(order) + 5]
    grad_ref, own_ref, away_ref, held, pulled, key_sum, value_sum, sems = refs[len(order) + 5 :]
    rows = pieces[0].shape[0]
    starts = row_starts(spots[3], order, rows)
    fetch([(p, held.at[pl.ds(s, rows)]) for p, s in zip(pieces, starts)], sems)
    count = held.shape[0]

    @pl.loop(0, count // STEP)
    def _(step):
        block = pl.ds(pl.multiple_of(step * STEP, STEP), STEP)
        pulled[block] = low(contract(held[block], weight_ref[QKV:], 1, 1))

    key_sum[...] = jnp.zeros_like(key_sum)
    value_sum[...] = jnp.zeros_like(value_sum)
    lanes = head_lanes((STEP, PAIR))
    for first in range(0, count, STEP):
        stop = first + STEP
        queries = mixed_ref[first:stop, :PAIR] * jnp.bfloat16(HD**-0.5)
        keys, values = mixed_ref[:stop, PAIR : 2 * PAIR], mixed_ref[:stop, 2 * PAIR :]
        key_lanes = head_lanes(keys.shape)
        grads = pulled[first:stop]
        products = wide(grads) * att_ref[first:stop]
        query_grad = None
        for head in range(2):
            chosen = jnp.where(lanes == head, queries, 0)
            chosen_grads = jnp.where(lanes == head, grads, 0)
            delta = jnp.sum(jnp.where(lanes == head, products, 0.0), -1, keepdims=True)
            scores = score_block(chosen, keys, slope_ref[head], first)
            probs = jnp.exp(scores - lse_ref[first:stop, head * HD : head * HD + 1])
            prob_grad = contract(chosen_grads, values, 1, 1)
            score_grad = low(probs * (prob_grad - delta))
            term = contract(score_grad, jnp.where(key_lanes == head, keys, 0), 1, 0)
            query_grad = term if head == 0 else query_grad + term
            key_sum[:stop] += contract(score_grad, chosen, 0, 0)
            value_sum[:stop] += contract(low(probs), chosen_grads, 0, 0)
        grad_ref[first:stop, :PAIR] = low(query_grad * HD**-0.5)
    grad_ref[:, PAIR : 2 * PAIR] = low(key_sum[...])
    grad_ref[:, 2 * PAIR :] = low(value_sum[...])
    split_rows(
        lambda start: contract(grad_ref[pl.ds(start, rows)], weight_ref[:QKV], 1, 0),
        order, starts, rows, own_ref, away_ref,
    )


def pack_small(spots, dp_count, blk_count, vectors, pairs, hidden, small):
    dp, seq, blk = spots[0], spots[1], spots[2]
    small[...] = jnp.zeros_like(small)
    count = small.shape[0] // SMALL
    plane_count = count // dp_count
    width = vectors.shape[1]
    piece = width // count
    empty = jnp.zeros((8, LANES - piece), jnp.float32)
    for k in range(count):
        part = jnp.concatenate([vectors[:, k * piece : (k + 1) * piece], empty], 1)
        small[k * SMALL : k * SMALL + 8] = part
    owners = dp_count * blk_count
    size = 2 * HD // owners
    lane = lax.broadcasted_iota(jnp.int32, (1, LANES), 1)
    mine = owners // blk_count
    for owner in range(owners):
        spot = (dp ^ (owner // blk_count)) * plane_count + seq * blk_count + owner % blk_count
        for head in range(2):
            part = pairs[head]
            if owner:
                part = jnp.concatenate([part[:, owner * size :], part[:, : owner * size]], 1)
            row = spot * SMALL + 6 + blk * 2 + head
            small[pl.ds(row, 1)] = jnp.where(lane < size, part, 0.0)
        part = hidden[:, owner % mine * LANES : (owner % mine + 1) * LANES]
        row = spot * SMALL + 6 + 2 * blk_count
        small[pl.ds(row, 1)] = jnp.where(blk == owner // mine, part, 0.0)


def attend_weights_kernel(order, dp_count, blk_count, spots, *refs):
    pieces = refs[: len(order)]
    xhat_ref, grad_ref, att_ref, weight_ref, vector_ref = refs[len(order) : len(order) + 5]
    sums_ref, hidden_ref = refs[len(order) + 5 : len(order) + 7]
    outs = refs[len(order) + 7 :]
    parts, (held, small, sems) = outs[:dp_count], outs[dp_count:]
    rows = pieces[0].shape[0]
    starts = row_starts(spots[3], order, rows)
    fetch([(p, held.at[pl.ds(s, rows)]) for p, s in zip(pieces, starts)], sems)
    mixed_grad, attended = grad_ref[...], low(att_ref[...])
    sums = jnp.sum(wide(mixed_grad), 0, keepdims=True)
    column = jnp.broadcast_to(sums, (8, QKV)).T[:, :1]
    cut = weight_ref.shape[1] // dp_count
    lines = [[], []]
    for d, part in enumerate(parts):
        block = slice(d * cut, (d + 1) * cut)
        plain = contract(mixed_grad, low(xhat_ref[:, block]), 0, 0)
        joint_grad = vector_ref[:1, block] * plain + vector_ref[1:2, block] * column
        part[:QKV] = joint_grad.astype(part.dtype)
        part[QKV:COLUMNS] = contract(attended, held[:, block], 0, 0).astype(part.dtype)
        weights = wide(weight_ref[:QKV, block])
        for k, product in enumerate((weights * plain, weights * column)):
            lines[k].append(jnp.sum(product, 0, keepdims=True))
    lines = [jnp.concatenate(line, 1) for line in lines]
    vectors = jnp.concatenate(lines + [sums_ref[:4], jnp.zeros_like(sums_ref[:2])], 0)
    pairs = [
        jnp.concatenate([sums[:, h * HD : (h + 1) * HD], sums[:, 2 * PAIR + h * HD : 2 * PAIR + (h + 1) * HD]], 1)
        for h in range(2)
    ]
    pack_small(spots, dp_count, blk_count, vectors, pairs, hidden_ref[:1], small)
    plane_rows = small.shape[0] // dp_count
    deep = plane_rows // blk_count
    for d, part in enumerate(parts):
        for b in range(blk_count):
            start = d * plane_rows + b * deep
            part[COLUMNS:, b * LANES : (b + 1) * LANES] = small[start : start + deep].astype(part.dtype)


def split_kernel(count, blk_count, has_small, after, spots, *refs):
    parts, outs = refs[:count], refs[count + after :]
    total = outs[-1]
    if len(parts[0].shape) == 3:
        total[...] = jnp.sum(wide(parts[0][...]), 0)
    else:
        total[...] = wide(summed(parts[0], parts[1:]))
    rows = outs[0].shape[0]
    for b in range(blk_count):
        start = pl.multiple_of((spots[2] ^ b) * LANES, LANES)
        outs[b][...] = total[:rows, pl.ds(start, LANES)].astype(outs[b].dtype)
    if has_small:
        small_ref = outs[blk_count]
        devices = small_ref.shape[0] // SMALL
        deep = devices // blk_count
        for m in range(devices):
            start = pl.multiple_of((spots[3] ^ m) * SMALL, SMALL)
            row, lane = rows + m % deep * SMALL, m // deep * LANES
            small_ref[pl.ds(start, SMALL)] = total[row : row + SMALL, lane : lane + LANES]


def attend_final_kernel(blk_count, spots, *refs):
    blocks, (joint_ref, output_ref) = refs[:blk_count], refs[blk_count:]
    for b, block in enumerate(blocks):
        other = spots[2] ^ b
        values = wide(block[...])
        turned = values[:QKV].T
        ordered = jnp.concatenate(
            [turned[:, part * PAIR + h * HD : part * PAIR + (h + 1) * HD] for h in range(2) for part in range(3)],
            1,
        )
        joint_ref[:, pl.ds(pl.multiple_of(other * QKV, LANES), QKV)] = ordered
        output_ref[pl.ds(pl.multiple_of(other * PAIR, PAIR), PAIR)] = values[QKV:]


def forward_final_kernel(blk_count, spots, *refs):
    blocks, (expand_ref, reduce_ref) = refs[:blk_count], refs[blk_count:]
    units = reduce_ref.shape[0] // blk_count
    for b, block in enumerate(blocks):
        start = pl.multiple_of((spots[2] ^ b) * units, units)
        expand_ref[:, pl.ds(start, units)] = wide(block[:units]).T
        reduce_ref[pl.ds(start, units)] = wide(block[units:])


def forward_fetch(order, dp_count, spots, pieces, weights, left, right, held, sems):
    cut = weights.shape[2]
    fetch(
        halves(pieces[:-2], left)
        + gathered(spots, pieces[-2:], order, right)
        + [
            (weights.at[spots[0] ^ d], held.at[:, pl.ds(d * cut, cut)]) for d in range(dp_count)
        ],
        sems,
    )


def forward_kernel(order, dp_count, spots, *refs):
    count = len(order) + 2
    pieces, weights, refs = refs[:count], refs[count], refs[count + 1 :]
    bias_ref, act_ref, grad_ref, own_ref, away_ref, sum_ref, left, right, held, sems = refs
    forward_fetch(order, dp_count, spots, pieces, weights, left, right, held, sems)
    units = act_ref.shape[1]
    half = left.shape[0] // 2
    sum_ref[...] = jnp.zeros_like(sum_ref)
    root = (2.0 / jnp.pi) ** 0.5
    for first in range(0, left.shape[0], STEP):
        stop = first + STEP
        hidden = contract(left[first:stop], held[:units], 1, 1) + bias_ref[:1]
        square = hidden * hidden
        bend = jnp.tanh(root * hidden * (1.0 + 0.044715 * square))
        act_ref[first:stop] = low(0.5 * hidden * (1.0 + bend))
        slope = 0.5 * (1.0 + bend) + 0.5 * hidden * (1.0 - bend * bend) * root * (
            1.0 + 3 * 0.044715 * square
        )
        hidden_grad = low(contract(right[first:stop], held[units:], 1, 1) * slope)
        grad_ref[first:stop] = hidden_grad
        sum_ref[...] += jnp.sum(wide(hidden_grad), 0, keepdims=True)
        part = contract(hidden_grad, held[:units], 1, 0)
        if first < half:
            own_ref[first:stop] = part
        else:
            away_ref[first - half : stop - half] = low(part)


def forward_weights_kernel(order, dp_count, spots, *refs):
    count = len(order) + 2
    pieces, weights, refs = refs[:count], refs[count], refs[count + 1 :]
    act_ref, grad_ref, _ = refs[:3]
    part_ref, own_ref, away_ref, left, right, held, sems = refs[3:]
    forward_fetch(order, dp_count, spots, pieces, weights, left, right, held, sems)
    units, cut = act_ref.shape[1], weights.shape[2]
    for d in range(dp_count):
        block = slice(d * cut, (d + 1) * cut)
        spot = spots[0] ^ d
        part_ref[spot, :units] = low(contract(grad_ref[...], left[:, block], 0, 0))
        part_ref[spot, units:] = low(contract(act_ref[...], right[:, block], 0, 0))
    half = left.shape[0] // 2
    for first in range(0, left.shape[0], STEP):
        stop = first + STEP
        result = contract(act_ref[first:stop], held[units:], 1, 0)
        if first < half:
            own_ref[first:stop] = result
        else:
            away_ref[first - half : stop - half] = low(result)


def add_kernel(count, own_ref, came_ref, *refs):
    total_ref, *pieces = refs[count:]
    rows = total_ref.shape[0]
    total_ref[...] = own_ref[:rows] + wide(came_ref[:rows])
    for k, piece in enumerate(pieces):
        block = slice((k + 1) * rows, (k + 2) * rows)
        piece[...] = low(own_ref[block] + wide(came_ref[block]))


def summed(total_ref, came):
    total = total_ref[...]
    for piece in came:
        total = total + wide(piece[...])
    return total


def middle_kernel(count, total_ref, *refs):
    came = refs[:count]
    tokens_ref, vector_ref, middle_ref, normed_ref = refs[count:]
    middle = wide(tokens_ref[...]) + (summed(total_ref, came) + vector_ref[2:3])
    middle_ref[...] = middle
    normed_ref[...] = low(normalise(middle)[0] * vector_ref[3:4] + vector_ref[4:5])


def middle_back_kernel(count, total_ref, *refs):
    came = refs[:count]
    middle_ref, cot_ref, vector_ref, grad_ref, branch_ref, sums_ref = refs[count:]
    grad = summed(total_ref, came)
    xhat, scale = normalise(middle_ref[...])
    upstream = wide(cot_ref[: grad_ref.shape[0]])
    total = upstream + norm_back(grad, xhat, scale, vector_ref[3:4])
    grad_ref[...] = total
    branch = low(total)
    branch_ref[...] = branch
    sums_ref[...] = jnp.zeros_like(sums_ref)
    for k, values in enumerate((wide(branch), grad * xhat, grad, upstream)):
        sums_ref[k : k + 1] = jnp.sum(values, 0, keepdims=True)


def place_columns(spots, dp_count, values, out_ref):
    size = out_ref.shape[1] // dp_count
    for d in range(dp_count):
        start = pl.multiple_of((spots[0] ^ d) * size, size)
        out_ref[:, pl.ds(start, size)] = values[:, d * size : (d + 1) * size]


def add_rows_kernel(count, spots, own_ref, came_ref, result_own, result_came, _, out_ref):
    rows, width = own_ref.shape[0] // count, own_ref.shape[1]
    for k in range(count):
        block = slice(k * rows, (k + 1) * rows)
        start = pl.multiple_of((spots[4] ^ k) * rows, rows)
        out_ref[pl.ds(start, rows), :width] = low(own_ref[block] + wide(came_ref[block]))
        out_ref[pl.ds(start, rows), width:] = low(result_own[block] + wide(result_came[block]))


def final_kernel(dp_count, spots, parts_ref, grad_ref, tokens_ref, middle_ref, vector_ref, input_ref, output_ref):
    width = grad_ref.shape[1]
    grad = jnp.sum(wide(parts_ref[:, :, :width]), 0)
    xhat, scale = normalise(wide(tokens_ref[...]))
    result = grad_ref[...] + norm_back(grad, xhat, scale, vector_ref[:1])
    place_columns(spots, dp_count, low(result), input_ref)
    result = jnp.sum(wide(parts_ref[:, :, width:]), 0)
    result = middle_ref[...] + (result + vector_ref[5:6])
    place_columns(spots, dp_count, low(result), output_ref)


def local_heads(
    tokens,
    first_gain,
    first_shift,
    joint_weight,
    joint_bias,
    output_weight,
    output_bias,
    second_gain,
    second_shift,
    expand_weight,
    expand_bias,
    reduce_weight,
    reduce_bias,
    cotangent,
):
    dp_count, seq_count, blk_count = (lax.axis_size(axis) for axis in ALL)
    dp, seq, blk = (lax.axis_index(axis) for axis in ALL)
    plane_count = seq_count * blk_count
    place = seq * blk_count + blk
    chip = seq // 2 * blk_count + blk
    spots = jnp.stack([dp, seq, blk, place, chip]).astype(jnp.int32)
    tok_rows, width = tokens.shape
    units = expand_weight.shape[1] // blk_count
    cut = width // dp_count
    piece = first_gain.shape[0]
    core = blk_count
    chips = [p for p in range(plane_count) if not p & core]
    order = chips + [p ^ core for p in chips]
    chip_count = len(chips)
    row_count, half_rows = plane_count * tok_rows, chip_count * tok_rows
    f32, bf16 = jnp.float32, jnp.bfloat16
    halves_out = [struct(half_rows, width, f32), struct(half_rows, width, bf16)]
    own_out = [struct(tok_rows, width, f32)]
    low_out = [struct(tok_rows, width, bf16)]
    copies_out = [struct(half_rows, width, bf16)]
    dma = lambda count: pltpu.SemaphoreType.DMA((count,))
    held = lambda columns: pltpu.VMEM((row_count, columns), bf16)
    kernel = functools.partial

    def gather_plane(block):
        mine = [block] + [swap(block, PLANE, plane_count, chip) for chip in chips[1:]]
        return mine + [swap(p, PLANE, plane_count, core) for p in mine]

    groups = [[p ^ side for p in chips] for side in (0, core)]

    def between_chips(blocks):
        blocks = blocks.reshape(chip_count, tok_rows, blocks.shape[1])
        return lax.all_to_all(blocks, PLANE, 0, 0, axis_index_groups=groups, tiled=True)

    def gather_copies(copies):
        mine = between_chips(copies).reshape(half_rows, width)
        return [mine, swap(mine, PLANE, plane_count, core)]

    def scatter_plane(own, away, after=()):
        came = swap(away, PLANE, plane_count, core)
        outs = own_out + low_out * (chip_count - 1)
        total, *pieces = call(
            kernel(add_kernel, len(after)),
            outs,
            [VMEM, VMEM] + [ANY] * len(after),
            [own, came] + list(after),
        )
        pieces = [swap(p, PLANE, plane_count, chip) for chip, p in zip(chips[1:], pieces)]
        return [total] + pieces

    def exchange_blk(blocks):
        return [swap(p, "blk", blk_count, b) if b else p for b, p in enumerate(blocks)]

    sources = [joint_weight, output_weight, tokens]
    sources += [
        v.reshape(1, -1)
        for v in (first_gain, first_shift, output_bias, second_gain, second_shift, reduce_bias)
    ]
    sources += [joint_bias, expand_bias]
    *blocks, tokens_own, small = call(
        kernel(prepare_attention_kernel, dp_count, blk_count),
        [struct(COLUMNS, LANES, bf16)] * blk_count + low_out + [struct(SMALL, LANES, bf16)],
        [SMEM] + [HBM] * len(sources),
        [spots] + sources,
        [pltpu.VMEM((joint_weight.shape[1], LANES), bf16)]
        + [pltpu.VMEM(v.shape, v.dtype) for v in sources]
        + [dma(len(sources))],
        room=60,
    )
    bits = [1 << b for b in range(plane_count.bit_length() - 1)]
    blocks = exchange_blk(blocks)
    for bit in bits:
        small = jnp.concatenate([small, swap(small, PLANE, plane_count, bit)], 0)
    small_deep = plane_count * SMALL // blk_count
    block = call(
        kernel(pack_kernel, blk_count, True),
        [struct(COLUMNS + small_deep, cut, bf16)],
        [SMEM] + [VMEM] * (blk_count + 1),
        [spots] + blocks + [small],
    )[0]
    blocks = [block] + [swap(block, "dp", dp_count, d) for d in range(1, dp_count)]
    token_group = gather_plane(tokens_own)

    cotangent_own = call(
        kernel(cotangent_kernel, dp_count),
        copies_out,
        [SMEM, VMEM] + [ANY] * 2,
        [spots, cotangent] + blocks[1:3],
    )[0]
    forward_blocks = call(
        kernel(prepare_forward_kernel, blk_count),
        [struct(2 * units, LANES, bf16)] * blk_count,
        [SMEM] + [VMEM] * 2 + [ANY],
        [spots, expand_weight, reduce_weight, blocks[1]],
        [pltpu.VMEM((expand_weight.shape[1], LANES), bf16)],
    )
    forward_block = call(
        kernel(pack_kernel, blk_count, False),
        [struct(dp_count * 2 * units, cut, bf16)],
        [SMEM] + [VMEM] * blk_count,
        [spots] + exchange_blk(forward_blocks),
    )[0]
    forward_weights = lax.all_to_all(
        forward_block.reshape(dp_count, 2 * units, cut), "dp", 0, 0, tiled=True
    )
    cot_group = gather_copies(cotangent_own)

    xhat = call(
        kernel(normalise_kernel, order),
        [struct(row_count, width, f32)],
        [SMEM] + [HBM] * plane_count,
        [spots] + token_group,
        [held(width), dma(plane_count)],
        2,
    )[0]
    vectors, joint_row, expand_row = call(
        kernel(unpack_kernel, dp_count, plane_count, blk_count, joint_bias.shape[0]),
        [struct(8, width, f32), struct(8, QKV, f32), struct(8, units, f32)],
        [SMEM] + [HBM] * dp_count + [ANY] * 2,
        [spots] + blocks + [xhat, tokens_own],
        [
            pltpu.VMEM((dp_count, small_deep, cut), bf16),
            pltpu.VMEM((dp_count * plane_count * SMALL, LANES), f32),
            dma(dp_count),
        ],
    )
    head_ids = place * 2 + jnp.arange(2, dtype=jnp.int32)
    slopes = jnp.exp2(-8.0 * (head_ids + 1).astype(f32) / H)
    mixed, attended, log_sums, weights, own, away = call(
        kernel(attend_kernel, order, dp_count),
        [struct(row_count, QKV, bf16), struct(row_count, PAIR, f32)]
        + [struct(row_count, PAIR, f32), struct(COLUMNS, width, bf16)]
        + halves_out,
        [SMEM, SMEM] + [HBM] * dp_count + [VMEM] * 3 + [ANY] * 2,
        [spots, slopes] + blocks + [xhat, vectors, joint_row, cot_group[0], forward_block],
        [dma(dp_count)],
        10,
        24,
    )
    branch = scatter_plane(own, away)

    middle, normed_two = call(
        kernel(middle_kernel, chip_count - 1),
        own_out + low_out,
        [VMEM] * (chip_count + 2),
        branch + [tokens_own, vectors],
    )
    normed_group = gather_plane(normed_two)
    forward_operands = [spots] + normed_group + cot_group + [forward_weights]
    forward_specs = [SMEM] + [HBM] * (plane_count + 3)
    forward_scratch = [held(width), held(width), pltpu.VMEM((2 * units, width), bf16)]
    forward_scratch.append(dma(2 * plane_count + dp_count))
    activated, hidden_grad, own, away, hidden_sums = call(
        kernel(forward_kernel, order, dp_count),
        [struct(row_count, units, bf16)] * 2 + halves_out + [struct(8, units, f32)],
        forward_specs + [VMEM],
        forward_operands + [expand_row],
        forward_scratch,
        8,
        60,
    )
    normed_two_grad = scatter_plane(own, away)
    middle_grad, branch_grad, middle_sums = call(
        kernel(middle_back_kernel, chip_count - 1),
        own_out + low_out + [struct(8, width, f32)],
        [VMEM] * (chip_count + 3),
        normed_two_grad + [middle, cotangent_own, vectors],
    )
    forward_grad, own, away = call(
        kernel(forward_weights_kernel, order, dp_count),
        [jax.ShapeDtypeStruct((dp_count, 2 * units, cut), bf16)] + halves_out,
        forward_specs + [VMEM, VMEM, ANY],
        forward_operands + [activated, hidden_grad, normed_two_grad[0]],
        forward_scratch,
        8,
        60,
    )
    forward_grad = lax.all_to_all(forward_grad, "dp", 0, 0, tiled=True)
    forward_grad = call(
        kernel(split_kernel, 1, blk_count, False, 0),
        [struct(2 * units, LANES, f32)] + [struct(2 * units, LANES, bf16)] * (blk_count - 1),
        [SMEM, VMEM],
        [spots, forward_grad],
        [pltpu.VMEM((2 * units, cut), f32)],
    )
    forward_grad = exchange_blk(forward_grad)
    expand_grad, reduce_grad = call(
        kernel(forward_final_kernel, blk_count),
        [struct(LANES, blk_count * units, f32), struct(blk_count * units, LANES, f32)],
        [SMEM] + [VMEM] * blk_count,
        [spots] + forward_grad,
    )

    branch_group = gather_plane(branch_grad)
    result_own, result_came = own, swap(away, PLANE, plane_count, core)
    mixed_grad, own, away = call(
        kernel(attend_back_kernel, order),
        [struct(row_count, QKV, bf16)] + halves_out,
        [SMEM, SMEM] + [HBM] * plane_count + [VMEM] * 4 + [ANY],
        [spots, slopes] + branch_group + [mixed, attended, log_sums, weights, spots],
        [held(width), held(PAIR)]
        + [pltpu.VMEM((row_count, PAIR), f32)] * 2
        + [dma(plane_count)],
        10,
        24,
    )
    block_out = lambda dtype: struct(COLUMNS + small_deep, cut, dtype)
    attention_grad = call(
        kernel(attend_weights_kernel, order, dp_count, blk_count),
        [block_out(f32)] + [block_out(bf16)] * (dp_count - 1),
        [SMEM] + [HBM] * plane_count + [VMEM] * 7,
        [spots]
        + branch_group
        + [xhat, mixed_grad, attended, weights, vectors, middle_sums, hidden_sums],
        [held(width), pltpu.VMEM((dp_count * plane_count * SMALL, LANES), f32), dma(plane_count)],
        3,
        24,
    )
    pieces = call(
        kernel(add_rows_kernel, chip_count),
        [struct(half_rows, 2 * width, bf16)],
        [SMEM] + [VMEM] * 4 + [ANY],
        [spots, own, swap(away, PLANE, plane_count, core), result_own, result_came]
        + list(attention_grad[1:2]),
    )[0]
    pieces = between_chips(pieces)
    input_grad, layer_output = call(
        kernel(final_kernel, dp_count),
        low_out * 2,
        [SMEM] + [VMEM] * 5,
        [spots, pieces, middle_grad, tokens_own, middle, vectors],
    )
    attention_grad = [attention_grad[0]] + [
        swap(attention_grad[d], "dp", dp_count, d) for d in range(1, dp_count)
    ]
    *attention_grad, small = call(
        kernel(split_kernel, dp_count, blk_count, True, 2),
        [struct(COLUMNS, LANES, f32)]
        + [struct(COLUMNS, LANES, bf16)] * (blk_count - 1)
        + [struct(plane_count * SMALL, LANES, f32)],
        [SMEM] + [VMEM] * dp_count + [ANY] * 2,
        [spots] + attention_grad + [pieces, forward_grad[-1]],
        [pltpu.VMEM((COLUMNS + small_deep, cut), f32)],
    )
    joint_grad, output_grad = call(
        kernel(attend_final_kernel, blk_count),
        [struct(LANES, blk_count * QKV, f32), struct(blk_count * PAIR, LANES, f32)],
        [SMEM] + [VMEM] * blk_count,
        [spots] + exchange_blk(attention_grad),
    )
    for bit in reversed(bits):
        small = small[: bit * SMALL] + swap(small[bit * SMALL :], PLANE, plane_count, bit)
    pair_rows, pair_columns = joint_bias.shape
    return (
        layer_output,
        input_grad,
        small[0, :piece],
        small[1, :piece],
        joint_grad,
        small[6 : 6 + pair_rows, :pair_columns],
        output_grad,
        small[2, :piece],
        small[3, :piece],
        small[4, :piece],
        expand_grad,
        small[6 + pair_rows : 7 + pair_rows],
        reduce_grad,
        small[5, :piece],
    )


def local_any(*arrays):
    dp_count, seq_count, blk_count = (lax.axis_size(axis) for axis in ALL)
    own_width = arrays[0].shape[1] // (dp_count * blk_count)
    if H == 2 * seq_count * blk_count and own_width == LANES and blk_count == 2:
        return local_heads(*arrays)
    return local(*arrays)


def solution(mesh):
    return jax.shard_map(
        local_heads if H == 2 * mesh.shape["seq"] * mesh.shape["blk"] else local,
        mesh=mesh,
        in_specs=(
            P(("dp", "seq", "blk"), None),
            P(("dp", "seq", "blk")),
            P(("dp", "seq", "blk")),
            P(("dp", "blk"), "seq"),
            P("seq", ("dp", "blk")),
            P("seq", ("dp", "blk")),
            P(("dp", "seq", "blk")),
            P(("dp", "seq", "blk")),
            P(("dp", "seq", "blk")),
            P(("dp", "blk"), "seq"),
            P("seq", ("dp", "blk")),
            P("seq", ("dp", "blk")),
            P(("dp", "seq", "blk")),
            P(("dp", "seq", "blk"), None),
        ),
        out_specs=(
            P(("dp", "seq", "blk"), None),
            P(("dp", "seq", "blk"), None),
            P(("dp", "seq", "blk")),
            P(("dp", "seq", "blk")),
            P(("dp", "blk"), "seq"),
            P("seq", ("dp", "blk")),
            P("seq", ("dp", "blk")),
            P(("dp", "seq", "blk")),
            P(("dp", "seq", "blk")),
            P(("dp", "seq", "blk")),
            P(("dp", "blk"), "seq"),
            P("seq", ("dp", "blk")),
            P("seq", ("dp", "blk")),
            P(("dp", "seq", "blk")),
        ),
        check_vma=False,
    )
```
